32 devices in a mesh: pb: 4 (over x, core), pa: 4 (over z), ta: 2 (over y).
Axes of the slice: x: 2, y: 2, z: 4, core: 2. Of those that a mesh axis runs over, the one named last changes fastest.
Arguments:
- rows_in: bfloat16 [22528, 1024], P(('pb', 'pa')), may hold values from -6 to 6
- w_qkv: bfloat16 [3, 1024, 1024], P(None, ('pb', 'pa'), 'ta'), may hold values from -0.1875 to 0.1875
- b_qv: float32 [2, 1024], P(None, 'ta'), may hold values from -3 to 3
- w_out: bfloat16 [1024, 1024], P('ta', ('pb', 'pa')), may hold values from -0.75 to 0.75
- b_out: float32 [1024], replicated, may hold values from -3 to 3
- ln1_gain: float32 [1024], replicated, may hold values from 0.1 to 1.9
- ln1_bias: float32 [1024], replicated, may hold values from -3 to 3
- w_in: bfloat16 [1024, 4096], P(('pb', 'pa'), 'ta'), may hold values from -0.1875 to 0.1875
- b_in: float32 [4096], P('ta'), may hold values from -3 to 3
- w_fin: bfloat16 [4096, 1024], P('ta', ('pb', 'pa')), may hold values from -0.09375 to 0.09375
- b_fin: float32 [1024], replicated, may hold values from -3 to 3
- ln2_gain: float32 [1024], replicated, may hold values from 0.1 to 1.9
- ln2_bias: float32 [1024], replicated, may hold values from -3 to 3
- w_head: bfloat16 [1024, 1024], P(('pb', 'pa')), may hold values from -0.1875 to 0.1875
- b_head: float32 [1024], replicated, may hold values from -2 to 2
- lengths: int32 [16, 4], P(('pb', 'pa')), may hold values from 1 to 1024, 1280 in all within a row
- query_len: int32 [16, 4], P('pb'), may hold values from 1 to 32
- score_grad: float32 [4, 4, 4, 16], P('pb', None, None, 'pa'), may hold values from -6 to 6
Outputs:
- scores: float32 [4, 4, 4, 16], P('pb', None, 'ta', 'pa')
- grad_rows: float32 [22528, 1024], P(('pb', 'pa', 'ta'))
- grad_w_qkv: float32 [3, 1024, 1024], P(None, ('pb', 'pa'), 'ta')
- grad_b_qv: float32 [2, 1024], P(None, ('pb', 'pa', 'ta'))
- grad_w_out: float32 [1024, 1024], P('ta', ('pb', 'pa'))
- grad_b_out: float32 [1024], P(('pb', 'pa', 'ta'))
- grad_ln1_gain: float32 [1024], P(('pb', 'pa', 'ta'))
- grad_ln1_bias: float32 [1024], P(('pb', 'pa', 'ta'))
- grad_w_in: float32 [1024, 4096], P(('pb', 'pa'), 'ta')
- grad_b_in: float32 [4096], P(('pb', 'pa', 'ta'))
- grad_w_fin: float32 [4096, 1024], P('ta', ('pb', 'pa'))
- grad_b_fin: float32 [1024], P(('pb', 'pa', 'ta'))
- grad_ln2_gain: float32 [1024], P(('pb', 'pa', 'ta'))
- grad_ln2_bias: float32 [1024], P(('pb', 'pa', 'ta'))
- grad_w_head: float32 [1024, 1024], P(('pb', 'pa', 'ta'))
- grad_b_head: float32 [1024], P(('pb', 'pa', 'ta'))
The draws below stay inside these ranges and needn't reach their ends.
Inputs may be any that keep to these rules, and one draw needn't show every extreme that they name: The 4 passage lengths of a group sum to 1280; the longest is exactly 1024.
All inputs are finite; a program needn't handle non-finite values.
Results may differ from the reference program's by a relative error of at most 0.018.
Values may be sent and summed in bfloat16 or wider, within the bound.
No kernel may reach another device: no remote copies, remote signals or barrier semaphores. Data moves between devices by JAX's collectives and lax.ppermute only.
A program may use at most 192 MiB of HBM per device.

```python
import math
from functools import partial
import jax
import jax.numpy as jnp
import numpy as np
from jax import lax

D = 1024
HEADS = 16
HDIM = 64
FF = 4096
QLEN = 32
QN = 4
PN = 4
PLEN = 1024
PTOK = 1280
QTOK = 128
ROWS = 1408
GROUPS = 16
TOKENS = 22528
N_PB = 4
N_PA = 4
N_TA = 2


def place_ends(drawn, key, least, top_value):
    dims = drawn.shape
    index_at = [jax.random.randint(jax.random.fold_in(key, axis), (), 0, dims[axis]) for axis in range(len(dims))]
    drawn = drawn.at[tuple(index_at)].set(least)
    longest = dims.index(max(dims))
    index_at[longest] = (index_at[longest] + 1) % dims[longest]
    return drawn.at[tuple(index_at)].set(top_value)


def block_scale(rng, shape, pieces, smallest, top_value):
    factor_of, own = 1.0, jax.random.fold_in(rng, 6)
    for axis_at, blocks in pieces:
        draws = jnp.exp(jax.random.uniform(jax.random.fold_in(own, axis_at), (blocks,), jnp.float32, smallest / len(pieces), top_value / len(pieces)))
        factor_of = factor_of * jnp.repeat(draws, shape[axis_at] // blocks).reshape([-1 if axis == axis_at else 1 for axis in range(len(shape))])
    return factor_of


def profile(amount, total, reach, slope):
    portions = [(1 << 20) // math.isqrt(grade ** slope) + 1 for grade in range(2, amount + 1)]
    rest, given = total - reach - (amount - 1), [1] * (amount - 1)
    while rest > 0:
        free = [i for i in range(amount - 1) if given[i] < reach]
        mass, left = sum([portions[i] for i in free]), rest
        for i in free:
            more = min(reach - given[i], max(1, left * portions[i] // mass), rest)
            given[i] = given[i] + more
            rest = rest - more
    return np.array([reach] + given)


def uneven(own_key, count, total, reach, slope):
    if count == 2:
        one = jax.random.randint(own_key, (), max(1, total - reach), min(reach, total - 1) + 1)
        return jnp.stack([one, total - one])
    sizes = jnp.asarray(profile(count, total, reach, slope), jnp.int32)
    twos = (count - 1) // 2
    source_of, receiver = sizes[1:1 + 2 * twos:2], sizes[2:2 + 2 * twos:2]
    room = jnp.minimum(source_of - 1, reach - receiver)
    moved = jax.random.randint(jax.random.fold_in(own_key, 1), (twos,), 0, 1 << 20) % (room + 1)
    sizes = sizes.at[1:1 + 2 * twos:2].set(source_of - moved).at[2:2 + 2 * twos:2].set(receiver + moved)
    return sizes[jax.random.permutation(jax.random.fold_in(own_key, 2), count)]


def bell_draw(own_key, dims, scale, most, pieces=(), held_as=jnp.bfloat16):
    drawn = scale * jax.random.normal(own_key, dims, jnp.float32)
    if pieces:
        drawn = drawn * block_scale(own_key, dims, pieces, -0.22, 0.18)
    return jnp.clip(drawn, -most, most).astype(held_as)


def setup_inputs(seed: int = 0) -> dict:
    streams_of = jax.random.split(jax.random.key(seed), 19)
    return {
        "rows_in": bell_draw(streams_of[0], (TOKENS, D), 1.0, 6.0, ((0, 16),)),
        "w_qkv": bell_draw(streams_of[1], (3, D, D), D ** -0.5, 0.1875, ((1, 16), (2, 2))),
        "b_qv": bell_draw(streams_of[2], (2, D), 0.5, 3.0, ((1, 2),), jnp.float32),
        "w_out": bell_draw(streams_of[3], (D, D), (D // 16) ** -0.5, 0.75, ((0, 2), (1, 16))),
        "b_out": bell_draw(streams_of[4], (D,), 0.5, 3.0, (), jnp.float32),
        "ln1_gain": jnp.clip(1.0 + 0.18 * jax.random.normal(streams_of[5], (D,), jnp.float32), 0.1, 1.9),
        "ln1_bias": bell_draw(streams_of[6], (D,), 0.5, 3.0, (), jnp.float32),
        "w_in": bell_draw(streams_of[7], (D, FF), D ** -0.5, 0.1875, ((0, 16), (1, 2))),
        "b_in": bell_draw(streams_of[8], (FF,), 0.5, 3.0, ((0, 2),), jnp.float32),
        "w_fin": bell_draw(streams_of[9], (FF, D), FF ** -0.5, 0.09375, ((0, 2), (1, 16))),
        "b_fin": bell_draw(streams_of[10], (D,), 0.5, 3.0, (), jnp.float32),
        "ln2_gain": jnp.clip(1.0 + 0.18 * jax.random.normal(streams_of[11], (D,), jnp.float32), 0.1, 1.9),
        "ln2_bias": bell_draw(streams_of[12], (D,), 0.5, 3.0, (), jnp.float32),
        "w_head": bell_draw(streams_of[13], (D, D), D ** -0.5, 0.1875, ((0, 16),)),
        "b_head": bell_draw(streams_of[14], (D,), 0.3, 2.0, (), jnp.float32),
        "lengths": jax.vmap(lambda own: uneven(own, PN, PTOK, PLEN, 2))(jax.random.split(streams_of[15], GROUPS)).reshape((GROUPS, PN)).astype(jnp.int32),
        "query_len": place_ends(jax.random.randint(streams_of[16], (GROUPS, QN), 1, QLEN + 1), jax.random.fold_in(streams_of[16], 1), 1, QLEN).astype(jnp.int32),
        "score_grad": bell_draw(streams_of[17], (N_PB, N_PA, QN, N_PA * PN), 1.0, 6.0, ((0, 4), (3, 4)), jnp.float32),
    }


@jax.custom_vjp
def low(v):
    return lax.optimization_barrier(v.astype(jnp.bfloat16)).astype(jnp.float32)

@jax.custom_vjp
def low_back(v):
    return v

def low_keep(v):
    return (low(v), None)

def low_pass(kept, grad):
    return (grad,)

def back_keep(v):
    return (v, None)

def back_low(kept, grad):
    return (low(grad),)
low.defvjp(low_keep, low_pass)
low_back.defvjp(back_keep, back_low)
sharpness_divisor = 0.02
epsilon = 1e-05
unit_eps = 1e-06
distractor_document = -1e+30

def highest(left_op, right_op):
    return jnp.dot(left_op, right_op, precision=lax.Precision.HIGHEST)

def layer_norm(hidden, gain_vec, bias_vec):
    centered = hidden - lax.optimization_barrier(jnp.mean(hidden, axis=-1, keepdims=True))
    spread = lax.optimization_barrier(jnp.mean(centered * centered, axis=-1, keepdims=True))
    return centered * lax.rsqrt(spread + epsilon) * gain_vec + bias_vec

def encode_group(weights, inputs):
    w_qkv, b_qv, w_out, b_out, ln1_gain, ln1_bias, w_in, b_in, w_fin, b_fin, ln2_gain, ln2_bias, w_head, b_head = weights
    rows_group, segment, valid = inputs
    row_count = rows_group.shape[0]
    queries = low(low_back(highest(rows_group, w_qkv[0])) + b_qv[0])
    key_rows = low(low_back(highest(rows_group, w_qkv[1])))
    values = low(low_back(highest(rows_group, w_qkv[2])) + b_qv[1])
    queries = queries.reshape(row_count, HEADS, HDIM)
    key_rows = key_rows.reshape(row_count, HEADS, HDIM)
    values = values.reshape(row_count, HEADS, HDIM)
    qk_scale = 1.0 / math.sqrt(HDIM)
    logits = jnp.einsum('qhd,khd->hqk', queries, key_rows, precision=lax.Precision.HIGHEST)
    logits = low_back(logits * qk_scale)
    allowed = (segment[:, None] == segment[None, :]) & valid[None, :]
    logits = jnp.where(allowed[None], logits, distractor_document)
    attn_prob = low(jax.nn.softmax(logits, axis=-1))
    context = jnp.einsum('hqk,khd->qhd', attn_prob, values, precision=lax.Precision.HIGHEST)
    context = low(low_back(context.reshape(row_count, D)))
    attended = low_back(highest(context, w_out))
    h_one = rows_group + attended + b_out
    normed = layer_norm(h_one, ln1_gain, ln1_bias)
    inner_act = low_back(highest(low(normed), w_in)) + b_in
    active = low(jax.nn.gelu(inner_act, approximate=False))
    branch = low_back(highest(active, w_fin))
    h_two = normed + branch + b_fin
    output = layer_norm(h_two, ln2_gain, ln2_bias)
    raw_embed = low_back(highest(low(output), w_head)) + b_head
    unit_embed = raw_embed * lax.rsqrt(lax.optimization_barrier(jnp.sum(raw_embed * raw_embed, axis=-1, keepdims=True)) + unit_eps)
    return low(unit_embed)

def score_group(query_units, token_valid, inputs):
    group_index, pass_units, owner = inputs
    row_index = group_index // N_PA
    asking = lax.dynamic_index_in_dim(query_units, row_index, 0, keepdims=False)
    weight_row = lax.dynamic_index_in_dim(token_valid, row_index, 0, keepdims=False)
    relevance_matrix = low_back(highest(asking, pass_units.T))
    belonging_indicator = owner[:, None] == jnp.arange(PN, dtype=jnp.int32)[None, :]
    divided_logit_matrix = jnp.where(belonging_indicator[None], relevance_matrix[:, :, None] / sharpness_divisor, distractor_document)
    smoothed_quantity = sharpness_divisor * jax.nn.logsumexp(divided_logit_matrix, axis=1)
    smoothed_quantity = smoothed_quantity * weight_row[:, None]
    return lax.optimization_barrier(jnp.sum(smoothed_quantity.reshape(N_PA, QN, QLEN, PN), axis=2))

def forward(rows_all, w_qkv, b_qv, w_out, b_out, ln1_gain, ln1_bias, w_in, b_in, w_fin, b_fin, ln2_gain, ln2_bias, w_head, b_head, lengths, query_len):
    weights = (w_qkv, b_qv, w_out, b_out, ln1_gain, ln1_bias, w_in, b_in, w_fin, b_fin, ln2_gain, ln2_bias, w_head, b_head)
    split_rows = rows_all.reshape(GROUPS, N_TA, ROWS // N_TA, D)
    qpart = QTOK // N_TA
    query_rows = split_rows[:, :, :qpart].reshape(GROUPS, QTOK, D)
    pass_rows = split_rows[:, :, qpart:].reshape(GROUPS, PTOK, D)
    ordered = jnp.concatenate([query_rows, pass_rows], axis=1)
    query_seg = jnp.arange(QTOK, dtype=jnp.int32) // QLEN
    query_pos = jnp.arange(QTOK, dtype=jnp.int32) % QLEN
    query_ok = query_pos[None, :] < query_len[:, query_seg]
    seg_ends = jnp.cumsum(lengths, axis=1)
    pass_index = jnp.arange(PTOK, dtype=jnp.int32)
    pass_seg = lax.optimization_barrier(jnp.sum((pass_index[None, :, None] >= seg_ends[:, None, :]).astype(jnp.int32), axis=2))
    segment = jnp.concatenate([jnp.broadcast_to(query_seg[None, :], (GROUPS, QTOK)), QN + pass_seg], axis=1)
    pass_ok = jnp.broadcast_to(pass_index[None, :] >= 0, (GROUPS, PTOK))
    valid = jnp.concatenate([query_ok, pass_ok], axis=1)
    encoded = lax.map(jax.checkpoint(partial(encode_group, weights)), (ordered, segment, valid))
    query_units = encoded[:, :QTOK].reshape(N_PB, N_PA * QTOK, D)
    pass_units = encoded[:, QTOK:]
    slot_pos = jnp.arange(QLEN, dtype=jnp.int32)
    token_valid = slot_pos[None, None, None, :] < query_len.reshape(N_PB, N_PA, QN, 1)
    token_valid = token_valid.reshape(N_PB, N_PA * QTOK).astype(jnp.float32)
    per_group = lax.map(jax.checkpoint(partial(score_group, query_units, token_valid)), (jnp.arange(GROUPS, dtype=jnp.int32), pass_units, pass_seg))
    per_group = per_group.reshape(N_PB, N_PA, N_PA, QN, PN).transpose(0, 2, 3, 1, 4)
    return per_group.reshape(N_PB, N_PA, QN, N_PA * PN)

def reference(rows_in, w_qkv, b_qv, w_out, b_out, ln1_gain, ln1_bias, w_in, b_in, w_fin, b_fin, ln2_gain, ln2_bias, w_head, b_head, lengths, query_len, score_grad):
    floats = [operand.astype(jnp.float32) for operand in (rows_in, w_qkv, b_qv, w_out, b_out, ln1_gain, ln1_bias, w_in, b_in, w_fin, b_fin, ln2_gain, ln2_bias, w_head, b_head)]

    def wrapped(*operands):
        return forward(*operands, lengths, query_len)
    scores, pullback = jax.vjp(wrapped, *floats)
    grads = pullback(score_grad.astype(jnp.float32))
    return (scores, grads[0], grads[1], grads[2], grads[3], grads[4], grads[5], grads[6], grads[7], grads[8], grads[9], grads[10], grads[11], grads[12], grads[13], grads[14])
```

```python
import functools
import math

import jax
import jax.numpy as jnp
from jax import lax
from jax.experimental import pallas as pl
from jax.experimental.pallas import tpu as pltpu
from jax.sharding import PartitionSpec as P

HDIM = 64
QLEN = 32
LANES = 128
SHARP = 0.02
LN_EPS = 1e-05
UNIT_EPS = 1e-06
BIG = -1e30
BF = jnp.bfloat16
F32 = jnp.float32
MIB = 1024 * 1024


def nn(a, b):
    return lax.dot_general(a, b, (((1,), (0,)), ((), ())), preferred_element_type=F32)


def nt(a, b):
    return lax.dot_general(a, b, (((1,), (1,)), ((), ())), preferred_element_type=F32)


def tn(a, b):
    return lax.dot_general(a, b, (((0,), (0,)), ((), ())), preferred_element_type=F32)


def permute_kernel(segments, block, low_bits, info, x_ref, o_ref):
    tiles = x_ref.shape[1] // LANES
    lane = lax.broadcasted_iota(jnp.int32, (1, LANES), 1)
    low = info[tiles]
    for j in range(tiles):
        source = pl.multiple_of(info[j] * LANES, LANES)
        row = 0
        for i, length in enumerate(segments):
            start = pl.multiple_of(info[tiles + 1 + i], 16)
            part = x_ref[pl.ds(start, length), pl.ds(source, LANES)]
            if low_bits:
                part = part.astype(F32)
                for bit in range(low_bits):
                    step = block << bit
                    up = pltpu.roll(part, step, 1)
                    down = pltpu.roll(part, LANES - step, 1)
                    swapped = jnp.where((lane & step) != 0, up, down)
                    part = jnp.where((low & (1 << bit)) != 0, swapped, part)
                part = part.astype(o_ref.dtype)
            o_ref[pl.ds(row, length), pl.ds(j * LANES, LANES)] = part
            row += length


def permute(x, info, segments, block, low_bits):
    rows = sum(segments)
    return pl.pallas_call(
        functools.partial(permute_kernel, segments, block, low_bits),
        out_shape=jax.ShapeDtypeStruct((rows, x.shape[1]), x.dtype),
        in_specs=[
            pl.BlockSpec(memory_space=pltpu.SMEM),
            pl.BlockSpec(memory_space=pltpu.VMEM),
        ],
        out_specs=pl.BlockSpec(memory_space=pltpu.VMEM),
        compiler_params=pltpu.CompilerParams(vmem_limit_bytes=56 * MIB),
        cost_estimate=pl.CostEstimate(
            flops=rows * x.shape[1], bytes_accessed=4 * rows * x.shape[1], transcendentals=0
        ),
    )(info, x)


def pick(sel, a, b):
    return jnp.where(sel, a.astype(F32), b.astype(F32)).astype(BF)


def split3(v):
    hi = v.astype(BF).astype(F32)
    mid = (v - hi).astype(BF).astype(F32)
    return hi, mid, v - hi - mid


def in_columns(col, v, base):
    hi, mid, lo = split3(v)
    return jnp.where(col == 7, hi, jnp.where(col == 8, mid, jnp.where(col == 9, lo, base)))


def attend_kernel(slots, tile_q, n_deps, q_ref, k_ref, v_ref, aq_ref, ak_ref, *rest):
    o_ref, l_ref, kx_ref, vx_ref = rest[n_deps:]
    lane = lax.broadcasted_iota(jnp.int32, (1, LANES), 1)
    col = lane % HDIM
    sides = (lane < HDIM, lane >= HDIM)
    for h, sel in enumerate(sides):
        kx_ref[h] = pick(sel, k_ref[...], ak_ref[...])
        vx_ref[h] = pick(sel, v_ref[...], jnp.ones_like(v_ref[...]))
    keys = k_ref.shape[0]

    def work(q_at, q_n, k_at, k_n):
        rows = pl.ds(q_at, q_n)
        q, aug = q_ref[rows, :], aq_ref[rows, :]
        outs, logs = [], []
        for h, sel in enumerate(sides):
            s = nt(pick(sel, q, aug), kx_ref[h, pl.ds(k_at, k_n), :])
            top = jnp.max(s, axis=1, keepdims=True)
            p = jnp.exp(s - top).astype(BF)
            o = nn(p, vx_ref[h, pl.ds(k_at, k_n), :])
            outs.append(o / pltpu.roll(o, HDIM, 1))
            logs.append(in_columns(col, -(top + jnp.log(o)), aug.astype(F32)))
        o_ref[rows, :] = jnp.where(sides[0], outs[0], outs[1]).astype(BF)
        l_ref[rows, :] = jnp.where(sides[0], logs[1], logs[0]).astype(BF)

    work(0, slots, 0, slots)
    tokens = q_ref.shape[0] - slots

    def step(i, carry):
        work(pl.multiple_of(slots + i * tile_q, 16), tile_q, slots, keys - slots)
        return carry

    lax.fori_loop(0, tokens // tile_q, step, 0)


def attend(qkv, rows, aug_q, aug_k, slots, tile_q, first, count, kept, deps=()):
    keys, width = qkv.shape[0], qkv.shape[1] // 3
    of = lambda n, m: pl.BlockSpec((n, LANES), lambda j: (0, 3 * (first + j) + m))
    out = pl.BlockSpec((rows, LANES), lambda j: (0, first + j))
    fixed = lambda n: pl.BlockSpec((n, LANES), lambda j: (0, 0))
    deps = tuple(kept) + tuple(deps)
    return pl.pallas_call(
        functools.partial(attend_kernel, slots, tile_q, len(deps)),
        grid=(count,),
        out_shape=(jax.ShapeDtypeStruct((rows, width), BF), jax.ShapeDtypeStruct((rows, width), BF)),
        in_specs=[of(rows, 0), of(keys, 1), of(keys, 2), fixed(rows), fixed(keys)]
        + [pl.BlockSpec(memory_space=pl.ANY)] * len(deps),
        out_specs=(out, out),
        input_output_aliases={5 + i: i for i in range(len(kept))},
        scratch_shapes=[pltpu.VMEM((2, keys, LANES), BF), pltpu.VMEM((2, keys, LANES), BF)],
        compiler_params=pltpu.CompilerParams(vmem_limit_bytes=56 * MIB),
        cost_estimate=pl.CostEstimate(
            flops=16 * rows * keys * count * LANES,
            bytes_accessed=2 * (3 * rows + 2 * keys) * count * LANES,
            transcendentals=2 * rows * keys * count,
        ),
    )(qkv, qkv, qkv, aug_q, aug_k, *deps)


def attend_back_kernel(
    slots, tile_k, scale, n_deps,
    q_ref, k_ref, v_ref, o_ref, do_ref, l_ref, ak_ref, *rest,
):
    (
        dqkv_ref, sum_ref,
        qx_ref, qz_ref, dx_ref, dz_ref, kx_ref, vx_ref, kt_ref, acc_ref,
    ) = rest[n_deps:]
    lane = lax.broadcasted_iota(jnp.int32, (1, LANES), 1)
    col = lane % HDIM
    sides = (lane < HDIM, lane >= HDIM)
    rows, keys = q_ref.shape[0], k_ref.shape[0]
    tokens = rows - slots
    grad = do_ref[...].astype(F32)
    prod = grad * o_ref[...].astype(F32)
    zero = jnp.zeros_like(grad)
    for h, sel in enumerate(sides):
        delta = jnp.sum(jnp.where(sel, prod, 0.0), axis=1, keepdims=True)
        qx_ref[h] = pick(sel, q_ref[...], l_ref[...])
        qz_ref[h] = pick(sel, q_ref[...], zero)
        dx_ref[h] = jnp.where(sel, grad, in_columns(col, -delta, zero)).astype(BF)
        dz_ref[h] = jnp.where(sel, grad, 0.0).astype(BF)
        kx_ref[h] = pick(sel, k_ref[...], ak_ref[...])
        vx_ref[h] = pick(sel, v_ref[...], ak_ref[...])
        kt_ref[h] = jnp.where(sel, k_ref[...].astype(F32), 0.0).T.astype(BF)

    def work(q_at, q_n, k_at, k_n, kt_at):
        dq = None
        dk = jnp.zeros((k_n, LANES), F32)
        dv = jnp.zeros((k_n, LANES), F32)
        for h in range(2):
            at, of = pl.ds(k_at, k_n), pl.ds(q_at, q_n)
            p = jnp.exp(nt(kx_ref[h, at, :], qx_ref[h, of, :]))
            dp = nt(vx_ref[h, at, :], dx_ref[h, of, :])
            ds = (p * dp).astype(BF)
            dv += nn(p.astype(BF), dz_ref[h, of, :])
            dk += nn(ds, qz_ref[h, of, :])
            part = nn(kt_ref[h, :, pl.ds(kt_at, k_n)], ds)
            dq = part if dq is None else dq + part
        return dq, dk, dv

    def keep(at, n, dk, dv):
        dqkv_ref[pl.ds(at, n), pl.ds(LANES, LANES)] = dk.astype(BF)
        dqkv_ref[pl.ds(at, n), pl.ds(2 * LANES, LANES)] = dv.astype(BF)

    dq, dk, dv = work(0, slots, 0, slots, 0)
    dq = dq.T * scale
    dqkv_ref[pl.ds(0, slots), pl.ds(0, LANES)] = dq.astype(BF)
    keep(0, slots, dk, dv)
    acc_ref[...] = jnp.zeros_like(acc_ref)
    sum_v = jnp.sum(dv, axis=0, keepdims=True)
    sum_q = jnp.sum(dq, axis=0, keepdims=True)
    for i in range((keys - slots) // tile_k):
        at = slots + i * tile_k
        dq, dk, dv = work(slots, tokens, at, tile_k, at)
        acc_ref[...] += dq
        keep(at, tile_k, dk, dv)
        sum_v += jnp.sum(dv, axis=0, keepdims=True)
    dq = acc_ref[...].T * scale
    dqkv_ref[pl.ds(slots, tokens), pl.ds(0, LANES)] = dq.astype(BF)
    dqkv_ref[pl.ds(rows, keys - rows), pl.ds(0, LANES)] = jnp.zeros((keys - rows, LANES), BF)
    sum_q += jnp.sum(dq, axis=0, keepdims=True)
    sum_ref[pl.ds(0, 1), :] = sum_q
    sum_ref[pl.ds(1, 1), :] = sum_v
    sum_ref[pl.ds(2, 6), :] = jnp.zeros((6, LANES), F32)


def attend_back(qkv, o, do, logs, aug_k, slots, tile_k, scale, first, count, kept, deps=()):
    rows, width = o.shape
    keys = qkv.shape[0]
    of = lambda n, m: pl.BlockSpec((n, LANES), lambda j: (0, 3 * (first + j) + m))
    col = lambda n: pl.BlockSpec((n, LANES), lambda j: (0, first + j))
    fixed = lambda n: pl.BlockSpec((n, LANES), lambda j: (0, 0))
    wide = lambda n: pltpu.VMEM((2, n, LANES), BF)
    deps = tuple(kept) + tuple(deps)
    return pl.pallas_call(
        functools.partial(attend_back_kernel, slots, tile_k, scale, len(deps)),
        grid=(count,),
        out_shape=(
            jax.ShapeDtypeStruct((keys, 3 * width), BF),
            jax.ShapeDtypeStruct((8, width), F32),
        ),
        in_specs=[of(rows, 0), of(keys, 1), of(keys, 2), col(rows), col(rows), col(rows), fixed(keys)]
        + [pl.BlockSpec(memory_space=pl.ANY)] * len(deps),
        out_specs=(pl.BlockSpec((keys, 3 * LANES), lambda j: (0, first + j)), col(8)),
        input_output_aliases={7 + i: i for i in range(len(kept))},
        scratch_shapes=[
            wide(rows), wide(rows), wide(rows), wide(rows), wide(keys), wide(keys),
            pltpu.VMEM((2, LANES, keys), BF),
            pltpu.VMEM((LANES, rows - slots), F32),
        ],
        compiler_params=pltpu.CompilerParams(vmem_limit_bytes=56 * MIB),
        cost_estimate=pl.CostEstimate(
            flops=40 * rows * keys * count * LANES,
            bytes_accessed=2 * (6 * rows + 4 * keys) * count * LANES,
            transcendentals=2 * rows * keys * count,
        ),
    )(qkv, qkv, qkv, o, do, logs, aug_k, *deps)


def nothing(*refs):
    return None


def tie(x, *deps):
    anywhere = pl.BlockSpec(memory_space=pl.ANY)
    return pl.pallas_call(
        nothing,
        out_shape=jax.ShapeDtypeStruct(x.shape, x.dtype),
        in_specs=[anywhere] * (1 + len(deps)),
        out_specs=anywhere,
        input_output_aliases={0: 0},
        cost_estimate=pl.CostEstimate(flops=0, bytes_accessed=0, transcendentals=0),
    )(x, *deps)


def chunk_of(m):
    return m if m <= 704 else m // 2


def mm_in_kernel(chunk, epilogue, start, finish, n_extra, n_deps, a_ref, h_ref, r_ref, *rest):
    extra, outs = rest[:n_extra], rest[n_extra + n_deps :]
    k = h_ref.shape[0]

    def step(i, carry):
        rows = pl.ds(pl.multiple_of(i * chunk, 16), chunk)
        acc = nn(a_ref[rows, pl.ds(0, k)], h_ref[...]) + nn(a_ref[rows, pl.ds(k, k)], r_ref[...])
        return epilogue(acc, rows, extra, outs, carry)

    last = lax.fori_loop(0, a_ref.shape[0] // chunk, step, start(h_ref.shape[1]))
    finish(last, outs)


def nought(tn):
    return 0


def leave(carry, outs):
    return None


def mm_in(a, h, r, col, width, tn, epilogue, extra, outs, start=nought, finish=leave, deps=()):
    m, k = a.shape[0], h.shape[0] // 2
    tiles = width // tn
    weight = pl.BlockSpec((k, tn), lambda t, j: (t, col // tn + j))
    wide = lambda n: pl.BlockSpec((n, tn), lambda t, j: (0, t * tiles + j))
    return pl.pallas_call(
        functools.partial(mm_in_kernel, chunk_of(m), epilogue, start, finish, len(extra), len(deps)),
        grid=(2, tiles),
        out_shape=tuple(jax.ShapeDtypeStruct((n, 2 * width), dt) for n, dt in outs),
        in_specs=[pl.BlockSpec((m, 2 * k), lambda t, j: (0, 0)), weight, weight]
        + [wide(e.shape[0]) for e in extra]
        + [pl.BlockSpec(memory_space=pl.ANY)] * len(deps),
        out_specs=tuple(wide(n) for n, _ in outs),
        compiler_params=pltpu.CompilerParams(vmem_limit_bytes=56 * MIB),
        cost_estimate=pl.CostEstimate(
            flops=8 * m * k * width,
            bytes_accessed=4 * m * k + 8 * k * width + sum(2 * width * n * 2 for n, _ in outs),
            transcendentals=0,
        ),
    )(a, h, r, *extra, *deps)


def mm_out_kernel(chunk, half_tiles, n_extra, epilogue, a0_ref, a1_ref, h0_ref, h1_ref, r0_ref, r1_ref, *rest):
    extra, o_ref = rest[:n_extra], rest[-1]

    def run(w0_ref, w1_ref):
        def step(i, carry):
            rows = pl.ds(pl.multiple_of(i * chunk, 16), chunk)
            acc = nt(a0_ref[rows, :], w0_ref[...]) + nt(a1_ref[rows, :], w1_ref[...])
            more = [e[rows, :] if e.shape[0] > 8 else e[pl.ds(0, 1), :] for e in extra]
            o_ref[rows, :] = epilogue(acc, *more).astype(o_ref.dtype)
            return carry

        lax.fori_loop(0, a0_ref.shape[0] // chunk, step, 0)

    i = pl.program_id(0)

    @pl.when(i < half_tiles)
    def _():
        run(h0_ref, h1_ref)

    @pl.when(i >= half_tiles)
    def _():
        run(r0_ref, r1_ref)


def mm_out(a, m, h, r, col, width, td, epilogue, extra, dtype, deps=()):
    k = h.shape[0] // 2
    half = k // td
    at = col // width
    lhs = lambda t: pl.BlockSpec((m, width), lambda i: (0, t))
    own = lambda t: pl.BlockSpec((td, width), lambda i: (t * half + jnp.minimum(i, half - 1), at))
    oth = lambda t: pl.BlockSpec((td, width), lambda i: (t * half + jnp.maximum(i - half, 0), at))
    wide = lambda n: pl.BlockSpec((n, td), lambda i: (0, i))
    return pl.pallas_call(
        functools.partial(mm_out_kernel, chunk_of(m), half, len(extra), epilogue),
        grid=(2 * half,),
        out_shape=jax.ShapeDtypeStruct((m, 2 * k), dtype),
        in_specs=[lhs(0), lhs(1), own(0), own(1), oth(0), oth(1)]
        + [wide(e.shape[0]) for e in extra]
        + [pl.BlockSpec(memory_space=pl.ANY)] * len(deps),
        out_specs=wide(m),
        compiler_params=pltpu.CompilerParams(vmem_limit_bytes=56 * MIB),
        cost_estimate=pl.CostEstimate(
            flops=8 * m * k * width,
            bytes_accessed=4 * m * width + 8 * k * width + 8 * m * k,
            transcendentals=0,
        ),
    )(a, a, h, h, r, r, *extra, *deps)


def put_plain(acc, rows, extra, outs, carry):
    outs[0][rows, :] = acc.astype(outs[0].dtype)
    return carry


def put_biased(acc, rows, extra, outs, carry):
    outs[0][rows, :] = (acc + extra[0][pl.ds(0, 1), :]).astype(outs[0].dtype)
    return carry


def put_scaled(acc, rows, extra, outs, carry):
    low = (acc + extra[0][pl.ds(0, 1), :]).astype(BF).astype(F32)
    outs[0][rows, :] = (low * extra[0][pl.ds(1, 1), :]).astype(BF)
    return carry


def put_gelu(acc, rows, extra, outs, carry):
    inner = acc + extra[0][pl.ds(0, 1), :]
    cdf, pdf = normal_parts(inner)
    outs[0][rows, :] = (inner * cdf).astype(BF)
    outs[1][rows, :] = (cdf + inner * pdf).astype(BF)
    return carry


def put_sloped(acc, rows, extra, outs, carry):
    grad = acc * extra[0][rows, :].astype(F32)
    outs[0][rows, :] = grad.astype(BF)
    return carry + jnp.sum(grad, axis=0, keepdims=True)


def row_of_zeros(tn):
    return jnp.zeros((1, tn), F32)


def put_sum(carry, outs):
    outs[1][...] = jnp.broadcast_to(carry, outs[1].shape)


def eight(*rows):
    return jnp.concatenate([jnp.stack(rows), jnp.zeros((8 - len(rows), rows[0].shape[0]), F32)])


def normal_parts(v):
    t = 1.0 / (1.0 + (0.3275911 * math.sqrt(0.5)) * jnp.abs(v))
    bell = jnp.exp(-0.5 * v * v)
    poly = 0.5 * 1.061405429 * t - 0.5 * 1.453152027
    poly = (poly * t + 0.5 * 1.421413741) * t - 0.5 * 0.284496736
    tail = ((poly * t + 0.5 * 0.254829592) * t) * bell
    return jnp.where(v < 0.0, tail, 1.0 - tail), bell * (1.0 / math.sqrt(2.0 * math.pi))


def norm_parts(v):
    centered = v - jnp.mean(v, axis=-1, keepdims=True)
    rstd = lax.rsqrt(jnp.mean(centered * centered, axis=-1, keepdims=True) + LN_EPS)
    return centered * rstd, rstd


def norm_back(c, vhat, rstd, gain):
    gc = c * gain
    back = (
        gc
        - jnp.mean(gc, axis=-1, keepdims=True)
        - vhat * jnp.mean(gc * vhat, axis=-1, keepdims=True)
    ) * rstd
    return back, jnp.sum(c * vhat, axis=0), jnp.sum(c, axis=0)


def make(n_pb, n_pa, n_ta):
    cores = 2
    n_x = n_pb // cores
    blocks = n_pb * n_pa

    def px(v, k):
        return lax.ppermute(v, "pb", [(i, i ^ (cores * k)) for i in range(n_pb)])

    def pc(v):
        return lax.ppermute(v, "pb", [(i, i ^ 1) for i in range(n_pb)])

    def pz(v, k):
        return lax.ppermute(v, "pa", [(i, i ^ k) for i in range(n_pa)])

    def py(v):
        return lax.ppermute(v, "ta", [(i, i ^ 1) for i in range(n_ta)])

    x_bits = n_x.bit_length() - 1
    z_bits = n_pa.bit_length() - 1

    def gather_z_step(have, bit):
        other = pz(have, 1 << bit)
        return jnp.stack([have, other], axis=1).reshape((-1,) + have.shape[1:])

    def gather_z_rest(have):
        for bit in reversed(range(z_bits - 1)):
            have = gather_z_step(have, bit)
        return have.reshape(-1, have.shape[-1])

    def gather_z(shard):
        return gather_z_rest(gather_z_step(shard[None], z_bits - 1))

    def gather_x(a):
        have = a[None]
        for bit in range(x_bits):
            have = jnp.concatenate([have, px(have, 1 << bit)], axis=0)
        return have

    def halves_of(a):
        n = a.shape[0] // 2
        return a[:n], a[n:]

    def gather_xy_one(near, far):
        return gather_x(near), py(far)

    def gather_xy_two(near, far, far_oth):
        n = far.shape[0]
        both = gather_x(jnp.concatenate([far, far_oth], axis=0))
        near_oth = py(near)
        own = jnp.concatenate([near, both[:, :n]], axis=1)
        oth = jnp.concatenate([near_oth, both[:, n:]], axis=1)
        cols = far.shape[1]
        return jnp.concatenate([own.reshape(-1, cols), oth.reshape(-1, cols)], axis=0)

    def add(a, b):
        return (a.astype(F32) + b.astype(F32)).astype(a.dtype)

    def away_part(lhs, rhs):
        return pc(tn(lhs[:, lhs.shape[1] // 2 :], rhs).astype(BF))

    def core_part(lhs, rhs, away):
        return (tn(lhs[:, : lhs.shape[1] // 2], rhs) + away.astype(F32)).astype(BF)

    def cut(parts, x, s, sides):
        size = parts[0].shape[0] // n_x
        half = size // 2
        row = x * size + s * half
        out = []
        for t in sides:
            for r in parts:
                n = r.shape[1] // n_ta
                out.append(r[row : row + half, t * n : (t + 1) * n])
        return jnp.concatenate(out, axis=1) if len(out) > 1 else out[0]

    def p1_send(parts):
        near = [cut(parts, k, 0, (0, 1)) for k in range(n_x)]
        far_own = jnp.concatenate([cut(parts, k, 1, (0,)) for k in range(n_x)], axis=0)
        far_oth = jnp.concatenate([cut(parts, k, 1, (1,)) for k in range(n_x)], axis=0)
        return near, far_own, far_oth

    def p1_go(sent):
        near, far_own, far_oth = sent
        return [px(near[k], k) for k in range(1, n_x)], py(far_oth)

    def p1_end(sent, got):
        near = sent[0][0]
        for g in got[0]:
            near = add(near, g)
        far = add(sent[1], got[1])
        n = near.shape[1] // 2
        half = far.shape[0] // n_x
        return near[:, :n], near[:, n:], [far[k * half : (k + 1) * half] for k in range(n_x)]

    def p2_go(state):
        near_own, near_oth, far = state
        return py(near_oth), [px(far[k], k) for k in range(1, n_x)]

    def p2_end(state, got, w):
        near = add(state[0], got[0])
        far = state[2][0]
        for g in got[1]:
            far = add(far, g)
        return jnp.concatenate([near, far], axis=0).reshape(n_pa, w, -1)

    def z_split(cur):
        cur = cur.reshape((cur.shape[0] // 2, 2) + cur.shape[1:])
        return cur[:, 0], cur[:, 1]

    def reduce_z(cur, first=0):
        for bit in range(first, z_bits):
            keep, give = z_split(cur)
            got = pz(give, 1 << bit)
            cur = add(keep, got) if bit < z_bits - 1 else keep.astype(F32) + got.astype(F32)
        return cur[0]

    def on_device(
        rows_in, w_qkv, b_qv, w_out, b_out, ln1_gain, ln1_bias, w_in, b_in, w_fin, b_fin,
        ln2_gain, ln2_bias, w_head, b_head, lengths, query_len, score_grad,
    ):
        t0 = lax.axis_index("ta")
        z0 = lax.axis_index("pa")
        p0 = lax.axis_index("pb")
        x0, c0 = p0 // cores, p0 % cores
        first_t = t0 == 0
        all_rows, width = rows_in.shape
        half_rows = all_rows // n_ta
        n_q, n_p = query_len.shape[1], lengths.shape[1]
        q_here = n_q // n_ta
        slots = q_here * QLEN
        toks = half_rows - slots
        block = width // blocks
        heads_half = w_qkv.shape[2]
        scale = 1.0 / math.sqrt(HDIM)

        per_tile = LANES // block
        z_tiles = n_pa // per_tile
        low_bits = per_tile.bit_length() - 1
        forward, backward = [], []
        for c in range(cores):
            for x in range(n_x):
                for z in range(z_tiles):
                    forward.append((((x ^ x0) * cores) + (c ^ c0)) * z_tiles + (z ^ (z0 // per_tile)))
        for x in range(n_x):
            for c in range(cores):
                for z in range(z_tiles):
                    backward.append((((c ^ c0) * n_x) + (x ^ x0)) * z_tiles + (z ^ (z0 // per_tile)))
        low = z0 % per_tile
        as_info = lambda v: jnp.stack([jnp.asarray(a, jnp.int32) for a in v])
        row_info = as_info(forward + [low, t0 * half_rows, (1 - t0) * half_rows + slots])
        vec_info = as_info(forward + [low, 0])
        back_info = as_info(backward + [low, 0])

        rows = permute(rows_in, row_info, (half_rows, toks), block, low_bits)
        vecs = jnp.stack(
            [b_out, ln1_gain, ln1_bias, b_fin, ln2_gain, ln2_bias, b_out, b_out]
        )
        vecs = permute(vecs, vec_info, (8,), block, low_bits)
        b_out_r, g1, be1, b_fin_r, g2, be2 = (vecs[i] for i in range(6))
        pairs = heads_half // LANES
        all_pairs = n_ta * pairs
        ff_half = w_in.shape[1]
        head_half = width // n_ta
        qkv_half = 3 * heads_half
        swapped = lambda v: jnp.concatenate([v[..., v.shape[-1] // 2 :], v[..., : v.shape[-1] // 2]], axis=-1)
        in_order = lambda v: jnp.where(first_t, v, swapped(v))

        packed = lambda v: v.reshape(v.shape[0], 3, pairs, LANES).transpose(0, 2, 1, 3)
        shard_q = packed(w_qkv.transpose(1, 0, 2).reshape(block, qkv_half)).reshape(block, -1)
        shard_m = jnp.concatenate([w_in, w_out.T], axis=1)
        head_mine = lax.dynamic_slice_in_dim(w_head, t0 * head_half, head_half, 1)
        shard_e = jnp.concatenate([w_fin.T, head_mine], axis=1)

        zq = gather_z(shard_q)
        near, far = halves_of(zq)
        zm_1 = gather_z_step(tie(shard_m, zq)[None], z_bits - 1)
        near_q, oth_q = gather_xy_one(near, far)
        near_q = tie(near_q, zm_1)
        zm = gather_z_rest(zm_1)
        h_q = tie(gather_xy_two(near_q, far, oth_q), zm)
        r_q = pc(h_q)
        near, far_m = halves_of(zm)
        near_m, oth_m = gather_xy_one(near, far_m)
        ze_1 = gather_z_step(tie(shard_e, zm)[None], z_bits - 1)
        bias_of = lambda b: packed(jnp.concatenate([b[0], jnp.zeros_like(b[0]), b[1]])[None]).reshape(-1)
        qkv_bias = jnp.concatenate([bias_of(b_qv), bias_of(py(b_qv))])
        b_in_r = jnp.concatenate([b_in, py(b_in)])

        row_id = jnp.arange(half_rows + toks, dtype=jnp.int32)
        is_slot = row_id < slots
        token = jnp.where(
            row_id < half_rows, t0 * toks + row_id - slots, (1 - t0) * toks + row_id - half_rows
        )
        ends = jnp.cumsum(lengths[0])
        pid = jnp.sum((token[:, None] >= ends[None, :]).astype(jnp.int32), axis=1)
        q_lens = lax.dynamic_index_in_dim(query_len, z0, 0, keepdims=False)
        q_lens = lax.dynamic_slice_in_dim(q_lens, t0 * q_here, q_here, 0)
        limit = jnp.sum(
            jnp.where(
                (row_id // QLEN)[:, None] == jnp.arange(q_here, dtype=jnp.int32)[None, :],
                q_lens[None, :], 0,
            ),
            axis=1,
        )
        dead = is_slot & (row_id % QLEN >= limit)
        seg = jnp.where(is_slot, n_p + row_id // QLEN, pid)
        lane_c = jnp.arange(LANES, dtype=jnp.int32)[None, :] % HDIM
        same = seg[:, None] == lane_c
        aug_k = jnp.where(
            lane_c < 6, same & ~dead[:, None], jnp.where(lane_c == 6, dead[:, None], (lane_c >= 7) & (lane_c < 10))
        )
        aug_k = aug_k.astype(BF)
        aug_q = jnp.where((lane_c < 7) & ~same[:half_rows], BIG, 0.0).astype(BF)

        col_scale = jnp.tile(jnp.repeat(jnp.array([scale, 1.0, 1.0], F32), LANES), all_pairs)
        (qkv,) = mm_in(
            rows, h_q, r_q, 0, qkv_half, qkv_half // 3, put_scaled, (eight(qkv_bias, col_scale),),
            ((half_rows + toks, BF),),
        )
        oth_m, near_m = tie(oth_m, qkv), tie(near_m, qkv)
        h_m = gather_xy_two(near_m, far_m, oth_m)
        ze_1 = tie(ze_1, qkv)
        ze = gather_z_rest(ze_1)
        kept, n_call = (), all_pairs // 4
        for i in range(4):
            kept = attend(
                qkv, half_rows, aug_q, aug_k, slots, toks // 2, i * n_call, n_call, kept,
                ((oth_m, near_m, ze_1), (), (ze,), ())[i],
            )
            if i == 1:
                ze = tie(ze, kept[0])
                near, far_e = halves_of(ze)
                near_e, oth_e = gather_xy_one(near, far_e)
            if i == 2:
                h_m = tie(h_m, kept[0])
                r_m = pc(h_m)
        ctx, logs = kept
        near_e, oth_e = tie(near_e, kept[0]), tie(oth_e, kept[0])
        h_one = mm_out(
            ctx, half_rows, h_m, r_m, ff_half, heads_half, heads_half // 2,
            lambda acc, res, b: acc + res.astype(F32) + b, (rows[:half_rows], eight(b_out_r)), F32,
            (near_e, oth_e),
        )
        h_e = gather_xy_two(near_e, far_e, oth_e)
        v1, r1 = norm_parts(h_one)
        normed = v1 * g1 + be1
        normed_low = normed.astype(BF)
        active, slope = mm_in(
            normed_low, h_m, r_m, 0, ff_half, ff_half // 4, put_gelu, (eight(b_in_r),),
            ((half_rows, BF), (half_rows, BF)),
        )
        h_e = tie(h_e, active)
        r_e = pc(h_e)
        h_two = mm_out(
            active, half_rows, h_e, r_e, 0, ff_half, heads_half // 2,
            lambda acc, res, b: acc + res + b, (normed, eight(b_fin_r)), F32,
        )
        v2, r2 = norm_parts(h_two)
        output_low = (v2 * g2 + be2).astype(BF)
        (raw,) = mm_in(
            output_low, h_e, r_e, ff_half, head_half, head_half, put_biased,
            (eight(in_order(b_head)),), ((half_rows, F32),),
        )
        inv = lax.rsqrt(jnp.sum(raw * raw, axis=-1, keepdims=True) + UNIT_EPS)
        unit = raw * inv
        unit_low = unit.astype(BF)

        passages = unit_low[slots:]
        mine = gather_z(unit_low[:slots])
        asked = jnp.concatenate([mine, swapped(py(mine))], axis=0)
        n_asked = asked.shape[0]
        z_rel = jnp.arange(n_pa, dtype=jnp.int32) ^ z0
        swap_t = lambda a: jnp.where(first_t, a, a[::-1])
        lens = swap_t(
            jnp.take(query_len, z_rel, axis=0).reshape(n_pa, n_ta, q_here).transpose(1, 0, 2)
        )
        valid = (
            jnp.arange(QLEN, dtype=jnp.int32)[None, None, None, :] < lens[..., None]
        ).astype(F32)
        up = swap_t(
            jnp.take(score_grad[0], z_rel, axis=0).reshape(n_pa, n_ta, q_here, n_p).transpose(1, 0, 2, 3)
        )
        token_grad = (up[:, :, :, None, :] * valid[..., None]).reshape(n_asked, n_p)
        member = (
            pid[slots:half_rows, None] == jnp.arange(n_p, dtype=jnp.int32)[None, :]
        ).astype(F32)
        powers = jnp.exp(nt(asked, passages) * (1.0 / SHARP))
        sums = jnp.dot(powers, member, precision=lax.Precision.HIGHEST)
        theirs = py(sums.reshape(n_ta, n_asked // n_ta, n_p)[::-1])
        sums = sums + theirs.reshape(n_asked, n_p)
        soft = (SHARP * jnp.log(sums)).reshape(n_ta, n_pa, q_here, QLEN, n_p)
        scores = jnp.sum(soft[0] * valid[0][..., None], axis=2)
        scores = jnp.take(scores, z_rel, axis=0)[None]
        coef = token_grad / sums
        coef_j = sum(coef[:, i : i + 1] * member[:, i][None, :] for i in range(n_p))
        sim_grad = (powers * coef_j).astype(BF)
        ask_grad = nn(sim_grad, passages).astype(BF).reshape(n_ta, n_pa * slots, width)
        ask_sum = add(ask_grad[0], py(swapped(ask_grad[1])))
        passage_grad = tn(sim_grad, asked)
        unit_grad = jnp.concatenate(
            [reduce_z(ask_sum.reshape(n_pa, slots, width)), passage_grad], axis=0
        )

        raw_grad = inv * (unit_grad - unit * jnp.sum(unit * unit_grad, axis=-1, keepdims=True))
        g_b_head = in_order(jnp.sum(raw_grad, axis=0))
        raw_low = raw_grad.astype(BF)
        output_grad = mm_out(
            raw_low, half_rows, h_e, r_e, ff_half, head_half, heads_half // 2, lambda acc: acc, (), F32
        )
        h_two_grad, g_g2, g_be2 = norm_back(output_grad, v2, r2, g2)
        g_b_fin = jnp.sum(h_two_grad, axis=0)
        branch_low = h_two_grad.astype(BF)
        away_fin = away_part(branch_low, active)
        away_head = away_part(output_low, raw_low)
        inner_low, sums_in = mm_in(
            branch_low, h_e, r_e, 0, ff_half, ff_half // 4, put_sloped, (slope,),
            ((half_rows, BF), (8, F32)), row_of_zeros, put_sum,
        )
        part_fin = core_part(branch_low, active, away_fin)
        part_head = core_part(output_low, raw_low, away_head)
        sent_f = p1_send([part_fin, part_head])
        got_f = p1_go(sent_f)
        away_in = away_part(normed_low, inner_low)
        normed_grad = mm_out(
            inner_low, half_rows, h_m, r_m, 0, ff_half, heads_half // 2,
            lambda acc, res: acc + res, (h_two_grad,), F32, (sent_f[0][-1], sent_f[2]),
        )
        h_one_grad, g_g1, g_be1 = norm_back(normed_grad, v1, r1, g1)
        g_b_out = jnp.sum(h_one_grad, axis=0)
        attended_low = h_one_grad.astype(BF)
        away_out = away_part(attended_low, ctx)
        (d_ctx,) = mm_in(
            attended_low, h_m, r_m, ff_half, heads_half, heads_half, put_plain, (), ((half_rows, BF),)
        )
        part_in = core_part(normed_low, inner_low, away_in)
        part_out = core_part(attended_low, ctx, away_out)
        sent_m = p1_send([part_in, part_out])
        got_m = p1_go(sent_m)
        state_f = p1_end(sent_f, got_f)
        got_f = p2_go(state_f)

        back = lambda i, kept, deps: attend_back(
            qkv, ctx, d_ctx, logs, aug_k, slots, toks // 5, scale,
            ((i + 2) % 4) * n_call, n_call, kept, deps,
        )
        quarter = qkv_half // 2
        columns = lambda a, i: a[:, i * quarter : (i + 1) * quarter]
        rows_x = width // (cores * n_x)
        x_blocks = lambda part: [part[k * rows_x : (k + 1) * rows_x] for k in range(n_x)]
        x_go = lambda blocks_of: [px(blocks_of[k], k) for k in range(1, n_x)]

        def x_end(blocks_of, got):
            total = blocks_of[0]
            for g in got:
                total = add(total, g)
            return total

        kept = back(0, (), (sent_m[0][-1], sent_m[2], state_f[1], state_f[2][-1]))
        cur_f = tie(p2_end(state_f, got_f, block), kept[1])
        keep_f, give_f = z_split(cur_f)
        z_f = pz(give_f, 1)
        kept = back(1, kept, (give_f,))
        away_1 = away_part(rows, kept[0][:, qkv_half:])
        state_m = p1_end(sent_m, [[tie(g, kept[1]) for g in got_m[0]], tie(got_m[1], kept[1])])
        got_m = p2_go(state_m)
        cur_f = tie(add(keep_f, z_f), kept[1])
        part_1 = core_part(rows, kept[0][:, qkv_half:], away_1)
        sent_1 = x_blocks(part_1)
        got_1 = x_go(sent_1)
        kept = back(2, kept, (state_m[1], state_m[2][-1], cur_f, sent_1[1]))
        away_2 = away_part(rows, columns(kept[0], 0))
        cur_m = tie(p2_end(state_m, got_m, block), kept[1])
        keep_m, give_m = z_split(cur_m)
        z_m = pz(give_m, 1)
        out_f = reduce_z(cur_f, 1)
        y_1 = x_end(sent_1, [tie(g, kept[1]) for g in got_1])
        part_2 = core_part(rows, columns(kept[0], 0), away_2)
        sent_2 = x_blocks(part_2)
        got_2 = x_go(sent_2)
        kept = back(3, kept, (give_m, y_1, sent_2[1]))
        d_qkv, sums_qv = kept
        y_1 = tie(py(y_1), sums_qv)
        to_other = mm_out(
            d_qkv[half_rows:], toks, h_q, r_q, 0, qkv_half, heads_half // 2, lambda acc: acc, (), BF
        )
        to_other = py(to_other)
        away_3 = away_part(rows, columns(d_qkv, 1))
        out_m = reduce_z(add(keep_m, z_m), 1)
        part_3 = core_part(rows, columns(d_qkv, 1), away_3)
        sent_3 = x_blocks(part_3)
        got_3 = x_go(sent_3)
        grad_rows = mm_out(
            d_qkv, half_rows, h_q, r_q, 0, qkv_half, heads_half // 2,
            lambda acc, res: acc + res, (h_one_grad,), F32,
        )
        as_z = lambda a: a.reshape(n_pa, block, -1)
        out_2 = reduce_z(as_z(add(x_end(sent_2, got_2), y_1[:, :quarter])))
        out_3 = reduce_z(as_z(add(x_end(sent_3, got_3), y_1[:, quarter:])))
        out_q = jnp.concatenate([out_2, out_3], axis=1)
        g_w_qkv = out_q.reshape(block, pairs, 3, LANES).transpose(2, 0, 1, 3).reshape(3, block, heads_half)
        g_w_fin, g_head = out_f[:, :ff_half], out_f[:, ff_half:]
        g_w_in, g_w_out = out_m[:, :ff_half], out_m[:, ff_half:]
        n_h = block // n_ta
        head_keep = jnp.where(first_t, g_head[:n_h], g_head[n_h:])
        head_got = py(jnp.where(first_t, g_head[n_h:], g_head[:n_h]))
        g_w_head = in_order(jnp.concatenate([head_keep, head_got], axis=1))
        grad_rows = grad_rows + jnp.concatenate(
            [jnp.zeros((slots, width), F32), to_other.astype(F32)], axis=0
        )
        grad_rows = permute(grad_rows, back_info, (half_rows,), block, low_bits)

        rel = jnp.arange(blocks, dtype=jnp.int32)
        rel_c, rel_x, rel_z = rel // (n_x * n_pa), (rel // n_pa) % n_x, rel % n_pa
        source = ((rel_x ^ x0) * cores + (rel_c ^ c0)) * n_pa + (rel_z ^ z0)
        by_block = lambda v: v.reshape(blocks, n_ta, -1)
        absolute = jnp.concatenate(
            [by_block(in_order(v)) for v in (sums_in[0], sums_qv[0], sums_qv[1])] + [by_block(g_b_head)],
            axis=2,
        )
        absolute = jnp.take(absolute, source, axis=0)
        vec = jnp.concatenate(
            [absolute] + [by_block(v) for v in (g_b_out, g_g1, g_be1, g_b_fin, g_g2, g_be2)], axis=2
        )
        vec = jnp.where(first_t, vec, vec[:, ::-1]).reshape(cores, blocks // cores, n_ta, -1)
        vec = vec[0] + pc(vec[1])
        vec = vec.reshape(n_x, n_pa, n_ta, -1)
        total = vec[0]
        for k in range(1, n_x):
            total = total + px(vec[k], k)
        vec = reduce_z(total[:, 0] + py(total[:, 1]))
        w32 = width // (blocks * n_ta)
        sizes = [n_ta * ff_half // (blocks * n_ta)] + [w32] * 9
        offs = [sum(sizes[:i]) for i in range(len(sizes) + 1)]
        (o_b_in, o_bq, o_bv, o_b_head, o_b_out, o_g1, o_be1, o_b_fin, o_g2, o_be2) = (
            vec[offs[i] : offs[i + 1]] for i in range(10)
        )
        return (
            scores, grad_rows, g_w_qkv, jnp.stack([o_bq, o_bv]), g_w_out.T, o_b_out, o_g1, o_be1,
            g_w_in, o_b_in, g_w_fin.T, o_b_fin, o_g2, o_be2, g_w_head, o_b_head,
        )

    return on_device


def solution(mesh):
    both = ("pb", "pa")
    every = ("pb", "pa", "ta")
    in_specs = (
        P(both, None), P(None, both, "ta"), P(None, "ta"), P("ta", both), P(), P(), P(),
        P(both, "ta"), P("ta"), P("ta", both), P(), P(), P(), P(both, None), P(),
        P(both, None), P("pb", None), P("pb", None, None, "pa"),
    )
    out_specs = (
        P("pb", None, "ta", "pa"), P(every, None), P(None, both, "ta"), P(None, every),
        P("ta", both), P(every), P(every), P(every), P(both, "ta"), P(every), P("ta", both),
        P(every), P(every), P(every), P(every, None), P(every),
    )
    step = make(mesh.shape["pb"], mesh.shape["pa"], mesh.shape["ta"])
    return jax.shard_map(step, mesh=mesh, in_specs=in_specs, out_specs=out_specs, check_vma=False)
```

```python
import functools
import math

import jax
import jax.numpy as jnp
from jax import lax
from jax.experimental import pallas as pl
from jax.experimental.pallas import tpu as pltpu
from jax.sharding import PartitionSpec as P

HDIM = 64
QLEN = 32
LANES = 128
SHARP = 0.02
LN_EPS = 1e-05
UNIT_EPS = 1e-06
BIG = -1e30
BF = jnp.bfloat16
F32 = jnp.float32
MIB = 1024 * 1024


def nn(a, b):
    return lax.dot_general(a, b, (((1,), (0,)), ((), ())), preferred_element_type=F32)


def nt(a, b):
    return lax.dot_general(a, b, (((1,), (1,)), ((), ())), preferred_element_type=F32)


def tn(a, b):
    return lax.dot_general(a, b, (((0,), (0,)), ((), ())), preferred_element_type=F32)


def permute_kernel(segments, block, low_bits, skip, info, x_ref, *rest):
    o_ref = rest[-1]
    tiles = x_ref.shape[1] // LANES
    lane = lax.broadcasted_iota(jnp.int32, (1, LANES), 1)
    low = info[tiles]
    for j in range(tiles):
        source = pl.multiple_of(info[j] * LANES, LANES)
        row = 0
        for i, length in enumerate(segments):
            start = pl.multiple_of(info[tiles + 1 + i], 16)
            part = x_ref[pl.ds(start, length), pl.ds(source, LANES)]
            if skip is not None:
                more = rest[0][:, pl.ds(source, LANES)].astype(F32)
                part = jnp.concatenate([part[:skip], part[skip:] + more], axis=0)
            if low_bits:
                part = part.astype(F32)
                for bit in range(low_bits):
                    step = block << bit
                    up = pltpu.roll(part, step, 1)
                    down = pltpu.roll(part, LANES - step, 1)
                    swapped = jnp.where((lane & step) != 0, up, down)
                    part = jnp.where((low & (1 << bit)) != 0, swapped, part)
                part = part.astype(o_ref.dtype)
            o_ref[pl.ds(row, length), pl.ds(j * LANES, LANES)] = part
            row += length


def permute(x, info, segments, block, low_bits, skip=None, more=()):
    rows = sum(segments)
    return pl.pallas_call(
        functools.partial(permute_kernel, segments, block, low_bits, skip),
        out_shape=jax.ShapeDtypeStruct((rows, x.shape[1]), x.dtype),
        in_specs=[
            pl.BlockSpec(memory_space=pltpu.SMEM),
            pl.BlockSpec(memory_space=pltpu.VMEM),
        ]
        + [pl.BlockSpec(memory_space=pltpu.VMEM)] * len(more),
        out_specs=pl.BlockSpec(memory_space=pltpu.VMEM),
        compiler_params=pltpu.CompilerParams(vmem_limit_bytes=56 * MIB),
        cost_estimate=pl.CostEstimate(
            flops=rows * x.shape[1], bytes_accessed=4 * rows * x.shape[1], transcendentals=0
        ),
    )(info, x, *more)


def pick(sel, a, b):
    return jnp.where(sel, a.astype(F32), b.astype(F32)).astype(BF)


def split3(v):
    hi = v.astype(BF).astype(F32)
    mid = (v - hi).astype(BF).astype(F32)
    return hi, mid, v - hi - mid


def in_columns(col, v, base):
    hi, mid, lo = split3(v)
    return jnp.where(col == 7, hi, jnp.where(col == 8, mid, jnp.where(col == 9, lo, base)))


def attend_kernel(slots, tile_q, n_deps, q_ref, k_ref, v_ref, aq_ref, ak_ref, *rest):
    o_ref, l_ref, kx_ref, vx_ref = rest[n_deps:]
    lane = lax.broadcasted_iota(jnp.int32, (1, LANES), 1)
    col = lane % HDIM
    sides = (lane < HDIM, lane >= HDIM)
    for h, sel in enumerate(sides):
        kx_ref[h] = pick(sel, k_ref[...], ak_ref[...])
        vx_ref[h] = pick(sel, v_ref[...], jnp.ones_like(v_ref[...]))
    keys = k_ref.shape[0]

    def work(q_at, q_n, k_at, k_n):
        rows = pl.ds(q_at, q_n)
        q, aug = q_ref[rows, :], aq_ref[rows, :]
        outs, logs = [], []
        for h, sel in enumerate(sides):
            s = nt(pick(sel, q, aug), kx_ref[h, pl.ds(k_at, k_n), :])
            top = jnp.max(s, axis=1, keepdims=True)
            p = jnp.exp(s - top).astype(BF)
            o = nn(p, vx_ref[h, pl.ds(k_at, k_n), :])
            outs.append(o / pltpu.roll(o, HDIM, 1))
            logs.append(in_columns(col, -(top + jnp.log(o)), aug.astype(F32)))
        o_ref[rows, :] = jnp.where(sides[0], outs[0], outs[1]).astype(BF)
        l_ref[rows, :] = jnp.where(sides[0], logs[1], logs[0]).astype(BF)

    work(0, slots, 0, slots)
    tokens = q_ref.shape[0] - slots

    def step(i, carry):
        work(pl.multiple_of(slots + i * tile_q, 16), tile_q, slots, keys - slots)
        return carry

    lax.fori_loop(0, tokens // tile_q, step, 0)


def attend(qkv, rows, aug_q, aug_k, slots, tile_q, first, count, kept, deps=()):
    keys, width = qkv.shape[0], qkv.shape[1] // 3
    of = lambda n, m: pl.BlockSpec((n, LANES), lambda j: (0, 3 * (first + j) + m))
    out = pl.BlockSpec((rows, LANES), lambda j: (0, first + j))
    fixed = lambda n: pl.BlockSpec((n, LANES), lambda j: (0, 0))
    deps = tuple(kept) + tuple(deps)
    return pl.pallas_call(
        functools.partial(attend_kernel, slots, tile_q, len(deps)),
        grid=(count,),
        out_shape=(jax.ShapeDtypeStruct((rows, width), BF), jax.ShapeDtypeStruct((rows, width), BF)),
        in_specs=[of(rows, 0), of(keys, 1), of(keys, 2), fixed(rows), fixed(keys)]
        + [pl.BlockSpec(memory_space=pl.ANY)] * len(deps),
        out_specs=(out, out),
        input_output_aliases={5 + i: i for i in range(len(kept))},
        scratch_shapes=[pltpu.VMEM((2, keys, LANES), BF), pltpu.VMEM((2, keys, LANES), BF)],
        compiler_params=pltpu.CompilerParams(vmem_limit_bytes=56 * MIB),
        cost_estimate=pl.CostEstimate(
            flops=16 * rows * keys * count * LANES,
            bytes_accessed=2 * (3 * rows + 2 * keys) * count * LANES,
            transcendentals=2 * rows * keys * count,
        ),
    )(qkv, qkv, qkv, aug_q, aug_k, *deps)


def attend_back_kernel(
    slots, tile_k, scale, n_deps,
    q_ref, k_ref, v_ref, o_ref, do_ref, l_ref, ak_ref, *rest,
):
    (
        dqkv_ref, sum_ref,
        qx_ref, qz_ref, dx_ref, dz_ref, kx_ref, vx_ref, kt_ref, acc_ref,
    ) = rest[n_deps:]
    lane = lax.broadcasted_iota(jnp.int32, (1, LANES), 1)
    col = lane % HDIM
    sides = (lane < HDIM, lane >= HDIM)
    rows, keys = q_ref.shape[0], k_ref.shape[0]
    tokens = rows - slots
    grad = do_ref[...].astype(F32)
    prod = grad * o_ref[...].astype(F32)
    zero = jnp.zeros_like(grad)
    for h, sel in enumerate(sides):
        delta = jnp.sum(jnp.where(sel, prod, 0.0), axis=1, keepdims=True)
        qx_ref[h] = pick(sel, q_ref[...], l_ref[...])
        qz_ref[h] = pick(sel, q_ref[...], zero)
        dx_ref[h] = jnp.where(sel, grad, in_columns(col, -delta, zero)).astype(BF)
        dz_ref[h] = jnp.where(sel, grad, 0.0).astype(BF)
        kx_ref[h] = pick(sel, k_ref[...], ak_ref[...])
        vx_ref[h] = pick(sel, v_ref[...], ak_ref[...])
        kt_ref[h] = jnp.where(sel, k_ref[...].astype(F32), 0.0).T.astype(BF)

    def work(q_at, q_n, k_at, k_n, kt_at):
        dq = None
        dk = jnp.zeros((k_n, LANES), F32)
        dv = jnp.zeros((k_n, LANES), F32)
        for h in range(2):
            at, of = pl.ds(k_at, k_n), pl.ds(q_at, q_n)
            p = jnp.exp(nt(kx_ref[h, at, :], qx_ref[h, of, :]))
            dp = nt(vx_ref[h, at, :], dx_ref[h, of, :])
            ds = (p * dp).astype(BF)
            dv += nn(p.astype(BF), dz_ref[h, of, :])
            dk += nn(ds, qz_ref[h, of, :])
            part = nn(kt_ref[h, :, pl.ds(kt_at, k_n)], ds)
            dq = part if dq is None else dq + part
        return dq, dk, dv

    def keep(at, n, dk, dv):
        dqkv_ref[pl.ds(at, n), pl.ds(LANES, LANES)] = dk.astype(BF)
        dqkv_ref[pl.ds(at, n), pl.ds(2 * LANES, LANES)] = dv.astype(BF)

    dq, dk, dv = work(0, slots, 0, slots, 0)
    dq = dq.T * scale
    dqkv_ref[pl.ds(0, slots), pl.ds(0, LANES)] = dq.astype(BF)
    keep(0, slots, dk, dv)
    acc_ref[...] = jnp.zeros_like(acc_ref)
    sum_v = jnp.sum(dv, axis=0, keepdims=True)
    sum_q = jnp.sum(dq, axis=0, keepdims=True)
    for i in range((keys - slots) // tile_k):
        at = slots + i * tile_k
        dq, dk, dv = work(slots, tokens, at, tile_k, at)
        acc_ref[...] += dq
        keep(at, tile_k, dk, dv)
        sum_v += jnp.sum(dv, axis=0, keepdims=True)
    dq = acc_ref[...].T * scale
    dqkv_ref[pl.ds(slots, tokens), pl.ds(0, LANES)] = dq.astype(BF)
    dqkv_ref[pl.ds(rows, keys - rows), pl.ds(0, LANES)] = jnp.zeros((keys - rows, LANES), BF)
    sum_q += jnp.sum(dq, axis=0, keepdims=True)
    sum_ref[pl.ds(0, 1), :] = sum_q
    sum_ref[pl.ds(1, 1), :] = sum_v
    sum_ref[pl.ds(2, 6), :] = jnp.zeros((6, LANES), F32)


def attend_back(qkv, o, do, logs, aug_k, slots, tile_k, scale, first, count, kept, deps=()):
    rows, width = o.shape
    keys = qkv.shape[0]
    of = lambda n, m: pl.BlockSpec((n, LANES), lambda j: (0, 3 * (first + j) + m))
    col = lambda n: pl.BlockSpec((n, LANES), lambda j: (0, first + j))
    fixed = lambda n: pl.BlockSpec((n, LANES), lambda j: (0, 0))
    wide = lambda n: pltpu.VMEM((2, n, LANES), BF)
    deps = tuple(kept) + tuple(deps)
    return pl.pallas_call(
        functools.partial(attend_back_kernel, slots, tile_k, scale, len(deps)),
        grid=(count,),
        out_shape=(
            jax.ShapeDtypeStruct((keys, 3 * width), BF),
            jax.ShapeDtypeStruct((8, width), F32),
        ),
        in_specs=[of(rows, 0), of(keys, 1), of(keys, 2), col(rows), col(rows), col(rows), fixed(keys)]
        + [pl.BlockSpec(memory_space=pl.ANY)] * len(deps),
        out_specs=(pl.BlockSpec((keys, 3 * LANES), lambda j: (0, first + j)), col(8)),
        input_output_aliases={7 + i: i for i in range(len(kept))},
        scratch_shapes=[
            wide(rows), wide(rows), wide(rows), wide(rows), wide(keys), wide(keys),
            pltpu.VMEM((2, LANES, keys), BF),
            pltpu.VMEM((LANES, rows - slots), F32),
        ],
        compiler_params=pltpu.CompilerParams(vmem_limit_bytes=56 * MIB),
        cost_estimate=pl.CostEstimate(
            flops=40 * rows * keys * count * LANES,
            bytes_accessed=2 * (6 * rows + 4 * keys) * count * LANES,
            transcendentals=2 * rows * keys * count,
        ),
    )(qkv, qkv, qkv, o, do, logs, aug_k, *deps)


def nothing(*refs):
    return None


def tie(x, *deps):
    anywhere = pl.BlockSpec(memory_space=pl.ANY)
    return pl.pallas_call(
        nothing,
        out_shape=jax.ShapeDtypeStruct(x.shape, x.dtype),
        in_specs=[anywhere] * (1 + len(deps)),
        out_specs=anywhere,
        input_output_aliases={0: 0},
        cost_estimate=pl.CostEstimate(flops=0, bytes_accessed=0, transcendentals=0),
    )(x, *deps)


def assemble_kernel(n_in, n_deps, n_out, copies, *refs):
    ins, outs, sem = refs[:n_in], refs[n_in + n_deps : n_in + n_deps + n_out], refs[-1]
    started = []
    for i, (source, at, target, to) in enumerate(copies):
        src = ins[source].at[at] if at else ins[source]
        dst = outs[target].at[to] if to else outs[target]
        started.append(pltpu.make_async_copy(src, dst, sem.at[i]))
    for c in started:
        c.start()
    for c in started:
        c.wait()


def assemble(arrays, shapes, copies, deps=()):
    anywhere = pl.BlockSpec(memory_space=pl.ANY)
    vmem = pl.BlockSpec(memory_space=pltpu.VMEM)
    size = sum(math.prod(s) for s in shapes)
    return pl.pallas_call(
        functools.partial(assemble_kernel, len(arrays), len(deps), len(shapes), copies),
        out_shape=tuple(jax.ShapeDtypeStruct(s, arrays[0].dtype) for s in shapes),
        in_specs=[anywhere] * (len(arrays) + len(deps)),
        out_specs=tuple(vmem for _ in shapes),
        scratch_shapes=[pltpu.SemaphoreType.DMA((len(copies),))],
        compiler_params=pltpu.CompilerParams(vmem_limit_bytes=56 * MIB),
        cost_estimate=pl.CostEstimate(flops=0, bytes_accessed=4 * size, transcendentals=0),
    )(*arrays, *deps)


def sums_kernel(n_in, n_deps, n_out, pieces, *refs):
    ins, outs = refs[:n_in], refs[n_in + n_deps : n_in + n_deps + n_out]
    for target, to, terms in pieces:
        total = ins[terms[0][0]][terms[0][1]].astype(F32)
        for source, at in terms[1:]:
            total = total + ins[source][at].astype(F32)
        outs[target][to] = total.astype(outs[target].dtype)


def sums(arrays, outs, pieces, deps=()):
    anywhere = pl.BlockSpec(memory_space=pl.ANY)
    vmem = pl.BlockSpec(memory_space=pltpu.VMEM)
    size = sum(a.size for a in arrays)
    return pl.pallas_call(
        functools.partial(sums_kernel, len(arrays), len(deps), len(outs), pieces),
        out_shape=tuple(jax.ShapeDtypeStruct(s, dt) for s, dt in outs),
        in_specs=[vmem] * len(arrays) + [anywhere] * len(deps),
        out_specs=tuple(vmem for _ in outs),
        compiler_params=pltpu.CompilerParams(vmem_limit_bytes=56 * MIB),
        cost_estimate=pl.CostEstimate(flops=size, bytes_accessed=4 * size, transcendentals=0),
    )(*arrays, *deps)


def chunk_of(m):
    return m if m <= 704 else m // 2


def mm_in_kernel(chunk, epilogue, start, finish, n_extra, n_deps, a_ref, h_ref, r_ref, *rest):
    extra, outs = rest[:n_extra], rest[n_extra + n_deps :]
    k = h_ref.shape[0]

    def step(i, carry):
        rows = pl.ds(pl.multiple_of(i * chunk, 16), chunk)
        acc = nn(a_ref[rows, pl.ds(0, k)], h_ref[...]) + nn(a_ref[rows, pl.ds(k, k)], r_ref[...])
        return epilogue(acc, rows, extra, outs, carry)

    last = lax.fori_loop(0, a_ref.shape[0] // chunk, step, start(h_ref.shape[1]))
    finish(last, outs)


def nought(tn):
    return 0


def leave(carry, outs):
    return None


def mm_in(a, h, r, col, width, tn, epilogue, extra, outs, start=nought, finish=leave, deps=()):
    m, k = a.shape[0], h.shape[0] // 2
    tiles = width // tn
    weight = pl.BlockSpec((k, tn), lambda t, j: (t, col // tn + j))
    wide = lambda n: pl.BlockSpec((n, tn), lambda t, j: (0, t * tiles + j))
    return pl.pallas_call(
        functools.partial(mm_in_kernel, chunk_of(m), epilogue, start, finish, len(extra), len(deps)),
        grid=(2, tiles),
        out_shape=tuple(jax.ShapeDtypeStruct((n, 2 * width), dt) for n, dt in outs),
        in_specs=[pl.BlockSpec((m, 2 * k), lambda t, j: (0, 0)), weight, weight]
        + [wide(e.shape[0]) for e in extra]
        + [pl.BlockSpec(memory_space=pl.ANY)] * len(deps),
        out_specs=tuple(wide(n) for n, _ in outs),
        compiler_params=pltpu.CompilerParams(vmem_limit_bytes=56 * MIB),
        cost_estimate=pl.CostEstimate(
            flops=8 * m * k * width,
            bytes_accessed=4 * m * k + 8 * k * width + sum(2 * width * n * 2 for n, _ in outs),
            transcendentals=0,
        ),
    )(a, h, r, *extra, *deps)


def mm_out_kernel(chunk, half_tiles, n_extra, epilogue, a0_ref, a1_ref, h0_ref, h1_ref, r0_ref, r1_ref, *rest):
    extra, o_ref = rest[:n_extra], rest[-1]

    def run(w0_ref, w1_ref):
        def step(i, carry):
            rows = pl.ds(pl.multiple_of(i * chunk, 16), chunk)
            acc = nt(a0_ref[rows, :], w0_ref[...]) + nt(a1_ref[rows, :], w1_ref[...])
            more = [e[rows, :] if e.shape[0] > 8 else e[pl.ds(0, 1), :] for e in extra]
            o_ref[rows, :] = epilogue(acc, *more).astype(o_ref.dtype)
            return carry

        lax.fori_loop(0, a0_ref.shape[0] // chunk, step, 0)

    i = pl.program_id(0)

    @pl.when(i < half_tiles)
    def _():
        run(h0_ref, h1_ref)

    @pl.when(i >= half_tiles)
    def _():
        run(r0_ref, r1_ref)


def mm_out(a, m, h, r, col, width, td, epilogue, extra, dtype, deps=(), row=0):
    k = h.shape[0] // 2
    half = k // td
    at = col // width
    lhs = lambda t: pl.BlockSpec((m, width), lambda i: (0, t))
    if row:
        lhs = lambda t: pl.BlockSpec((pl.Element(m), pl.Element(width)), lambda i: (row, t * width))
    own = lambda t: pl.BlockSpec((td, width), lambda i: (t * half + jnp.minimum(i, half - 1), at))
    oth = lambda t: pl.BlockSpec((td, width), lambda i: (t * half + jnp.maximum(i - half, 0), at))
    wide = lambda n: pl.BlockSpec((min(n, m), td), lambda i: (0, i))
    return pl.pallas_call(
        functools.partial(mm_out_kernel, chunk_of(m), half, len(extra), epilogue),
        grid=(2 * half,),
        out_shape=jax.ShapeDtypeStruct((m, 2 * k), dtype),
        in_specs=[lhs(0), lhs(1), own(0), own(1), oth(0), oth(1)]
        + [wide(e.shape[0]) for e in extra]
        + [pl.BlockSpec(memory_space=pl.ANY)] * len(deps),
        out_specs=wide(m),
        compiler_params=pltpu.CompilerParams(vmem_limit_bytes=56 * MIB),
        cost_estimate=pl.CostEstimate(
            flops=8 * m * k * width,
            bytes_accessed=4 * m * width + 8 * k * width + 8 * m * k,
            transcendentals=0,
        ),
    )(a, a, h, h, r, r, *extra, *deps)


def put_plain(acc, rows, extra, outs, carry):
    outs[0][rows, :] = acc.astype(outs[0].dtype)
    return carry


def put_biased(acc, rows, extra, outs, carry):
    outs[0][rows, :] = (acc + extra[0][pl.ds(0, 1), :]).astype(outs[0].dtype)
    return carry


def put_scaled(acc, rows, extra, outs, carry):
    low = (acc + extra[0][pl.ds(0, 1), :]).astype(BF).astype(F32)
    outs[0][rows, :] = (low * extra[0][pl.ds(1, 1), :]).astype(BF)
    return carry


def put_gelu(acc, rows, extra, outs, carry):
    inner = acc + extra[0][pl.ds(0, 1), :]
    out, slope = gelu_parts(inner)
    outs[0][rows, :] = out.astype(BF)
    outs[1][rows, :] = slope.astype(BF)
    return carry


def put_sloped(acc, rows, extra, outs, carry):
    grad = acc * extra[0][rows, :].astype(F32)
    outs[0][rows, :] = grad.astype(BF)
    return carry + jnp.sum(grad, axis=0, keepdims=True)


def row_of_zeros(tn):
    return jnp.zeros((1, tn), F32)


def put_sum(carry, outs):
    outs[1][...] = jnp.broadcast_to(carry, outs[1].shape)


def eight(*rows):
    return jnp.concatenate([jnp.stack(rows), jnp.zeros((8 - len(rows), rows[0].shape[0]), F32)])


def gelu_parts(v):
    size = jnp.abs(v)
    t = 1.0 / ((0.3275911 * math.sqrt(0.5)) * size + 1.0)
    bell = jnp.exp(-0.5 * (v * v))
    poly = (0.5 * 1.061405429) * t - 0.5 * 1.453152027
    poly = (poly * t + 0.5 * 1.421413741) * t - 0.5 * 0.284496736
    poly = (poly * t + 0.5 * 0.254829592) * t
    low = bell * (poly - size * (1.0 / math.sqrt(2.0 * math.pi)))
    return jnp.maximum(v, 0.0) - size * (poly * bell), jnp.where(v < 0.0, low, 1.0 - low)


def norm_parts(v):
    centered = v - jnp.mean(v, axis=-1, keepdims=True)
    rstd = lax.rsqrt(jnp.mean(centered * centered, axis=-1, keepdims=True) + LN_EPS)
    return centered * rstd, rstd


def norm_back(c, vhat, rstd, gain):
    gc = c * gain
    back = (
        gc
        - jnp.mean(gc, axis=-1, keepdims=True)
        - vhat * jnp.mean(gc * vhat, axis=-1, keepdims=True)
    ) * rstd
    return back, jnp.sum(c * vhat, axis=0), jnp.sum(c, axis=0)


def make(n_pb, n_pa, n_ta):
    cores = 2
    n_x = n_pb // cores
    blocks = n_pb * n_pa

    def px(v, k):
        return lax.ppermute(v, "pb", [(i, i ^ (cores * k)) for i in range(n_pb)])

    def pc(v):
        return lax.ppermute(v, "pb", [(i, i ^ 1) for i in range(n_pb)])

    def pz(v, k):
        return lax.ppermute(v, "pa", [(i, i ^ k) for i in range(n_pa)])

    def py(v):
        return lax.ppermute(v, "ta", [(i, i ^ 1) for i in range(n_ta)])

    x_bits = n_x.bit_length() - 1
    z_bits = n_pa.bit_length() - 1

    def after(v, *deps):
        return tie(v, *deps) if deps else v

    every = slice(None)

    def z_go(have, bit):
        return pz(have, 1 << bit)

    def z_end(have, other, deps=()):
        n, w, cols = have.shape
        (out,) = assemble(
            (have, other), ((n, 2, w, cols),), ((0, (), 0, (every, 0)), (1, (), 0, (every, 1))), deps
        )
        return out.reshape(2 * n, w, cols)

    def z_last(have, other, deps=()):
        n, w, cols = have.shape
        h = n // 2
        near, far = assemble(
            (have, other), ((h, 2, w, cols), (h, 2, w, cols)),
            tuple(
                (source, (pl.ds(s * h, h),), s, (every, source)) for s in range(2) for source in range(2)
            ),
            deps,
        )
        return near.reshape(n, w, cols), far.reshape(n, w, cols)

    def z_rest(have, other):
        have = z_end(have, other)
        for bit in reversed(range(1, z_bits - 1)):
            have = z_end(have, z_go(have, bit))
        return have, z_go(have, 0)

    def gather_z(shard):
        have = shard[None]
        for bit in reversed(range(z_bits)):
            have = z_end(have, z_go(have, bit))
        return have.reshape(-1, have.shape[-1])

    def joined(parts, deps=()):
        (out,) = assemble(
            tuple(parts), ((len(parts),) + parts[0].shape,),
            tuple((i, (), 0, (i,)) for i in range(len(parts))), deps,
        )
        return out

    def spread_x(a):
        have, arrays = [(0, None)], [a]
        for bit in range(x_bits):
            whole = arrays[0] if bit == 0 else joined([arrays[i] if p is None else arrays[i][p] for i, p in have])
            arrays.append(px(whole, 1 << bit))
            last = len(arrays) - 1
            have = have + ([(last, None)] if bit == 0 else [(last, p) for p in range(len(have))])
        return [arrays[i] if p is None else arrays[i][p] for i, p in have]

    def xy_go(near, far):
        return spread_x(near), [far, py(far)]

    def xy_one(going, deps=()):
        near_xs, far_ts = going
        return joined(near_xs, deps), joined(far_ts, deps)

    def xy_two_go(near_x, far_t):
        return near_x, py(near_x), spread_x(far_t)

    def xy_two(going, deps=()):
        near_x, near_oth, far_x = going
        _, h, w, cols = near_x.shape
        copies = []
        for x in range(n_x):
            for t in range(n_ta):
                copies.append((t, (x,), 0, (t, x, 0)))
                copies.append((n_ta + x, (t,), 0, (t, x, 1)))
        (out,) = assemble(
            (near_x, near_oth, *far_x), ((n_ta, n_x, 2, h, w, cols),), tuple(copies), deps
        )
        return out.reshape(-1, cols)

    def add(a, b):
        return (a.astype(F32) + b.astype(F32)).astype(a.dtype)

    def away_part(lhs, rhs):
        return pc(tn(lhs[:, lhs.shape[1] // 2 :], rhs).astype(BF))

    def core_part(lhs, rhs, away):
        return (tn(lhs[:, : lhs.shape[1] // 2], rhs) + away.astype(F32)).astype(BF)

    def p1_send(parts, deps=()):
        rows = parts[0].shape[0]
        size = rows // n_x
        half = size // 2
        widths = [r.shape[1] // n_ta for r in parts]
        cols = sum(widths)
        copies = []
        for i, n in enumerate(widths):
            at = sum(widths[:i])
            for t in range(n_ta):
                for x in range(n_x):
                    copies.append((
                        i, (pl.ds(x * size, half), pl.ds(t * n, n)), x, (every, pl.ds(t * cols + at, n)),
                    ))
                    copies.append((
                        i, (pl.ds(x * size + half, half), pl.ds(t * n, n)),
                        n_x + t, (pl.ds(x * half, half), pl.ds(at, n)),
                    ))
        shapes = ((half, n_ta * cols),) * n_x + ((n_x * half, cols),) * n_ta
        out = assemble(tuple(parts), shapes, tuple(copies), deps)
        return out[:n_x], out[n_x], out[n_x + 1]

    def p1_go(sent):
        near, far_own, far_oth = sent
        return [px(near[k], k) for k in range(1, n_x)], py(far_oth)

    def p1_end(sent, got, deps=()):
        near, far_own, _ = sent
        half, cols = near[0].shape[0], far_own.shape[1]
        n = len(got[0])
        pieces = []
        for t in range(n_ta):
            at = (every, pl.ds(t * cols, cols))
            pieces.append((t, (), [(i, at) for i in range(n + 1)]))
        for x in range(n_x):
            at = (pl.ds(x * half, half), every)
            pieces.append((n_ta + x, (), [(n + 1, at), (n + 2, at)]))
        pieces = [(o, to or (every, every), terms) for o, to, terms in pieces]
        out = sums(
            (near[0], *got[0], far_own, got[1]), (((half, cols), BF),) * (n_ta + n_x), pieces, deps
        )
        return out[0], out[1], out[2:]

    def p2_go(state):
        near_own, near_oth, far = state
        return py(near_oth), [px(far[k], k) for k in range(1, n_x)]

    def p2_end(state, got, w, deps=()):
        half, cols = state[0].shape
        h = half // w
        pieces = []
        for b in range(2 * h):
            at = (pl.ds((b % h) * w, w), every)
            terms = [(0, at), (1, at)] if b < h else [(i, at) for i in range(2, 3 + len(got[1]))]
            pieces.append((b % 2, (b // 2,), terms))
        return sums(
            (state[0], got[0], state[2][0], *got[1]), (((h, w, cols), BF),) * 2, pieces, deps
        )

    def z_next(keep, got, deps=()):
        n, w, cols = keep.shape
        pieces = [(b % 2, (b // 2,), [(0, (b,)), (1, (b,))]) for b in range(n)]
        return sums((keep, got), (((n // 2, w, cols), BF),) * 2, pieces, deps)

    def z_done(keep, got, deps=()):
        _, w, cols = keep.shape
        (out,) = sums((keep, got), (((1, w, cols), F32),), [(0, (0,), [(0, (0,)), (1, (0,))])], deps)
        return out[0]

    def z_split(cur):
        cur = cur.reshape((cur.shape[0] // 2, 2) + cur.shape[1:])
        return cur[:, 0], cur[:, 1]

    def reduce_z(cur):
        for bit in range(z_bits):
            keep, give = z_split(cur)
            got = pz(give, 1 << bit)
            cur = keep.astype(F32) + got.astype(F32) if bit == z_bits - 1 else add(keep, got)
        return cur[0]

    def reduce_z_from(keep, give, first):
        for bit in range(first, z_bits - 1):
            keep, give = z_next(keep, pz(give, 1 << bit))
        return z_done(keep, pz(give, 1 << (z_bits - 1)))

    def on_device(
        rows_in, w_qkv, b_qv, w_out, b_out, ln1_gain, ln1_bias, w_in, b_in, w_fin, b_fin,
        ln2_gain, ln2_bias, w_head, b_head, lengths, query_len, score_grad,
    ):
        t0 = lax.axis_index("ta")
        z0 = lax.axis_index("pa")
        p0 = lax.axis_index("pb")
        x0, c0 = p0 // cores, p0 % cores
        first_t = t0 == 0
        all_rows, width = rows_in.shape
        half_rows = all_rows // n_ta
        n_q, n_p = query_len.shape[1], lengths.shape[1]
        q_here = n_q // n_ta
        slots = q_here * QLEN
        toks = half_rows - slots
        block = width // blocks
        heads_half = w_qkv.shape[2]
        scale = 1.0 / math.sqrt(HDIM)

        per_tile = LANES // block
        z_tiles = n_pa // per_tile
        low_bits = per_tile.bit_length() - 1
        forward, backward = [], []
        for c in range(cores):
            for x in range(n_x):
                for z in range(z_tiles):
                    forward.append((((x ^ x0) * cores) + (c ^ c0)) * z_tiles + (z ^ (z0 // per_tile)))
        for x in range(n_x):
            for c in range(cores):
                for z in range(z_tiles):
                    backward.append((((c ^ c0) * n_x) + (x ^ x0)) * z_tiles + (z ^ (z0 // per_tile)))
        low = z0 % per_tile
        as_info = lambda v: jnp.stack([jnp.asarray(a, jnp.int32) for a in v])
        row_info = as_info(forward + [low, t0 * half_rows, (1 - t0) * half_rows + slots])
        vec_info = as_info(forward + [low, 0])
        back_info = as_info(backward + [low, 0])

        rows = permute(rows_in, row_info, (half_rows, toks), block, low_bits)
        vecs = jnp.stack(
            [b_out, ln1_gain, ln1_bias, b_fin, ln2_gain, ln2_bias, b_out, b_out]
        )
        vecs = permute(vecs, vec_info, (8,), block, low_bits)
        b_out_r, g1, be1, b_fin_r, g2, be2 = (vecs[i] for i in range(6))
        pairs = heads_half // LANES
        all_pairs = n_ta * pairs
        ff_half = w_in.shape[1]
        head_half = width // n_ta
        qkv_half = 3 * heads_half
        swapped = lambda v: jnp.concatenate([v[..., v.shape[-1] // 2 :], v[..., : v.shape[-1] // 2]], axis=-1)
        in_order = lambda v: jnp.where(first_t, v, swapped(v))

        row_id = jnp.arange(half_rows + toks, dtype=jnp.int32)
        is_slot = row_id < slots
        token = jnp.where(
            row_id < half_rows, t0 * toks + row_id - slots, (1 - t0) * toks + row_id - half_rows
        )
        ends = jnp.cumsum(lengths[0])
        pid = jnp.sum((token[:, None] >= ends[None, :]).astype(jnp.int32), axis=1)
        q_lens = lax.dynamic_index_in_dim(query_len, z0, 0, keepdims=False)
        q_lens = lax.dynamic_slice_in_dim(q_lens, t0 * q_here, q_here, 0)
        limit = jnp.sum(
            jnp.where(
                (row_id // QLEN)[:, None] == jnp.arange(q_here, dtype=jnp.int32)[None, :],
                q_lens[None, :], 0,
            ),
            axis=1,
        )
        dead = is_slot & (row_id % QLEN >= limit)
        seg = jnp.where(is_slot, n_p + row_id // QLEN, pid)
        lane_c = jnp.arange(LANES, dtype=jnp.int32)[None, :] % HDIM
        same = seg[:, None] == lane_c
        aug_k = jnp.where(
            lane_c < 6, same & ~dead[:, None], jnp.where(lane_c == 6, dead[:, None], (lane_c >= 7) & (lane_c < 10))
        )
        aug_k = aug_k.astype(BF)
        aug_q = jnp.where((lane_c < 7) & ~same[:half_rows], BIG, 0.0).astype(BF)

        packed = lambda v: v.reshape(v.shape[0], 3, pairs, LANES).transpose(0, 2, 1, 3)
        shard_q = packed(w_qkv.transpose(1, 0, 2).reshape(block, qkv_half)).reshape(block, -1)
        shard_m = jnp.concatenate([w_in, w_out.T], axis=1)
        head_mine = lax.dynamic_slice_in_dim(w_head, t0 * head_half, head_half, 1)
        shard_e = jnp.concatenate([w_fin.T, head_mine], axis=1)

        q_0 = shard_q[None]
        q_1 = z_go(q_0, z_bits - 1)
        m_0 = tie(shard_m[None], q_1)
        m_1 = z_go(m_0, z_bits - 1)
        q_2, q_3 = z_rest(q_0, q_1)
        near_q, far_q = z_last(q_2, q_3, (m_1,))
        e_0 = tie(shard_e[None], m_1)
        e_1 = z_go(e_0, z_bits - 1)
        near_q, far_q = xy_one(xy_go(near_q, far_q), (rows, aug_q, aug_k))
        near_m, far_m = z_last(*z_rest(m_0, m_1))
        h_q = xy_two(xy_two_go(near_q, far_q), (near_m, e_1))
        r_q = pc(h_q)
        bias_of = lambda b: packed(jnp.concatenate([b[0], jnp.zeros_like(b[0]), b[1]])[None]).reshape(-1)
        qkv_bias = jnp.concatenate([bias_of(b_qv), bias_of(py(b_qv))])
        b_in_r = jnp.concatenate([b_in, py(b_in)])

        col_scale = jnp.tile(jnp.repeat(jnp.array([scale, 1.0, 1.0], F32), LANES), all_pairs)
        (qkv,) = mm_in(
            rows, h_q, r_q, 0, qkv_half, qkv_half // 3, put_scaled, (eight(qkv_bias, col_scale),),
            ((half_rows + toks, BF),), deps=(near_m,),
        )
        near_m, far_m = xy_one(xy_go(near_m, far_m), (qkv,))
        n_call = all_pairs // 4
        part = lambda i, kept, deps: attend(
            qkv, half_rows, aug_q, aug_k, slots, toks, i * n_call, n_call, kept, deps
        )
        e_2, e_3 = z_rest(e_0, e_1)
        going = xy_two_go(near_m, far_m)
        kept = part(0, (), (near_m, far_m, e_2))
        near_e, far_e = z_last(e_2, e_3, (kept[0],))
        kept = part(1, kept, (near_e,))
        kept = part(2, kept, ())
        h_m = xy_two(going, (kept[0],))
        r_m = pc(h_m)
        kept = part(3, kept, (h_m,))
        r_m = tie(r_m, kept[0])
        near_e, far_e = xy_one(xy_go(near_e, far_e), (kept[0],))
        ctx, logs = kept
        h_one = mm_out(
            ctx, half_rows, h_m, r_m, ff_half, heads_half, heads_half // 2,
            lambda acc, res, b: acc + res.astype(F32) + b, (rows, eight(b_out_r)), F32,
            (near_e, far_e),
        )
        v1, r1 = norm_parts(h_one)
        normed = v1 * g1 + be1
        normed_low = normed.astype(BF)
        active, slope = mm_in(
            normed_low, h_m, r_m, 0, ff_half, ff_half // 4, put_gelu, (eight(b_in_r),),
            ((half_rows, BF), (half_rows, BF)),
        )
        h_e = xy_two(xy_two_go(near_e, far_e), (active,))
        r_e = pc(h_e)
        h_two = mm_out(
            active, half_rows, h_e, r_e, 0, ff_half, heads_half // 2,
            lambda acc, res, b: acc + res + b, (normed, eight(b_fin_r)), F32,
        )
        v2, r2 = norm_parts(h_two)
        output_low = (v2 * g2 + be2).astype(BF)
        (raw,) = mm_in(
            output_low, h_e, r_e, ff_half, head_half, head_half, put_biased,
            (eight(in_order(b_head)),), ((half_rows, F32),),
        )
        inv = lax.rsqrt(jnp.sum(raw * raw, axis=-1, keepdims=True) + UNIT_EPS)
        unit = raw * inv
        unit_low = unit.astype(BF)

        passages = unit_low[slots:]
        mine = gather_z(unit_low[:slots])
        asked = jnp.concatenate([mine, swapped(py(mine))], axis=0)
        n_asked = asked.shape[0]
        z_rel = jnp.arange(n_pa, dtype=jnp.int32) ^ z0
        swap_t = lambda a: jnp.where(first_t, a, a[::-1])
        lens = swap_t(
            jnp.take(query_len, z_rel, axis=0).reshape(n_pa, n_ta, q_here).transpose(1, 0, 2)
        )
        valid = (
            jnp.arange(QLEN, dtype=jnp.int32)[None, None, None, :] < lens[..., None]
        ).astype(F32)
        up = swap_t(
            jnp.take(score_grad[0], z_rel, axis=0).reshape(n_pa, n_ta, q_here, n_p).transpose(1, 0, 2, 3)
        )
        token_grad = (up[:, :, :, None, :] * valid[..., None]).reshape(n_asked, n_p)
        member = (
            pid[slots:half_rows, None] == jnp.arange(n_p, dtype=jnp.int32)[None, :]
        ).astype(F32)
        powers = jnp.exp(nt(asked, passages) * (1.0 / SHARP))
        sums = jnp.dot(powers, member, precision=lax.Precision.HIGHEST)
        theirs = py(sums.reshape(n_ta, n_asked // n_ta, n_p)[::-1])
        sums = sums + theirs.reshape(n_asked, n_p)
        soft = (SHARP * jnp.log(sums)).reshape(n_ta, n_pa, q_here, QLEN, n_p)
        scores = jnp.sum(soft[0] * valid[0][..., None], axis=2)
        scores = jnp.take(scores, z_rel, axis=0)[None]
        coef = token_grad / sums
        coef_j = sum(coef[:, i : i + 1] * member[:, i][None, :] for i in range(n_p))
        sim_grad = (powers * coef_j).astype(BF)
        ask_grad = nn(sim_grad, passages).astype(BF).reshape(n_ta, n_pa * slots, width)
        ask_sum = add(ask_grad[0], py(swapped(ask_grad[1])))
        passage_grad = tn(sim_grad, asked)
        unit_grad = jnp.concatenate(
            [reduce_z(ask_sum.reshape(n_pa, slots, width)), passage_grad], axis=0
        )

        raw_grad = inv * (unit_grad - unit * jnp.sum(unit * unit_grad, axis=-1, keepdims=True))
        g_b_head = in_order(jnp.sum(raw_grad, axis=0))
        raw_low = raw_grad.astype(BF)
        output_grad = mm_out(
            raw_low, half_rows, h_e, r_e, ff_half, head_half, heads_half // 2, lambda acc: acc, (), F32
        )
        h_two_grad, g_g2, g_be2 = norm_back(output_grad, v2, r2, g2)
        g_b_fin = jnp.sum(h_two_grad, axis=0)
        branch_low = h_two_grad.astype(BF)
        away_fin = away_part(branch_low, active)
        away_head = away_part(output_low, raw_low)
        inner_low, sums_in = mm_in(
            branch_low, h_e, r_e, 0, ff_half, ff_half // 4, put_sloped, (slope,),
            ((half_rows, BF), (8, F32)), row_of_zeros, put_sum,
        )
        part_fin = core_part(branch_low, active, tie(away_fin, inner_low))
        part_head = core_part(output_low, raw_low, tie(away_head, inner_low))
        sent_f = p1_send([part_fin, part_head])
        got_f = p1_go(sent_f)
        away_in = away_part(normed_low, inner_low)
        normed_grad = mm_out(
            inner_low, half_rows, h_m, r_m, 0, ff_half, heads_half // 2,
            lambda acc, res: acc + res, (h_two_grad,), F32, (sent_f[0][-1], sent_f[2]),
        )
        h_one_grad, g_g1, g_be1 = norm_back(normed_grad, v1, r1, g1)
        g_b_out = jnp.sum(h_one_grad, axis=0)
        attended_low = h_one_grad.astype(BF)
        away_out = away_part(attended_low, ctx)
        (d_ctx,) = mm_in(
            attended_low, h_m, r_m, ff_half, heads_half, heads_half, put_plain, (), ((half_rows, BF),)
        )
        part_in = core_part(normed_low, inner_low, tie(away_in, d_ctx))
        part_out = core_part(attended_low, ctx, tie(away_out, d_ctx))
        sent_m = p1_send([part_in, part_out])
        got_m = p1_go(sent_m)
        state_f = p1_end(sent_f, got_f, (sent_m[2],))
        got_f = p2_go(state_f)

        back = lambda i, kept, deps: attend_back(
            qkv, ctx, d_ctx, logs, aug_k, slots, 2 * toks // 5, scale,
            ((i + 2) % 4) * n_call, n_call, kept, deps,
        )
        quarter = qkv_half // 2
        columns = lambda a, i: a[:, i * quarter : (i + 1) * quarter]
        rows_x = width // (cores * n_x)
        x_blocks = lambda part: [part[k * rows_x : (k + 1) * rows_x] for k in range(n_x)]
        x_go = lambda blocks_of: [px(blocks_of[k], k) for k in range(1, n_x)]

        def x_end(blocks_of, got):
            total = blocks_of[0]
            for g in got:
                total = add(total, g)
            return total

        kept = back(0, (), (sent_m[0][-1], sent_m[2], state_f[1], state_f[2][-1]))
        keep_f, give_f = p2_end(state_f, got_f, block, (kept[1],))
        z_f = pz(give_f, 1)
        kept = back(1, kept, (give_f,))
        away_1 = away_part(rows, kept[0][:, qkv_half:])
        keep_f, give_f = z_next(keep_f, z_f, (kept[1],))
        z_f = pz(give_f, 2)
        part_1 = core_part(rows, kept[0][:, qkv_half:], tie(away_1, give_f))
        sent_1 = x_blocks(part_1)
        got_1 = x_go(sent_1)
        kept = back(2, kept, (give_f, sent_1[1]))
        state_m = p1_end(sent_m, got_m, (kept[1],))
        away_2 = away_part(rows, columns(kept[0], 0))
        got_m = p2_go(state_m)
        y_1 = x_end(sent_1, [tie(g, kept[1]) for g in got_1])
        part_2 = core_part(rows, columns(kept[0], 0), tie(away_2, y_1))
        sent_2 = x_blocks(part_2)
        got_2 = x_go(sent_2)
        if z_bits == 2:
            out_f = z_done(keep_f, z_f, (kept[1],))
        else:
            out_f = reduce_z_from(*z_next(keep_f, z_f), 2)
        kept = back(3, kept, (y_1, sent_2[1], state_m[1], state_m[2][-1]))
        d_qkv, sums_qv = kept
        y_1 = py(y_1)
        away_3 = away_part(rows, columns(d_qkv, 1))
        to_other = mm_out(
            d_qkv, toks, h_q, r_q, 0, qkv_half, heads_half // 2, lambda acc: acc, (), BF,
            (away_3,), row=half_rows,
        )
        d_qkv = tie(d_qkv, to_other)
        sums_qv = tie(sums_qv, to_other)
        part_3 = core_part(rows, columns(d_qkv, 1), away_3)
        sent_3 = x_blocks(part_3)
        got_3 = x_go(sent_3)
        to_other = py(to_other)
        keep_m, give_m = p2_end(state_m, got_m, block, (sums_qv,))
        out_m = reduce_z_from(keep_m, give_m, 0)
        y_1 = tie(y_1, sums_qv)
        got_2 = [tie(g, sums_qv) for g in got_2]
        grad_rows = mm_out(
            d_qkv, half_rows, h_q, r_q, 0, qkv_half, heads_half // 2,
            lambda acc, res: acc + res, (h_one_grad,), F32, (sent_3[1],),
        )
        as_z = lambda a: a.reshape(n_pa, block, -1)
        out_2 = reduce_z(as_z(add(x_end(sent_2, got_2), y_1[:, :quarter])))
        out_3 = reduce_z(as_z(add(x_end(sent_3, got_3), y_1[:, quarter:])))
        out_q = jnp.concatenate([out_2, out_3], axis=1)
        g_w_qkv = out_q.reshape(block, pairs, 3, LANES).transpose(2, 0, 1, 3).reshape(3, block, heads_half)
        g_w_fin, g_head = out_f[:, :ff_half], out_f[:, ff_half:]
        g_w_in, g_w_out = out_m[:, :ff_half], out_m[:, ff_half:]
        n_h = block // n_ta
        head_keep = jnp.where(first_t, g_head[:n_h], g_head[n_h:])
        head_got = py(jnp.where(first_t, g_head[n_h:], g_head[:n_h]))
        g_w_head = in_order(jnp.concatenate([head_keep, head_got], axis=1))
        grad_rows = permute(
            grad_rows, back_info, (half_rows,), block, low_bits, slots, (to_other,)
        )

        d_vecs = permute(
            eight(g_b_out, g_g1, g_be1, g_b_fin, g_g2, g_be2), back_info, (8,), block, low_bits
        )
        vec = jnp.concatenate(
            [d_vecs, in_order(sums_in[0]).reshape(-1, width), g_b_head[None], in_order(sums_qv[:2])]
        )
        vec = vec + pc(vec)
        for bit in range(x_bits):
            vec = vec + px(vec, 1 << bit)
        vec = vec + py(vec)
        for bit in range(z_bits):
            vec = vec + pz(vec, 1 << bit)
        place = (p0 * n_pa + z0) * n_ta + t0
        w32 = width // (blocks * n_ta)
        ff_rows = n_ta * ff_half // width
        mine = lax.dynamic_slice_in_dim(vec, place * w32, w32, 1)
        o_b_out, o_g1, o_be1, o_b_fin, o_g2, o_be2 = (mine[i] for i in range(6))
        o_b_head, o_bqv = mine[8 + ff_rows], mine[9 + ff_rows : 11 + ff_rows]
        o_b_in = lax.dynamic_slice_in_dim(
            vec[8 : 8 + ff_rows].reshape(-1), place * (ff_rows * w32), ff_rows * w32, 0
        )
        return (
            scores, grad_rows, g_w_qkv, o_bqv, g_w_out.T, o_b_out, o_g1, o_be1,
            g_w_in, o_b_in, g_w_fin.T, o_b_fin, o_g2, o_be2, g_w_head, o_b_head,
        )

    return on_device


def solution(mesh):
    both = ("pb", "pa")
    every = ("pb", "pa", "ta")
    in_specs = (
        P(both, None), P(None, both, "ta"), P(None, "ta"), P("ta", both), P(), P(), P(),
        P(both, "ta"), P("ta"), P("ta", both), P(), P(), P(), P(both, None), P(),
        P(both, None), P("pb", None), P("pb", None, None, "pa"),
    )
    out_specs = (
        P("pb", None, "ta", "pa"), P(every, None), P(None, both, "ta"), P(None, every),
        P("ta", both), P(every), P(every), P(every), P(both, "ta"), P(every), P("ta", both),
        P(every), P(every), P(every), P(every, None), P(every),
    )
    step = make(mesh.shape["pb"], mesh.shape["pa"], mesh.shape["ta"])
    return jax.shard_map(step, mesh=mesh, in_specs=in_specs, out_specs=out_specs, check_vma=False)
```

```python
import functools
import math

import jax
import jax.numpy as jnp
from jax import lax
from jax.experimental import pallas as pl
from jax.experimental.pallas import tpu as pltpu
from jax.sharding import PartitionSpec as P

HDIM = 64
QLEN = 32
LANES = 128
SHARP = 0.02
LN_EPS = 1e-05
UNIT_EPS = 1e-06
BIG = -1e30
BF = jnp.bfloat16
F32 = jnp.float32
MIB = 1024 * 1024


def nn(a, b):
    return lax.dot_general(a, b, (((1,), (0,)), ((), ())), preferred_element_type=F32)


def nt(a, b):
    return lax.dot_general(a, b, (((1,), (1,)), ((), ())), preferred_element_type=F32)


def tn(a, b):
    return lax.dot_general(a, b, (((0,), (0,)), ((), ())), preferred_element_type=F32)


def permute_kernel(segments, block, low_bits, skip, info, x_ref, *rest):
    o_ref = rest[-1]
    tiles = x_ref.shape[1] // LANES
    lane = lax.broadcasted_iota(jnp.int32, (1, LANES), 1)
    low = info[tiles]
    for j in range(tiles):
        source = pl.multiple_of(info[j] * LANES, LANES)
        row = 0
        for i, length in enumerate(segments):
            start = pl.multiple_of(info[tiles + 1 + i], 16)
            part = x_ref[pl.ds(start, length), pl.ds(source, LANES)]
            if skip is not None:
                more = rest[0][:, pl.ds(source, LANES)].astype(F32)
                part = jnp.concatenate([part[:skip], part[skip:] + more], axis=0)
            if low_bits:
                part = part.astype(F32)
                for bit in range(low_bits):
                    step = block << bit
                    up = pltpu.roll(part, step, 1)
                    down = pltpu.roll(part, LANES - step, 1)
                    swapped = jnp.where((lane & step) != 0, up, down)
                    part = jnp.where((low & (1 << bit)) != 0, swapped, part)
                part = part.astype(o_ref.dtype)
            o_ref[pl.ds(row, length), pl.ds(j * LANES, LANES)] = part
            row += length


def permute(x, info, segments, block, low_bits, skip=None, more=()):
    rows = sum(segments)
    return pl.pallas_call(
        functools.partial(permute_kernel, segments, block, low_bits, skip),
        out_shape=jax.ShapeDtypeStruct((rows, x.shape[1]), x.dtype),
        in_specs=[
            pl.BlockSpec(memory_space=pltpu.SMEM),
            pl.BlockSpec(memory_space=pltpu.VMEM),
        ]
        + [pl.BlockSpec(memory_space=pltpu.VMEM)] * len(more),
        out_specs=pl.BlockSpec(memory_space=pltpu.VMEM),
        compiler_params=pltpu.CompilerParams(vmem_limit_bytes=56 * MIB),
        cost_estimate=pl.CostEstimate(
            flops=rows * x.shape[1], bytes_accessed=4 * rows * x.shape[1], transcendentals=0
        ),
    )(info, x, *more)


def pick(sel, a, b):
    return jnp.where(sel, a.astype(F32), b.astype(F32)).astype(BF)


def split3(v):
    hi = v.astype(BF).astype(F32)
    mid = (v - hi).astype(BF).astype(F32)
    return hi, mid, v - hi - mid


def in_columns(col, v, base):
    hi, mid, lo = split3(v)
    return jnp.where(col == 7, hi, jnp.where(col == 8, mid, jnp.where(col == 9, lo, base)))


def attend_kernel(slots, tile_q, n_deps, q_ref, k_ref, v_ref, aq_ref, ak_ref, *rest):
    o_ref, l_ref, kx_ref, vx_ref = rest[n_deps:]
    lane = lax.broadcasted_iota(jnp.int32, (1, LANES), 1)
    col = lane % HDIM
    sides = (lane < HDIM, lane >= HDIM)
    for h, sel in enumerate(sides):
        kx_ref[h] = pick(sel, k_ref[...], ak_ref[...])
        vx_ref[h] = pick(sel, v_ref[...], jnp.ones_like(v_ref[...]))
    keys = k_ref.shape[0]

    def work(q_at, q_n, k_at, k_n):
        rows = pl.ds(q_at, q_n)
        q, aug = q_ref[rows, :], aq_ref[rows, :]
        outs, logs = [], []
        for h, sel in enumerate(sides):
            s = nt(pick(sel, q, aug), kx_ref[h, pl.ds(k_at, k_n), :])
            top = jnp.max(s, axis=1, keepdims=True)
            p = jnp.exp(s - top).astype(BF)
            o = nn(p, vx_ref[h, pl.ds(k_at, k_n), :])
            outs.append(o / pltpu.roll(o, HDIM, 1))
            logs.append(in_columns(col, -(top + jnp.log(o)), aug.astype(F32)))
        o_ref[rows, :] = jnp.where(sides[0], outs[0], outs[1]).astype(BF)
        l_ref[rows, :] = jnp.where(sides[0], logs[1], logs[0]).astype(BF)

    work(0, slots, 0, slots)
    tokens = q_ref.shape[0] - slots

    def step(i, carry):
        work(pl.multiple_of(slots + i * tile_q, 16), tile_q, slots, keys - slots)
        return carry

    lax.fori_loop(0, tokens // tile_q, step, 0)


def attend(qkv, rows, aug_q, aug_k, slots, tile_q, first, count, kept, deps=()):
    keys, width = qkv.shape[0], qkv.shape[1] // 3
    of = lambda n, m: pl.BlockSpec((n, LANES), lambda j: (0, 3 * (first + j) + m))
    out = pl.BlockSpec((rows, LANES), lambda j: (0, first + j))
    fixed = lambda n: pl.BlockSpec((n, LANES), lambda j: (0, 0))
    deps = tuple(kept) + tuple(deps)
    return pl.pallas_call(
        functools.partial(attend_kernel, slots, tile_q, len(deps)),
        grid=(count,),
        out_shape=(jax.ShapeDtypeStruct((rows, width), BF), jax.ShapeDtypeStruct((rows, width), BF)),
        in_specs=[of(rows, 0), of(keys, 1), of(keys, 2), fixed(rows), fixed(keys)]
        + [pl.BlockSpec(memory_space=pl.ANY)] * len(deps),
        out_specs=(out, out),
        input_output_aliases={5 + i: i for i in range(len(kept))},
        scratch_shapes=[pltpu.VMEM((2, keys, LANES), BF), pltpu.VMEM((2, keys, LANES), BF)],
        compiler_params=pltpu.CompilerParams(vmem_limit_bytes=56 * MIB),
        cost_estimate=pl.CostEstimate(
            flops=16 * rows * keys * count * LANES,
            bytes_accessed=2 * (3 * rows + 2 * keys) * count * LANES,
            transcendentals=2 * rows * keys * count,
        ),
    )(qkv, qkv, qkv, aug_q, aug_k, *deps)


def attend_back_kernel(
    slots, tile_k, scale, n_deps,
    q_ref, k_ref, v_ref, o_ref, do_ref, l_ref, ak_ref, *rest,
):
    (
        dqkv_ref, sum_ref,
        qx_ref, qz_ref, dx_ref, dz_ref, kx_ref, vx_ref, kt_ref, acc_ref,
    ) = rest[n_deps:]
    lane = lax.broadcasted_iota(jnp.int32, (1, LANES), 1)
    col = lane % HDIM
    sides = (lane < HDIM, lane >= HDIM)
    rows, keys = q_ref.shape[0], k_ref.shape[0]
    tokens = rows - slots
    grad = do_ref[...].astype(F32)
    prod = grad * o_ref[...].astype(F32)
    zero = jnp.zeros_like(grad)
    for h, sel in enumerate(sides):
        delta = jnp.sum(jnp.where(sel, prod, 0.0), axis=1, keepdims=True)
        qx_ref[h] = pick(sel, q_ref[...], l_ref[...])
        qz_ref[h] = pick(sel, q_ref[...], zero)
        dx_ref[h] = jnp.where(sel, grad, in_columns(col, -delta, zero)).astype(BF)
        dz_ref[h] = jnp.where(sel, grad, 0.0).astype(BF)
        kx_ref[h] = pick(sel, k_ref[...], ak_ref[...])
        vx_ref[h] = pick(sel, v_ref[...], ak_ref[...])
        kt_ref[h] = jnp.where(sel, k_ref[...].astype(F32), 0.0).T.astype(BF)

    def work(q_at, q_n, k_at, k_n, kt_at):
        dq = None
        dk = jnp.zeros((k_n, LANES), F32)
        dv = jnp.zeros((k_n, LANES), F32)
        for h in range(2):
            at, of = pl.ds(k_at, k_n), pl.ds(q_at, q_n)
            p = jnp.exp(nt(kx_ref[h, at, :], qx_ref[h, of, :]))
            dp = nt(vx_ref[h, at, :], dx_ref[h, of, :])
            ds = (p * dp).astype(BF)
            dv += nn(p.astype(BF), dz_ref[h, of, :])
            dk += nn(ds, qz_ref[h, of, :])
            part = nn(kt_ref[h, :, pl.ds(kt_at, k_n)], ds)
            dq = part if dq is None else dq + part
        return dq, dk, dv

    def keep(at, n, dk, dv):
        dqkv_ref[pl.ds(at, n), pl.ds(LANES, LANES)] = dk.astype(BF)
        dqkv_ref[pl.ds(at, n), pl.ds(2 * LANES, LANES)] = dv.astype(BF)

    dq, dk, dv = work(0, slots, 0, slots, 0)
    dq = dq.T * scale
    dqkv_ref[pl.ds(0, slots), pl.ds(0, LANES)] = dq.astype(BF)
    keep(0, slots, dk, dv)
    acc_ref[...] = jnp.zeros_like(acc_ref)
    sum_v = jnp.sum(dv, axis=0, keepdims=True)
    sum_q = jnp.sum(dq, axis=0, keepdims=True)
    for i in range((keys - slots) // tile_k):
        at = slots + i * tile_k
        dq, dk, dv = work(slots, tokens, at, tile_k, at)
        acc_ref[...] += dq
        keep(at, tile_k, dk, dv)
        sum_v += jnp.sum(dv, axis=0, keepdims=True)
    dq = acc_ref[...].T * scale
    dqkv_ref[pl.ds(slots, tokens), pl.ds(0, LANES)] = dq.astype(BF)
    dqkv_ref[pl.ds(rows, keys - rows), pl.ds(0, LANES)] = jnp.zeros((keys - rows, LANES), BF)
    sum_q += jnp.sum(dq, axis=0, keepdims=True)
    sum_ref[pl.ds(0, 1), :] = sum_q
    sum_ref[pl.ds(1, 1), :] = sum_v
    sum_ref[pl.ds(2, 6), :] = jnp.zeros((6, LANES), F32)


def attend_back(qkv, o, do, logs, aug_k, slots, tile_k, scale, first, count, kept, deps=()):
    rows, width = o.shape
    keys = qkv.shape[0]
    of = lambda n, m: pl.BlockSpec((n, LANES), lambda j: (0, 3 * (first + j) + m))
    col = lambda n: pl.BlockSpec((n, LANES), lambda j: (0, first + j))
    fixed = lambda n: pl.BlockSpec((n, LANES), lambda j: (0, 0))
    wide = lambda n: pltpu.VMEM((2, n, LANES), BF)
    deps = tuple(kept) + tuple(deps)
    return pl.pallas_call(
        functools.partial(attend_back_kernel, slots, tile_k, scale, len(deps)),
        grid=(count,),
        out_shape=(
            jax.ShapeDtypeStruct((keys, 3 * width), BF),
            jax.ShapeDtypeStruct((8, width), F32),
        ),
        in_specs=[of(rows, 0), of(keys, 1), of(keys, 2), col(rows), col(rows), col(rows), fixed(keys)]
        + [pl.BlockSpec(memory_space=pl.ANY)] * len(deps),
        out_specs=(pl.BlockSpec((keys, 3 * LANES), lambda j: (0, first + j)), col(8)),
        input_output_aliases={7 + i: i for i in range(len(kept))},
        scratch_shapes=[
            wide(rows), wide(rows), wide(rows), wide(rows), wide(keys), wide(keys),
            pltpu.VMEM((2, LANES, keys), BF),
            pltpu.VMEM((LANES, rows - slots), F32),
        ],
        compiler_params=pltpu.CompilerParams(vmem_limit_bytes=56 * MIB),
        cost_estimate=pl.CostEstimate(
            flops=40 * rows * keys * count * LANES,
            bytes_accessed=2 * (6 * rows + 4 * keys) * count * LANES,
            transcendentals=2 * rows * keys * count,
        ),
    )(qkv, qkv, qkv, o, do, logs, aug_k, *deps)


def nothing(*refs):
    return None


def tie(x, *deps):
    anywhere = pl.BlockSpec(memory_space=pl.ANY)
    return pl.pallas_call(
        nothing,
        out_shape=jax.ShapeDtypeStruct(x.shape, x.dtype),
        in_specs=[anywhere] * (1 + len(deps)),
        out_specs=anywhere,
        input_output_aliases={0: 0},
        cost_estimate=pl.CostEstimate(flops=0, bytes_accessed=0, transcendentals=0),
    )(x, *deps)


def assemble_kernel(n_in, n_deps, n_out, copies, *refs):
    ins, outs, sem = refs[:n_in], refs[n_in + n_deps : n_in + n_deps + n_out], refs[-1]
    started = []
    for i, (source, at, target, to) in enumerate(copies):
        src = ins[source].at[at] if at else ins[source]
        dst = outs[target].at[to] if to else outs[target]
        started.append(pltpu.make_async_copy(src, dst, sem.at[i]))
    for c in started:
        c.start()
    for c in started:
        c.wait()


def assemble(arrays, shapes, copies, deps=()):
    anywhere = pl.BlockSpec(memory_space=pl.ANY)
    vmem = pl.BlockSpec(memory_space=pltpu.VMEM)
    size = sum(math.prod(s) for s in shapes)
    return pl.pallas_call(
        functools.partial(assemble_kernel, len(arrays), len(deps), len(shapes), copies),
        out_shape=tuple(jax.ShapeDtypeStruct(s, arrays[0].dtype) for s in shapes),
        in_specs=[anywhere] * (len(arrays) + len(deps)),
        out_specs=tuple(vmem for _ in shapes),
        scratch_shapes=[pltpu.SemaphoreType.DMA((len(copies),))],
        compiler_params=pltpu.CompilerParams(vmem_limit_bytes=56 * MIB),
        cost_estimate=pl.CostEstimate(flops=0, bytes_accessed=4 * size, transcendentals=0),
    )(*arrays, *deps)


def sums_kernel(n_in, n_deps, n_out, pieces, *refs):
    ins, outs = refs[:n_in], refs[n_in + n_deps : n_in + n_deps + n_out]
    for target, to, terms in pieces:
        total = ins[terms[0][0]][terms[0][1]].astype(F32)
        for source, at in terms[1:]:
            total = total + ins[source][at].astype(F32)
        outs[target][to] = total.astype(outs[target].dtype)


def sums(arrays, outs, pieces, deps=()):
    anywhere = pl.BlockSpec(memory_space=pl.ANY)
    vmem = pl.BlockSpec(memory_space=pltpu.VMEM)
    size = sum(a.size for a in arrays)
    return pl.pallas_call(
        functools.partial(sums_kernel, len(arrays), len(deps), len(outs), pieces),
        out_shape=tuple(jax.ShapeDtypeStruct(s, dt) for s, dt in outs),
        in_specs=[vmem] * len(arrays) + [anywhere] * len(deps),
        out_specs=tuple(vmem for _ in outs),
        compiler_params=pltpu.CompilerParams(vmem_limit_bytes=56 * MIB),
        cost_estimate=pl.CostEstimate(flops=size, bytes_accessed=4 * size, transcendentals=0),
    )(*arrays, *deps)


def own_kernel(n_x, tiles, n_deps, la_ref, lb_ref, ra_ref, rb_ref, ga_ref, gb_ref, *rest):
    rest, (ta_ref, tb_ref) = rest[n_deps:-2], rest[-2:]
    nears, far_own, far_oth = rest[:n_x], rest[n_x], rest[n_x + 1]
    t, j = pl.program_id(0), pl.program_id(1)
    size = ga_ref.shape[0] // n_x
    half = size // 2

    @pl.when((t == 0) & (j == 0))
    def _():
        ta_ref[...] = la_ref[...].astype(F32).T.astype(BF)
        tb_ref[...] = lb_ref[...].astype(F32).T.astype(BF)

    def run(l_ref, r_ref, g_ref):
        part = (nn(l_ref[...], r_ref[...]) + g_ref[...].astype(F32)).astype(BF)
        for x in range(n_x):
            nears[x][...] = part[x * size : x * size + half]

        @pl.when(t == 0)
        def _():
            for x in range(n_x):
                far_own[pl.ds(x * half, half), :] = part[x * size + half : (x + 1) * size]

        @pl.when(t > 0)
        def _():
            for x in range(n_x):
                far_oth[pl.ds(x * half, half), :] = part[x * size + half : (x + 1) * size]

    @pl.when(j < tiles)
    def _():
        run(ta_ref, ra_ref, ga_ref)

    @pl.when(j == tiles)
    def _():
        run(tb_ref, rb_ref, gb_ref)


def own_parts(n_x, lhs_a, rhs_a, away_a, lhs_b, rhs_b, away_b, deps=()):
    m = lhs_a.shape[0]
    k = away_a.shape[0]
    tile = rhs_b.shape[1] // 2
    tiles = rhs_a.shape[1] // (2 * tile)
    cols = (tiles + 1) * tile
    half = k // (2 * n_x)
    left = pl.BlockSpec((m, k), lambda t, j: (0, 0))
    first = lambda n: pl.BlockSpec((n, tile), lambda t, j: (0, t * tiles + jnp.minimum(j, tiles - 1)))
    second = lambda n: pl.BlockSpec((n, tile), lambda t, j: (0, t))
    return pl.pallas_call(
        functools.partial(own_kernel, n_x, tiles, len(deps)),
        grid=(2, tiles + 1),
        out_shape=(jax.ShapeDtypeStruct((half, 2 * cols), BF),) * n_x
        + (jax.ShapeDtypeStruct((n_x * half, cols), BF),) * 2,
        in_specs=[left, left, first(m), second(m), first(k), second(k)]
        + [pl.BlockSpec(memory_space=pl.ANY)] * len(deps),
        out_specs=(pl.BlockSpec((half, tile), lambda t, j: (0, t * (tiles + 1) + j)),) * n_x
        + (
            pl.BlockSpec((n_x * half, tile), lambda t, j: (0, jnp.where(t == 0, j, tiles))),
            pl.BlockSpec((n_x * half, tile), lambda t, j: (0, jnp.where(t == 0, 0, j))),
        ),
        scratch_shapes=[pltpu.VMEM((k, m), BF), pltpu.VMEM((k, m), BF)],
        compiler_params=pltpu.CompilerParams(vmem_limit_bytes=56 * MIB),
        cost_estimate=pl.CostEstimate(
            flops=4 * m * k * cols, bytes_accessed=4 * (m + 2 * k) * cols, transcendentals=0
        ),
    )(lhs_a, lhs_b, rhs_a, rhs_b, away_a, away_b, *deps)


def chunk_of(m):
    return m if m <= 704 else m // 2


def mm_in_kernel(chunk, epilogue, start, finish, n_extra, n_deps, a_ref, h_ref, r_ref, *rest):
    extra, outs = rest[:n_extra], rest[n_extra + n_deps :]
    k = h_ref.shape[0]

    def step(i, carry):
        rows = pl.ds(pl.multiple_of(i * chunk, 16), chunk)
        acc = nn(a_ref[rows, pl.ds(0, k)], h_ref[...]) + nn(a_ref[rows, pl.ds(k, k)], r_ref[...])
        return epilogue(acc, rows, extra, outs, carry)

    last = lax.fori_loop(0, a_ref.shape[0] // chunk, step, start(h_ref.shape[1]))
    finish(last, outs)


def nought(tn):
    return 0


def leave(carry, outs):
    return None


def mm_in(a, h, r, col, width, tn, epilogue, extra, outs, start=nought, finish=leave, deps=()):
    m, k = a.shape[0], h.shape[0] // 2
    tiles = width // tn
    weight = pl.BlockSpec((k, tn), lambda t, j: (t, col // tn + j))
    wide = lambda n: pl.BlockSpec((n, tn), lambda t, j: (0, t * tiles + j))
    return pl.pallas_call(
        functools.partial(mm_in_kernel, chunk_of(m), epilogue, start, finish, len(extra), len(deps)),
        grid=(2, tiles),
        out_shape=tuple(jax.ShapeDtypeStruct((n, 2 * width), dt) for n, dt in outs),
        in_specs=[pl.BlockSpec((m, 2 * k), lambda t, j: (0, 0)), weight, weight]
        + [wide(e.shape[0]) for e in extra]
        + [pl.BlockSpec(memory_space=pl.ANY)] * len(deps),
        out_specs=tuple(wide(n) for n, _ in outs),
        compiler_params=pltpu.CompilerParams(vmem_limit_bytes=56 * MIB),
        cost_estimate=pl.CostEstimate(
            flops=8 * m * k * width,
            bytes_accessed=4 * m * k + 8 * k * width + sum(2 * width * n * 2 for n, _ in outs),
            transcendentals=0,
        ),
    )(a, h, r, *extra, *deps)


def mm_out_kernel(chunk, half_tiles, n_extra, epilogue, a0_ref, a1_ref, h0_ref, h1_ref, r0_ref, r1_ref, *rest):
    extra, o_ref = rest[:n_extra], rest[-1]

    def run(w0_ref, w1_ref):
        def step(i, carry):
            rows = pl.ds(pl.multiple_of(i * chunk, 16), chunk)
            acc = nt(a0_ref[rows, :], w0_ref[...]) + nt(a1_ref[rows, :], w1_ref[...])
            more = [e[rows, :] if e.shape[0] > 8 else e[pl.ds(0, 1), :] for e in extra]
            o_ref[rows, :] = epilogue(acc, *more).astype(o_ref.dtype)
            return carry

        lax.fori_loop(0, a0_ref.shape[0] // chunk, step, 0)

    i = pl.program_id(0)

    @pl.when(i < half_tiles)
    def _():
        run(h0_ref, h1_ref)

    @pl.when(i >= half_tiles)
    def _():
        run(r0_ref, r1_ref)


def mm_out(a, m, h, r, col, width, td, epilogue, extra, dtype, deps=(), row=0):
    k = h.shape[0] // 2
    half = k // td
    at = col // width
    lhs = lambda t: pl.BlockSpec((m, width), lambda i: (0, t))
    if row:
        lhs = lambda t: pl.BlockSpec((pl.Element(m), pl.Element(width)), lambda i: (row, t * width))
    own = lambda t: pl.BlockSpec((td, width), lambda i: (t * half + jnp.minimum(i, half - 1), at))
    oth = lambda t: pl.BlockSpec((td, width), lambda i: (t * half + jnp.maximum(i - half, 0), at))
    wide = lambda n: pl.BlockSpec((min(n, m), td), lambda i: (0, i))
    return pl.pallas_call(
        functools.partial(mm_out_kernel, chunk_of(m), half, len(extra), epilogue),
        grid=(2 * half,),
        out_shape=jax.ShapeDtypeStruct((m, 2 * k), dtype),
        in_specs=[lhs(0), lhs(1), own(0), own(1), oth(0), oth(1)]
        + [wide(e.shape[0]) for e in extra]
        + [pl.BlockSpec(memory_space=pl.ANY)] * len(deps),
        out_specs=wide(m),
        compiler_params=pltpu.CompilerParams(vmem_limit_bytes=56 * MIB),
        cost_estimate=pl.CostEstimate(
            flops=8 * m * k * width,
            bytes_accessed=4 * m * width + 8 * k * width + 8 * m * k,
            transcendentals=0,
        ),
    )(a, a, h, h, r, r, *extra, *deps)


def put_plain(acc, rows, extra, outs, carry):
    outs[0][rows, :] = acc.astype(outs[0].dtype)
    return carry


def put_biased(acc, rows, extra, outs, carry):
    outs[0][rows, :] = (acc + extra[0][pl.ds(0, 1), :]).astype(outs[0].dtype)
    return carry


def put_scaled(acc, rows, extra, outs, carry):
    low = (acc + extra[0][pl.ds(0, 1), :]).astype(BF).astype(F32)
    outs[0][rows, :] = (low * extra[0][pl.ds(1, 1), :]).astype(BF)
    return carry


def put_gelu(acc, rows, extra, outs, carry):
    inner = acc + extra[0][pl.ds(0, 1), :]
    out, slope = gelu_parts(inner)
    outs[0][rows, :] = out.astype(BF)
    outs[1][rows, :] = slope.astype(BF)
    return carry


def put_sloped(acc, rows, extra, outs, carry):
    grad = acc * extra[0][rows, :].astype(F32)
    outs[0][rows, :] = grad.astype(BF)
    return carry + jnp.sum(grad, axis=0, keepdims=True)


def row_of_zeros(tn):
    return jnp.zeros((1, tn), F32)


def put_sum(carry, outs):
    outs[1][...] = jnp.broadcast_to(carry, outs[1].shape)


def eight(*rows):
    return jnp.concatenate([jnp.stack(rows), jnp.zeros((8 - len(rows), rows[0].shape[0]), F32)])


def gelu_parts(v):
    size = jnp.abs(v)
    t = 1.0 / ((0.3275911 * math.sqrt(0.5)) * size + 1.0)
    bell = jnp.exp(-0.5 * (v * v))
    poly = (0.5 * 1.061405429) * t - 0.5 * 1.453152027
    poly = (poly * t + 0.5 * 1.421413741) * t - 0.5 * 0.284496736
    poly = (poly * t + 0.5 * 0.254829592) * t
    low = bell * (poly - size * (1.0 / math.sqrt(2.0 * math.pi)))
    return jnp.maximum(v, 0.0) - size * (poly * bell), jnp.where(v < 0.0, low, 1.0 - low)


def norm_parts(v):
    centered = v - jnp.mean(v, axis=-1, keepdims=True)
    rstd = lax.rsqrt(jnp.mean(centered * centered, axis=-1, keepdims=True) + LN_EPS)
    return centered * rstd, rstd


def norm_back(c, vhat, rstd, gain):
    gc = c * gain
    back = (
        gc
        - jnp.mean(gc, axis=-1, keepdims=True)
        - vhat * jnp.mean(gc * vhat, axis=-1, keepdims=True)
    ) * rstd
    return back, jnp.sum(c * vhat, axis=0), jnp.sum(c, axis=0)


def make(n_pb, n_pa, n_ta):
    cores = 2
    n_x = n_pb // cores
    blocks = n_pb * n_pa

    def px(v, k):
        return lax.ppermute(v, "pb", [(i, i ^ (cores * k)) for i in range(n_pb)])

    def pc(v):
        return lax.ppermute(v, "pb", [(i, i ^ 1) for i in range(n_pb)])

    def pz(v, k):
        return lax.ppermute(v, "pa", [(i, i ^ k) for i in range(n_pa)])

    def py(v):
        return lax.ppermute(v, "ta", [(i, i ^ 1) for i in range(n_ta)])

    x_bits = n_x.bit_length() - 1
    z_bits = n_pa.bit_length() - 1

    def after(v, *deps):
        return tie(v, *deps) if deps else v

    every = slice(None)

    def z_go(have, bit):
        return pz(have, 1 << bit)

    def z_end(have, other, deps=()):
        n, w, cols = have.shape
        (out,) = assemble(
            (have, other), ((n, 2, w, cols),), ((0, (), 0, (every, 0)), (1, (), 0, (every, 1))), deps
        )
        return out.reshape(2 * n, w, cols)

    def z_last(have, other, deps=()):
        n, w, cols = have.shape
        h = n // 2
        near, far = assemble(
            (have, other), ((h, 2, w, cols), (h, 2, w, cols)),
            tuple(
                (source, (pl.ds(s * h, h),), s, (every, source)) for s in range(2) for source in range(2)
            ),
            deps,
        )
        return near.reshape(n, w, cols), far.reshape(n, w, cols)

    def z_rest(have, other):
        have = z_end(have, other)
        for bit in reversed(range(1, z_bits - 1)):
            have = z_end(have, z_go(have, bit))
        return have, z_go(have, 0)

    def gather_z(shard):
        have = shard[None]
        for bit in reversed(range(z_bits)):
            have = z_end(have, z_go(have, bit))
        return have.reshape(-1, have.shape[-1])

    def joined(parts, deps=()):
        (out,) = assemble(
            tuple(parts), ((len(parts),) + parts[0].shape,),
            tuple((i, (), 0, (i,)) for i in range(len(parts))), deps,
        )
        return out

    def spread_x(a):
        have, arrays = [(0, None)], [a]
        for bit in range(x_bits):
            whole = arrays[0] if bit == 0 else joined([arrays[i] if p is None else arrays[i][p] for i, p in have])
            arrays.append(px(whole, 1 << bit))
            last = len(arrays) - 1
            have = have + ([(last, None)] if bit == 0 else [(last, p) for p in range(len(have))])
        return [arrays[i] if p is None else arrays[i][p] for i, p in have]

    def xy_go(near, far):
        return spread_x(near), [far, py(far)]

    def xy_one(going, deps=()):
        near_xs, far_ts = going
        return joined(near_xs, deps), joined(far_ts, deps)

    def xy_two_go(near_x, far_t):
        return near_x, py(near_x), spread_x(far_t)

    def xy_two(going, deps=()):
        near_x, near_oth, far_x = going
        _, h, w, cols = near_x.shape
        copies = []
        for x in range(n_x):
            for t in range(n_ta):
                copies.append((t, (x,), 0, (t, x, 0)))
                copies.append((n_ta + x, (t,), 0, (t, x, 1)))
        (out,) = assemble(
            (near_x, near_oth, *far_x), ((n_ta, n_x, 2, h, w, cols),), tuple(copies), deps
        )
        return out.reshape(-1, cols)

    def add(a, b):
        return (a.astype(F32) + b.astype(F32)).astype(a.dtype)

    def away_part(lhs, rhs):
        return pc(tn(lhs[:, lhs.shape[1] // 2 :], rhs).astype(BF))

    def core_part(lhs, rhs, away):
        return (tn(lhs[:, : lhs.shape[1] // 2], rhs) + away.astype(F32)).astype(BF)

    def p1_send(parts, deps=()):
        rows = parts[0].shape[0]
        size = rows // n_x
        half = size // 2
        widths = [r.shape[1] // n_ta for r in parts]
        cols = sum(widths)
        copies = []
        for i, n in enumerate(widths):
            at = sum(widths[:i])
            for t in range(n_ta):
                for x in range(n_x):
                    copies.append((
                        i, (pl.ds(x * size, half), pl.ds(t * n, n)), x, (every, pl.ds(t * cols + at, n)),
                    ))
                    copies.append((
                        i, (pl.ds(x * size + half, half), pl.ds(t * n, n)),
                        n_x + t, (pl.ds(x * half, half), pl.ds(at, n)),
                    ))
        shapes = ((half, n_ta * cols),) * n_x + ((n_x * half, cols),) * n_ta
        out = assemble(tuple(parts), shapes, tuple(copies), deps)
        return out[:n_x], out[n_x], out[n_x + 1]

    def p1_go(sent):
        near, far_own, far_oth = sent
        return [px(near[k], k) for k in range(1, n_x)], py(far_oth)

    def p1_end(sent, got, deps=()):
        near, far_own, _ = sent
        half, cols = near[0].shape[0], far_own.shape[1]
        n = len(got[0])
        pieces = []
        for t in range(n_ta):
            at = (every, pl.ds(t * cols, cols))
            pieces.append((t, (), [(i, at) for i in range(n + 1)]))
        for x in range(n_x):
            at = (pl.ds(x * half, half), every)
            pieces.append((n_ta + x, (), [(n + 1, at), (n + 2, at)]))
        pieces = [(o, to or (every, every), terms) for o, to, terms in pieces]
        out = sums(
            (near[0], *got[0], far_own, got[1]), (((half, cols), BF),) * (n_ta + n_x), pieces, deps
        )
        return out[0], out[1], out[2:]

    def p2_go(state):
        near_own, near_oth, far = state
        return py(near_oth), [px(far[k], k) for k in range(1, n_x)]

    def p2_end(state, got, w, deps=()):
        half, cols = state[0].shape
        h = half // w
        pieces = []
        for b in range(2 * h):
            at = (pl.ds((b % h) * w, w), every)
            terms = [(0, at), (1, at)] if b < h else [(i, at) for i in range(2, 3 + len(got[1]))]
            pieces.append((b % 2, (b // 2,), terms))
        return sums(
            (state[0], got[0], state[2][0], *got[1]), (((h, w, cols), BF),) * 2, pieces, deps
        )

    def z_next(keep, got, deps=()):
        n, w, cols = keep.shape
        pieces = [(b % 2, (b // 2,), [(0, (b,)), (1, (b,))]) for b in range(n)]
        return sums((keep, got), (((n // 2, w, cols), BF),) * 2, pieces, deps)

    def z_done(keep, got, deps=()):
        _, w, cols = keep.shape
        (out,) = sums((keep, got), (((1, w, cols), F32),), [(0, (0,), [(0, (0,)), (1, (0,))])], deps)
        return out[0]

    def z_split(cur):
        cur = cur.reshape((cur.shape[0] // 2, 2) + cur.shape[1:])
        return cur[:, 0], cur[:, 1]

    def reduce_z(cur):
        for bit in range(z_bits):
            keep, give = z_split(cur)
            got = pz(give, 1 << bit)
            cur = keep.astype(F32) + got.astype(F32) if bit == z_bits - 1 else add(keep, got)
        return cur[0]

    def reduce_z_from(keep, give, first):
        for bit in range(first, z_bits - 1):
            keep, give = z_next(keep, pz(give, 1 << bit))
        return z_done(keep, pz(give, 1 << (z_bits - 1)))

    def on_device(
        rows_in, w_qkv, b_qv, w_out, b_out, ln1_gain, ln1_bias, w_in, b_in, w_fin, b_fin,
        ln2_gain, ln2_bias, w_head, b_head, lengths, query_len, score_grad,
    ):
        t0 = lax.axis_index("ta")
        z0 = lax.axis_index("pa")
        p0 = lax.axis_index("pb")
        x0, c0 = p0 // cores, p0 % cores
        first_t = t0 == 0
        all_rows, width = rows_in.shape
        half_rows = all_rows // n_ta
        n_q, n_p = query_len.shape[1], lengths.shape[1]
        q_here = n_q // n_ta
        slots = q_here * QLEN
        toks = half_rows - slots
        block = width // blocks
        heads_half = w_qkv.shape[2]
        scale = 1.0 / math.sqrt(HDIM)

        per_tile = LANES // block
        z_tiles = n_pa // per_tile
        low_bits = per_tile.bit_length() - 1
        forward, backward = [], []
        for c in range(cores):
            for x in range(n_x):
                for z in range(z_tiles):
                    forward.append((((x ^ x0) * cores) + (c ^ c0)) * z_tiles + (z ^ (z0 // per_tile)))
        for x in range(n_x):
            for c in range(cores):
                for z in range(z_tiles):
                    backward.append((((c ^ c0) * n_x) + (x ^ x0)) * z_tiles + (z ^ (z0 // per_tile)))
        low = z0 % per_tile
        as_info = lambda v: jnp.stack([jnp.asarray(a, jnp.int32) for a in v])
        row_info = as_info(forward + [low, t0 * half_rows, (1 - t0) * half_rows + slots])
        vec_info = as_info(forward + [low, 0])
        back_info = as_info(backward + [low, 0])

        rows = permute(rows_in, row_info, (half_rows, toks), block, low_bits)
        vecs = jnp.stack(
            [b_out, ln1_gain, ln1_bias, b_fin, ln2_gain, ln2_bias, b_out, b_out]
        )
        vecs = permute(vecs, vec_info, (8,), block, low_bits)
        b_out_r, g1, be1, b_fin_r, g2, be2 = (vecs[i] for i in range(6))
        pairs = heads_half // LANES
        all_pairs = n_ta * pairs
        ff_half = w_in.shape[1]
        head_half = width // n_ta
        qkv_half = 3 * heads_half
        swapped = lambda v: jnp.concatenate([v[..., v.shape[-1] // 2 :], v[..., : v.shape[-1] // 2]], axis=-1)
        in_order = lambda v: jnp.where(first_t, v, swapped(v))

        row_id = jnp.arange(half_rows + toks, dtype=jnp.int32)
        is_slot = row_id < slots
        token = jnp.where(
            row_id < half_rows, t0 * toks + row_id - slots, (1 - t0) * toks + row_id - half_rows
        )
        ends = jnp.cumsum(lengths[0])
        pid = jnp.sum((token[:, None] >= ends[None, :]).astype(jnp.int32), axis=1)
        q_lens = lax.dynamic_index_in_dim(query_len, z0, 0, keepdims=False)
        q_lens = lax.dynamic_slice_in_dim(q_lens, t0 * q_here, q_here, 0)
        limit = jnp.sum(
            jnp.where(
                (row_id // QLEN)[:, None] == jnp.arange(q_here, dtype=jnp.int32)[None, :],
                q_lens[None, :], 0,
            ),
            axis=1,
        )
        dead = is_slot & (row_id % QLEN >= limit)
        seg = jnp.where(is_slot, n_p + row_id // QLEN, pid)
        lane_c = jnp.arange(LANES, dtype=jnp.int32)[None, :] % HDIM
        same = seg[:, None] == lane_c
        aug_k = jnp.where(
            lane_c < 6, same & ~dead[:, None], jnp.where(lane_c == 6, dead[:, None], (lane_c >= 7) & (lane_c < 10))
        )
        aug_k = aug_k.astype(BF)
        aug_q = jnp.where((lane_c < 7) & ~same[:half_rows], BIG, 0.0).astype(BF)

        packed = lambda v: v.reshape(v.shape[0], 3, pairs, LANES).transpose(0, 2, 1, 3)
        shard_q = packed(w_qkv.transpose(1, 0, 2).reshape(block, qkv_half)).reshape(block, -1)
        shard_m = jnp.concatenate([w_in, w_out.T], axis=1)
        head_mine = lax.dynamic_slice_in_dim(w_head, t0 * head_half, head_half, 1)
        shard_e = jnp.concatenate([w_fin.T, head_mine], axis=1)

        q_0 = shard_q[None]
        q_1 = z_go(q_0, z_bits - 1)
        q_2, q_3 = z_rest(q_0, q_1)
        near_q, far_q = z_last(q_2, q_3)
        m_0 = tie(shard_m[None], near_q)
        m_1 = z_go(m_0, z_bits - 1)
        near_q, far_q = xy_one(xy_go(near_q, far_q), (rows, aug_q, aug_k))
        h_q = xy_two(xy_two_go(near_q, far_q), (m_1,))
        r_q = pc(h_q)
        m_2, m_3 = z_rest(m_0, m_1)
        bias_of = lambda b: packed(jnp.concatenate([b[0], jnp.zeros_like(b[0]), b[1]])[None]).reshape(-1)
        qkv_bias = jnp.concatenate([bias_of(b_qv), bias_of(py(b_qv))])
        b_in_r = jnp.concatenate([b_in, py(b_in)])

        col_scale = jnp.tile(jnp.repeat(jnp.array([scale, 1.0, 1.0], F32), LANES), all_pairs)
        (qkv,) = mm_in(
            rows, h_q, r_q, 0, qkv_half, qkv_half // 3, put_scaled, (eight(qkv_bias, col_scale),),
            ((half_rows + toks, BF),), deps=(m_2,),
        )
        near_m, far_m = z_last(m_2, m_3, (qkv,))
        e_0 = tie(shard_e[None], near_m)
        e_1 = z_go(e_0, z_bits - 1)
        n_call = all_pairs // 4
        part = lambda i, kept, deps: attend(
            qkv, half_rows, aug_q, aug_k, slots, toks, i * n_call, n_call, kept, deps
        )
        going = xy_go(near_m, far_m)
        kept = part(0, (), (near_m, e_0))
        near_m, far_m = xy_one(going, (kept[0],))
        going = xy_two_go(near_m, far_m)
        e_2 = z_end(e_0, e_1, (kept[0],))
        for bit in reversed(range(1, z_bits - 1)):
            e_2 = z_end(e_2, z_go(e_2, bit))
        e_3 = z_go(e_2, 0)
        kept = part(1, kept, (near_m, far_m, e_2))
        kept = part(2, kept, ())
        near_e, far_e = z_last(e_2, e_3, (kept[0],))
        going_e = xy_go(near_e, far_e)
        kept = part(3, kept, (near_e,))
        h_m = xy_two(going, (kept[0],))
        r_m = pc(h_m)
        near_e, far_e = xy_one(going_e, (h_m,))
        ctx, logs = kept
        h_one = mm_out(
            ctx, half_rows, h_m, r_m, ff_half, heads_half, heads_half // 2,
            lambda acc, res, b: acc + res.astype(F32) + b, (rows, eight(b_out_r)), F32,
            (near_e, far_e),
        )
        v1, r1 = norm_parts(h_one)
        normed = v1 * g1 + be1
        normed_low = normed.astype(BF)
        active, slope = mm_in(
            normed_low, h_m, r_m, 0, ff_half, ff_half // 4, put_gelu, (eight(b_in_r),),
            ((half_rows, BF), (half_rows, BF)),
        )
        h_e = xy_two(xy_two_go(near_e, far_e), (active,))
        r_e = pc(h_e)
        h_two = mm_out(
            active, half_rows, h_e, r_e, 0, ff_half, heads_half // 2,
            lambda acc, res, b: acc + res + b, (normed, eight(b_fin_r)), F32,
        )
        v2, r2 = norm_parts(h_two)
        output_low = (v2 * g2 + be2).astype(BF)
        (raw,) = mm_in(
            output_low, h_e, r_e, ff_half, head_half, head_half, put_biased,
            (eight(in_order(b_head)),), ((half_rows, F32),),
        )
        inv = lax.rsqrt(jnp.sum(raw * raw, axis=-1, keepdims=True) + UNIT_EPS)
        unit = raw * inv
        unit_low = unit.astype(BF)

        passages = unit_low[slots:]
        mine = gather_z(unit_low[:slots])
        asked = jnp.concatenate([mine, swapped(py(mine))], axis=0)
        n_asked = asked.shape[0]
        z_rel = jnp.arange(n_pa, dtype=jnp.int32) ^ z0
        swap_t = lambda a: jnp.where(first_t, a, a[::-1])
        lens = swap_t(
            jnp.take(query_len, z_rel, axis=0).reshape(n_pa, n_ta, q_here).transpose(1, 0, 2)
        )
        valid = (
            jnp.arange(QLEN, dtype=jnp.int32)[None, None, None, :] < lens[..., None]
        ).astype(F32)
        up = swap_t(
            jnp.take(score_grad[0], z_rel, axis=0).reshape(n_pa, n_ta, q_here, n_p).transpose(1, 0, 2, 3)
        )
        token_grad = (up[:, :, :, None, :] * valid[..., None]).reshape(n_asked, n_p)
        member = (
            pid[slots:half_rows, None] == jnp.arange(n_p, dtype=jnp.int32)[None, :]
        ).astype(F32)
        powers = jnp.exp(nt(asked, passages) * (1.0 / SHARP))
        sums = jnp.dot(powers, member, precision=lax.Precision.HIGHEST)
        theirs = py(sums.reshape(n_ta, n_asked // n_ta, n_p)[::-1])
        sums = sums + theirs.reshape(n_asked, n_p)
        soft = (SHARP * jnp.log(sums)).reshape(n_ta, n_pa, q_here, QLEN, n_p)
        scores = jnp.sum(soft[0] * valid[0][..., None], axis=2)
        scores = jnp.take(scores, z_rel, axis=0)[None]
        coef = token_grad / sums
        coef_j = sum(coef[:, i : i + 1] * member[:, i][None, :] for i in range(n_p))
        sim_grad = (powers * coef_j).astype(BF)
        ask_grad = nn(sim_grad, passages).astype(BF).reshape(n_ta, n_pa * slots, width)
        ask_sum = add(ask_grad[0], py(swapped(ask_grad[1])))
        passage_grad = tn(sim_grad, asked)
        unit_grad = jnp.concatenate(
            [reduce_z(ask_sum.reshape(n_pa, slots, width)), passage_grad], axis=0
        )

        raw_grad = inv * (unit_grad - unit * jnp.sum(unit * unit_grad, axis=-1, keepdims=True))
        g_b_head = in_order(jnp.sum(raw_grad, axis=0))
        raw_low = raw_grad.astype(BF)
        output_grad = mm_out(
            raw_low, half_rows, h_e, r_e, ff_half, head_half, heads_half // 2, lambda acc: acc, (), F32
        )
        h_two_grad, g_g2, g_be2 = norm_back(output_grad, v2, r2, g2)
        g_b_fin = jnp.sum(h_two_grad, axis=0)
        branch_low = h_two_grad.astype(BF)
        away_fin = away_part(branch_low, active)
        away_head = away_part(output_low, raw_low)
        inner_low, sums_in = mm_in(
            branch_low, h_e, r_e, 0, ff_half, ff_half // 4, put_sloped, (slope,),
            ((half_rows, BF), (8, F32)), row_of_zeros, put_sum,
        )
        *near, far_own, far_oth = own_parts(
            n_x, branch_low, active, away_fin, output_low, raw_low, away_head, (inner_low,)
        )
        sent_f = (near, far_own, far_oth)
        got_f = p1_go(sent_f)
        away_in = away_part(normed_low, inner_low)
        normed_grad = mm_out(
            inner_low, half_rows, h_m, r_m, 0, ff_half, heads_half // 2,
            lambda acc, res: acc + res, (h_two_grad,), F32, (sent_f[0][-1], sent_f[2]),
        )
        state_f = p1_end(sent_f, got_f, (normed_grad,))
        got_f = p2_go(state_f)
        h_one_grad, g_g1, g_be1 = norm_back(normed_grad, v1, r1, g1)
        g_b_out = jnp.sum(h_one_grad, axis=0)
        attended_low = h_one_grad.astype(BF)
        away_out = away_part(attended_low, ctx)
        (d_ctx,) = mm_in(
            attended_low, h_m, r_m, ff_half, heads_half, heads_half, put_plain, (), ((half_rows, BF),),
            deps=(state_f[1], state_f[2][-1]),
        )
        *near, far_own, far_oth = own_parts(
            n_x, normed_low, inner_low, away_in, attended_low, ctx, away_out, (d_ctx,)
        )
        sent_m = (near, far_own, far_oth)
        got_m = p1_go(sent_m)

        back = lambda i, kept, deps: attend_back(
            qkv, ctx, d_ctx, logs, aug_k, slots, 2 * toks // 5, scale,
            ((i + 2) % 4) * n_call, n_call, kept, deps,
        )
        quarter = qkv_half // 2
        columns = lambda a, i: a[:, i * quarter : (i + 1) * quarter]
        rows_x = width // (cores * n_x)
        x_blocks = lambda part: [part[k * rows_x : (k + 1) * rows_x] for k in range(n_x)]
        x_go = lambda blocks_of: [px(blocks_of[k], k) for k in range(1, n_x)]

        def x_end(blocks_of, got):
            total = blocks_of[0]
            for g in got:
                total = add(total, g)
            return total

        keep_f, give_f = p2_end(state_f, got_f, block, (sent_m[2],))
        z_f = pz(give_f, 1)
        kept = back(0, (), (sent_m[0][-1], sent_m[2], give_f))
        keep_f, give_f = z_next(keep_f, z_f, (kept[1],))
        z_f = pz(give_f, 2)
        state_m = p1_end(sent_m, got_m, (kept[1],))
        got_m = p2_go(state_m)
        kept = back(1, kept, (give_f, state_m[1], state_m[2][-1]))
        if z_bits == 2:
            out_f = z_done(keep_f, z_f, (kept[1],))
        else:
            out_f = reduce_z_from(*z_next(keep_f, z_f), 2)
        keep_m, give_m = p2_end(state_m, got_m, block, (kept[1],))
        z_m = pz(give_m, 1)
        rows = tie(rows, give_m, out_f)
        away_1 = away_part(rows, kept[0][:, qkv_half:])
        part_1 = core_part(rows, kept[0][:, qkv_half:], away_1)
        sent_1 = x_blocks(part_1)
        got_1 = x_go(sent_1)
        kept = back(2, kept, (sent_1[1], give_m))
        keep_m, give_m = z_next(keep_m, z_m, (kept[1],))
        z_m = pz(give_m, 2)
        rows = tie(rows, give_m)
        away_2 = away_part(rows, columns(kept[0], 0))
        y_1 = x_end(sent_1, [tie(g, kept[1]) for g in got_1])
        part_2 = core_part(rows, columns(kept[0], 0), tie(away_2, y_1))
        sent_2 = x_blocks(part_2)
        got_2 = x_go(sent_2)
        g_w_fin, g_head = out_f[:, :ff_half], out_f[:, ff_half:]
        n_h = block // n_ta
        head_keep = jnp.where(first_t, g_head[:n_h], g_head[n_h:])
        head_got = py(jnp.where(first_t, g_head[n_h:], g_head[:n_h]))
        kept = back(3, kept, (y_1, sent_2[1], give_m))
        head_got = tie(head_got, kept[1])
        d_qkv, sums_qv = kept
        y_1 = py(y_1)
        if z_bits == 2:
            out_m = z_done(keep_m, z_m, (sums_qv,))
        else:
            out_m = reduce_z_from(*z_next(keep_m, z_m), 2)
        y_1 = tie(y_1, sums_qv)
        rows = tie(rows, y_1, out_m, head_got)
        away_3 = away_part(rows, columns(d_qkv, 1))
        to_other = mm_out(
            d_qkv, toks, h_q, r_q, 0, qkv_half, heads_half // 2, lambda acc: acc, (), BF,
            (away_3,), row=half_rows,
        )
        to_other_part = to_other
        d_qkv = tie(d_qkv, to_other)
        part_3 = core_part(rows, columns(d_qkv, 1), away_3)
        sent_3 = x_blocks(part_3)
        got_3 = x_go(sent_3)
        to_other = py(to_other)
        q_2 = add(x_end(sent_2, [tie(g, to_other_part) for g in got_2]), y_1[:, :quarter]).reshape(n_pa, block, -1)
        grad_rows = mm_out(
            d_qkv, half_rows, h_q, r_q, 0, qkv_half, heads_half // 2,
            lambda acc, res: acc + res, (h_one_grad,), F32, (sent_3[1], q_2),
        )
        to_other = tie(to_other, grad_rows)
        got_3 = [tie(g, grad_rows) for g in got_3]
        q_3 = add(x_end(sent_3, got_3), y_1[:, quarter:]).reshape(n_pa, block, -1)
        keep_q, give_q = z_split(jnp.concatenate([q_2, q_3], axis=2))
        keep_q, give_q = z_split(add(keep_q, pz(give_q, 1)))
        to_other, keep_q = tie(to_other, give_q), tie(keep_q, to_other)
        sums_qv = tie(sums_qv, to_other)
        if z_bits == 2:
            out_q = (keep_q.astype(F32) + pz(give_q, 2).astype(F32))[0]
        else:
            out_q = reduce_z_from(*z_next(keep_q, pz(give_q, 2)), 2)
        g_w_qkv = out_q.reshape(block, pairs, 3, LANES).transpose(2, 0, 1, 3).reshape(3, block, heads_half)
        g_w_in, g_w_out = out_m[:, :ff_half], out_m[:, ff_half:]
        g_w_head = in_order(jnp.concatenate([head_keep, head_got], axis=1))
        grad_rows = permute(
            grad_rows, back_info, (half_rows,), block, low_bits, slots, (to_other,)
        )

        d_vecs = permute(
            eight(g_b_out, g_g1, g_be1, g_b_fin, g_g2, g_be2), back_info, (8,), block, low_bits
        )
        vec = jnp.concatenate(
            [d_vecs, in_order(sums_in[0]).reshape(-1, width), g_b_head[None], in_order(sums_qv[:2])]
        )
        vec = vec + pc(vec)
        for bit in range(x_bits):
            vec = vec + px(vec, 1 << bit)
        vec = vec + py(vec)
        for bit in range(z_bits):
            vec = vec + pz(vec, 1 << bit)
        place = (p0 * n_pa + z0) * n_ta + t0
        w32 = width // (blocks * n_ta)
        ff_rows = n_ta * ff_half // width
        mine = lax.dynamic_slice_in_dim(vec, place * w32, w32, 1)
        o_b_out, o_g1, o_be1, o_b_fin, o_g2, o_be2 = (mine[i] for i in range(6))
        o_b_head, o_bqv = mine[8 + ff_rows], mine[9 + ff_rows : 11 + ff_rows]
        o_b_in = lax.dynamic_slice_in_dim(
            vec[8 : 8 + ff_rows].reshape(-1), place * (ff_rows * w32), ff_rows * w32, 0
        )
        return (
            scores, grad_rows, g_w_qkv, o_bqv, g_w_out.T, o_b_out, o_g1, o_be1,
            g_w_in, o_b_in, g_w_fin.T, o_b_fin, o_g2, o_be2, g_w_head, o_b_head,
        )

    return on_device


def solution(mesh):
    both = ("pb", "pa")
    every = ("pb", "pa", "ta")
    in_specs = (
        P(both, None), P(None, both, "ta"), P(None, "ta"), P("ta", both), P(), P(), P(),
        P(both, "ta"), P("ta"), P("ta", both), P(), P(), P(), P(both, None), P(),
        P(both, None), P("pb", None), P("pb", None, None, "pa"),
    )
    out_specs = (
        P("pb", None, "ta", "pa"), P(every, None), P(None, both, "ta"), P(None, every),
        P("ta", both), P(every), P(every), P(every), P(both, "ta"), P(every), P("ta", both),
        P(every), P(every), P(every), P(every, None), P(every),
    )
    step = make(mesh.shape["pb"], mesh.shape["pa"], mesh.shape["ta"])
    return jax.shard_map(step, mesh=mesh, in_specs=in_specs, out_specs=out_specs, check_vma=False)
```

```python
import functools
import math

import jax
import jax.numpy as jnp
from jax import lax
from jax.experimental import pallas as pl
from jax.experimental.pallas import tpu as pltpu
from jax.sharding import PartitionSpec as P

HDIM = 64
QLEN = 32
LANES = 128
SHARP = 0.02
LN_EPS = 1e-05
UNIT_EPS = 1e-06
BIG = -1e30
BF = jnp.bfloat16
F32 = jnp.float32
MIB = 1024 * 1024


def nn(a, b):
    return lax.dot_general(a, b, (((1,), (0,)), ((), ())), preferred_element_type=F32)


def nt(a, b):
    return lax.dot_general(a, b, (((1,), (1,)), ((), ())), preferred_element_type=F32)


def tn(a, b):
    return lax.dot_general(a, b, (((0,), (0,)), ((), ())), preferred_element_type=F32)


def permute_kernel(segments, block, low_bits, skip, info, x_ref, *rest):
    o_ref = rest[-1]
    tiles = x_ref.shape[1] // LANES
    lane = lax.broadcasted_iota(jnp.int32, (1, LANES), 1)
    low = info[tiles]
    for j in range(tiles):
        source = pl.multiple_of(info[j] * LANES, LANES)
        row = 0
        for i, length in enumerate(segments):
            start = pl.multiple_of(info[tiles + 1 + i], 16)
            part = x_ref[pl.ds(start, length), pl.ds(source, LANES)]
            if skip is not None:
                more = rest[0][:, pl.ds(source, LANES)].astype(F32)
                part = jnp.concatenate([part[:skip], part[skip:] + more], axis=0)
            if low_bits:
                part = part.astype(F32)
                for bit in range(low_bits):
                    step = block << bit
                    up = pltpu.roll(part, step, 1)
                    down = pltpu.roll(part, LANES - step, 1)
                    swapped = jnp.where((lane & step) != 0, up, down)
                    part = jnp.where((low & (1 << bit)) != 0, swapped, part)
                part = part.astype(o_ref.dtype)
            o_ref[pl.ds(row, length), pl.ds(j * LANES, LANES)] = part
            row += length


def permute(x, info, segments, block, low_bits, skip=None, more=()):
    rows = sum(segments)
    return pl.pallas_call(
        functools.partial(permute_kernel, segments, block, low_bits, skip),
        out_shape=jax.ShapeDtypeStruct((rows, x.shape[1]), x.dtype),
        in_specs=[
            pl.BlockSpec(memory_space=pltpu.SMEM),
            pl.BlockSpec(memory_space=pltpu.VMEM),
        ]
        + [pl.BlockSpec(memory_space=pltpu.VMEM)] * len(more),
        out_specs=pl.BlockSpec(memory_space=pltpu.VMEM),
        compiler_params=pltpu.CompilerParams(vmem_limit_bytes=56 * MIB),
        cost_estimate=pl.CostEstimate(
            flops=rows * x.shape[1], bytes_accessed=4 * rows * x.shape[1], transcendentals=0
        ),
    )(info, x, *more)


def pick(sel, a, b):
    return jnp.where(sel, a.astype(F32), b.astype(F32)).astype(BF)


def split3(v):
    hi = v.astype(BF).astype(F32)
    mid = (v - hi).astype(BF).astype(F32)
    return hi, mid, v - hi - mid


def in_columns(col, v, base):
    hi, mid, lo = split3(v)
    return jnp.where(col == 7, hi, jnp.where(col == 8, mid, jnp.where(col == 9, lo, base)))


def attend_kernel(slots, tile_q, n_deps, q_ref, k_ref, v_ref, aq_ref, ak_ref, *rest):
    o_ref, l_ref, kx_ref, vx_ref = rest[n_deps:]
    lane = lax.broadcasted_iota(jnp.int32, (1, LANES), 1)
    col = lane % HDIM
    sides = (lane < HDIM, lane >= HDIM)
    for h, sel in enumerate(sides):
        kx_ref[h] = pick(sel, k_ref[...], ak_ref[...])
        vx_ref[h] = pick(sel, v_ref[...], jnp.ones_like(v_ref[...]))
    keys = k_ref.shape[0]

    def work(q_at, q_n, k_at, k_n):
        rows = pl.ds(q_at, q_n)
        q, aug = q_ref[rows, :], aq_ref[rows, :]
        outs, logs = [], []
        for h, sel in enumerate(sides):
            s = nt(pick(sel, q, aug), kx_ref[h, pl.ds(k_at, k_n), :])
            top = jnp.max(s, axis=1, keepdims=True)
            p = jnp.exp(s - top).astype(BF)
            o = nn(p, vx_ref[h, pl.ds(k_at, k_n), :])
            outs.append(o / pltpu.roll(o, HDIM, 1))
            logs.append(in_columns(col, -(top + jnp.log(o)), aug.astype(F32)))
        o_ref[rows, :] = jnp.where(sides[0], outs[0], outs[1]).astype(BF)
        l_ref[rows, :] = jnp.where(sides[0], logs[1], logs[0]).astype(BF)

    work(0, slots, 0, slots)
    tokens = q_ref.shape[0] - slots

    def step(i, carry):
        work(pl.multiple_of(slots + i * tile_q, 16), tile_q, slots, keys - slots)
        return carry

    lax.fori_loop(0, tokens // tile_q, step, 0)


def attend(qkv, rows, aug_q, aug_k, slots, tile_q, first, count, kept, deps=()):
    keys, width = qkv.shape[0], qkv.shape[1] // 3
    of = lambda n, m: pl.BlockSpec((n, LANES), lambda j: (0, 3 * (first + j) + m))
    out = pl.BlockSpec((rows, LANES), lambda j: (0, first + j))
    fixed = lambda n: pl.BlockSpec((n, LANES), lambda j: (0, 0))
    deps = tuple(kept) + tuple(deps)
    return pl.pallas_call(
        functools.partial(attend_kernel, slots, tile_q, len(deps)),
        grid=(count,),
        out_shape=(jax.ShapeDtypeStruct((rows, width), BF), jax.ShapeDtypeStruct((rows, width), BF)),
        in_specs=[of(rows, 0), of(keys, 1), of(keys, 2), fixed(rows), fixed(keys)]
        + [pl.BlockSpec(memory_space=pl.ANY)] * len(deps),
        out_specs=(out, out),
        input_output_aliases={5 + i: i for i in range(len(kept))},
        scratch_shapes=[pltpu.VMEM((2, keys, LANES), BF), pltpu.VMEM((2, keys, LANES), BF)],
        compiler_params=pltpu.CompilerParams(vmem_limit_bytes=56 * MIB),
        cost_estimate=pl.CostEstimate(
            flops=16 * rows * keys * count * LANES,
            bytes_accessed=2 * (3 * rows + 2 * keys) * count * LANES,
            transcendentals=2 * rows * keys * count,
        ),
    )(qkv, qkv, qkv, aug_q, aug_k, *deps)


def attend_back_kernel(
    slots, tile_k, scale, n_deps,
    q_ref, k_ref, v_ref, o_ref, do_ref, l_ref, ak_ref, *rest,
):
    (
        dqkv_ref, sum_ref,
        qx_ref, qz_ref, dx_ref, dz_ref, kx_ref, vx_ref, kt_ref, acc_ref,
    ) = rest[n_deps:]
    lane = lax.broadcasted_iota(jnp.int32, (1, LANES), 1)
    col = lane % HDIM
    sides = (lane < HDIM, lane >= HDIM)
    rows, keys = q_ref.shape[0], k_ref.shape[0]
    tokens = rows - slots
    grad = do_ref[...].astype(F32)
    prod = grad * o_ref[...].astype(F32)
    zero = jnp.zeros_like(grad)
    for h, sel in enumerate(sides):
        delta = jnp.sum(jnp.where(sel, prod, 0.0), axis=1, keepdims=True)
        qx_ref[h] = pick(sel, q_ref[...], l_ref[...])
        qz_ref[h] = pick(sel, q_ref[...], zero)
        dx_ref[h] = jnp.where(sel, grad, in_columns(col, -delta, zero)).astype(BF)
        dz_ref[h] = jnp.where(sel, grad, 0.0).astype(BF)
        kx_ref[h] = pick(sel, k_ref[...], ak_ref[...])
        vx_ref[h] = pick(sel, v_ref[...], ak_ref[...])
        kt_ref[h] = jnp.where(sel, k_ref[...].astype(F32), 0.0).T.astype(BF)

    def work(q_at, q_n, k_at, k_n, kt_at):
        dq = None
        dk = jnp.zeros((k_n, LANES), F32)
        dv = jnp.zeros((k_n, LANES), F32)
        for h in range(2):
            at, of = pl.ds(k_at, k_n), pl.ds(q_at, q_n)
            p = jnp.exp(nt(kx_ref[h, at, :], qx_ref[h, of, :]))
            dp = nt(vx_ref[h, at, :], dx_ref[h, of, :])
            ds = (p * dp).astype(BF)
            dv += nn(p.astype(BF), dz_ref[h, of, :])
            dk += nn(ds, qz_ref[h, of, :])
            part = nn(kt_ref[h, :, pl.ds(kt_at, k_n)], ds)
            dq = part if dq is None else dq + part
        return dq, dk, dv

    def keep(at, n, dk, dv):
        dqkv_ref[pl.ds(at, n), pl.ds(LANES, LANES)] = dk.astype(BF)
        dqkv_ref[pl.ds(at, n), pl.ds(2 * LANES, LANES)] = dv.astype(BF)

    dq, dk, dv = work(0, slots, 0, slots, 0)
    dq = dq.T * scale
    dqkv_ref[pl.ds(0, slots), pl.ds(0, LANES)] = dq.astype(BF)
    keep(0, slots, dk, dv)
    acc_ref[...] = jnp.zeros_like(acc_ref)
    sum_v = jnp.sum(dv, axis=0, keepdims=True)
    sum_q = jnp.sum(dq, axis=0, keepdims=True)
    for i in range((keys - slots) // tile_k):
        at = slots + i * tile_k
        dq, dk, dv = work(slots, tokens, at, tile_k, at)
        acc_ref[...] += dq
        keep(at, tile_k, dk, dv)
        sum_v += jnp.sum(dv, axis=0, keepdims=True)
    dq = acc_ref[...].T * scale
    dqkv_ref[pl.ds(slots, tokens), pl.ds(0, LANES)] = dq.astype(BF)
    dqkv_ref[pl.ds(rows, keys - rows), pl.ds(0, LANES)] = jnp.zeros((keys - rows, LANES), BF)
    sum_q += jnp.sum(dq, axis=0, keepdims=True)
    sum_ref[pl.ds(0, 1), :] = sum_q
    sum_ref[pl.ds(1, 1), :] = sum_v
    sum_ref[pl.ds(2, 6), :] = jnp.zeros((6, LANES), F32)


def attend_back(qkv, o, do, logs, aug_k, slots, tile_k, scale, first, count, kept, deps=()):
    rows, width = o.shape
    keys = qkv.shape[0]
    of = lambda n, m: pl.BlockSpec((n, LANES), lambda j: (0, 3 * (first + j) + m))
    col = lambda n: pl.BlockSpec((n, LANES), lambda j: (0, first + j))
    fixed = lambda n: pl.BlockSpec((n, LANES), lambda j: (0, 0))
    wide = lambda n: pltpu.VMEM((2, n, LANES), BF)
    deps = tuple(kept) + tuple(deps)
    return pl.pallas_call(
        functools.partial(attend_back_kernel, slots, tile_k, scale, len(deps)),
        grid=(count,),
        out_shape=(
            jax.ShapeDtypeStruct((keys, 3 * width), BF),
            jax.ShapeDtypeStruct((8, width), F32),
        ),
        in_specs=[of(rows, 0), of(keys, 1), of(keys, 2), col(rows), col(rows), col(rows), fixed(keys)]
        + [pl.BlockSpec(memory_space=pl.ANY)] * len(deps),
        out_specs=(pl.BlockSpec((keys, 3 * LANES), lambda j: (0, first + j)), col(8)),
        input_output_aliases={7 + i: i for i in range(len(kept))},
        scratch_shapes=[
            wide(rows), wide(rows), wide(rows), wide(rows), wide(keys), wide(keys),
            pltpu.VMEM((2, LANES, keys), BF),
            pltpu.VMEM((LANES, rows - slots), F32),
        ],
        compiler_params=pltpu.CompilerParams(vmem_limit_bytes=56 * MIB),
        cost_estimate=pl.CostEstimate(
            flops=40 * rows * keys * count * LANES,
            bytes_accessed=2 * (6 * rows + 4 * keys) * count * LANES,
            transcendentals=2 * rows * keys * count,
        ),
    )(qkv, qkv, qkv, o, do, logs, aug_k, *deps)


def nothing(*refs):
    return None


def tie(x, *deps):
    anywhere = pl.BlockSpec(memory_space=pl.ANY)
    return pl.pallas_call(
        nothing,
        out_shape=jax.ShapeDtypeStruct(x.shape, x.dtype),
        in_specs=[anywhere] * (1 + len(deps)),
        out_specs=anywhere,
        input_output_aliases={0: 0},
        cost_estimate=pl.CostEstimate(flops=0, bytes_accessed=0, transcendentals=0),
    )(x, *deps)


def assemble_kernel(n_in, n_deps, n_out, copies, *refs):
    ins, outs, sem = refs[:n_in], refs[n_in + n_deps : n_in + n_deps + n_out], refs[-1]
    started = []
    for i, (source, at, target, to) in enumerate(copies):
        src = ins[source].at[at] if at else ins[source]
        dst = outs[target].at[to] if to else outs[target]
        started.append(pltpu.make_async_copy(src, dst, sem.at[i]))
    for c in started:
        c.start()
    for c in started:
        c.wait()


def assemble(arrays, shapes, copies, deps=()):
    anywhere = pl.BlockSpec(memory_space=pl.ANY)
    vmem = pl.BlockSpec(memory_space=pltpu.VMEM)
    size = sum(math.prod(s) for s in shapes)
    return pl.pallas_call(
        functools.partial(assemble_kernel, len(arrays), len(deps), len(shapes), copies),
        out_shape=tuple(jax.ShapeDtypeStruct(s, arrays[0].dtype) for s in shapes),
        in_specs=[anywhere] * (len(arrays) + len(deps)),
        out_specs=tuple(vmem for _ in shapes),
        scratch_shapes=[pltpu.SemaphoreType.DMA((len(copies),))],
        compiler_params=pltpu.CompilerParams(vmem_limit_bytes=56 * MIB),
        cost_estimate=pl.CostEstimate(flops=0, bytes_accessed=4 * size, transcendentals=0),
    )(*arrays, *deps)


def sums_kernel(n_in, n_deps, n_out, pieces, *refs):
    ins, outs = refs[:n_in], refs[n_in + n_deps : n_in + n_deps + n_out]
    for target, to, terms in pieces:
        total = ins[terms[0][0]][terms[0][1]].astype(F32)
        for source, at in terms[1:]:
            total = total + ins[source][at].astype(F32)
        outs[target][to] = total.astype(outs[target].dtype)


def sums(arrays, outs, pieces, deps=()):
    anywhere = pl.BlockSpec(memory_space=pl.ANY)
    vmem = pl.BlockSpec(memory_space=pltpu.VMEM)
    size = sum(a.size for a in arrays)
    return pl.pallas_call(
        functools.partial(sums_kernel, len(arrays), len(deps), len(outs), pieces),
        out_shape=tuple(jax.ShapeDtypeStruct(s, dt) for s, dt in outs),
        in_specs=[vmem] * len(arrays) + [anywhere] * len(deps),
        out_specs=tuple(vmem for _ in outs),
        compiler_params=pltpu.CompilerParams(vmem_limit_bytes=56 * MIB),
        cost_estimate=pl.CostEstimate(flops=size, bytes_accessed=4 * size, transcendentals=0),
    )(*arrays, *deps)


def own_kernel(n_x, tiles, n_deps, la_ref, lb_ref, ra_ref, rb_ref, ga_ref, gb_ref, *rest):
    rest, (ta_ref, tb_ref) = rest[n_deps:-2], rest[-2:]
    nears, far_own, far_oth = rest[:n_x], rest[n_x], rest[n_x + 1]
    t, j = pl.program_id(0), pl.program_id(1)
    size = ga_ref.shape[0] // n_x
    half = size // 2

    @pl.when((t == 0) & (j == 0))
    def _():
        ta_ref[...] = la_ref[...].astype(F32).T.astype(BF)
        tb_ref[...] = lb_ref[...].astype(F32).T.astype(BF)

    def run(l_ref, r_ref, g_ref):
        part = (nn(l_ref[...], r_ref[...]) + g_ref[...].astype(F32)).astype(BF)
        for x in range(n_x):
            nears[x][...] = part[x * size : x * size + half]

        @pl.when(t == 0)
        def _():
            for x in range(n_x):
                far_own[pl.ds(x * half, half), :] = part[x * size + half : (x + 1) * size]

        @pl.when(t > 0)
        def _():
            for x in range(n_x):
                far_oth[pl.ds(x * half, half), :] = part[x * size + half : (x + 1) * size]

    @pl.when(j < tiles)
    def _():
        run(ta_ref, ra_ref, ga_ref)

    @pl.when(j == tiles)
    def _():
        run(tb_ref, rb_ref, gb_ref)


def own_parts(n_x, lhs_a, rhs_a, away_a, lhs_b, rhs_b, away_b, deps=()):
    m = lhs_a.shape[0]
    k = away_a.shape[0]
    tile = rhs_b.shape[1] // 2
    tiles = rhs_a.shape[1] // (2 * tile)
    cols = (tiles + 1) * tile
    half = k // (2 * n_x)
    left = pl.BlockSpec((m, k), lambda t, j: (0, 0))
    first = lambda n: pl.BlockSpec((n, tile), lambda t, j: (0, t * tiles + jnp.minimum(j, tiles - 1)))
    second = lambda n: pl.BlockSpec((n, tile), lambda t, j: (0, t))
    return pl.pallas_call(
        functools.partial(own_kernel, n_x, tiles, len(deps)),
        grid=(2, tiles + 1),
        out_shape=(jax.ShapeDtypeStruct((half, 2 * cols), BF),) * n_x
        + (jax.ShapeDtypeStruct((n_x * half, cols), BF),) * 2,
        in_specs=[left, left, first(m), second(m), first(k), second(k)]
        + [pl.BlockSpec(memory_space=pl.ANY)] * len(deps),
        out_specs=(pl.BlockSpec((half, tile), lambda t, j: (0, t * (tiles + 1) + j)),) * n_x
        + (
            pl.BlockSpec((n_x * half, tile), lambda t, j: (0, jnp.where(t == 0, j, tiles))),
            pl.BlockSpec((n_x * half, tile), lambda t, j: (0, jnp.where(t == 0, 0, j))),
        ),
        scratch_shapes=[pltpu.VMEM((k, m), BF), pltpu.VMEM((k, m), BF)],
        compiler_params=pltpu.CompilerParams(vmem_limit_bytes=56 * MIB),
        cost_estimate=pl.CostEstimate(
            flops=4 * m * k * cols, bytes_accessed=4 * (m + 2 * k) * cols, transcendentals=0
        ),
    )(lhs_a, lhs_b, rhs_a, rhs_b, away_a, away_b, *deps)


def chunk_of(m):
    return m if m <= 704 else m // 2


def mm_in_kernel(chunk, epilogue, start, finish, n_extra, n_deps, a_ref, h_ref, r_ref, *rest):
    extra, outs = rest[:n_extra], rest[n_extra + n_deps :]
    k = h_ref.shape[0]

    def step(i, carry):
        rows = pl.ds(pl.multiple_of(i * chunk, 16), chunk)
        acc = nn(a_ref[rows, pl.ds(0, k)], h_ref[...]) + nn(a_ref[rows, pl.ds(k, k)], r_ref[...])
        return epilogue(acc, rows, extra, outs, carry)

    last = lax.fori_loop(0, a_ref.shape[0] // chunk, step, start(h_ref.shape[1]))
    finish(last, outs)


def nought(tn):
    return 0


def leave(carry, outs):
    return None


def mm_in(a, h, r, col, width, tn, epilogue, extra, outs, start=nought, finish=leave, deps=()):
    m, k = a.shape[0], h.shape[0] // 2
    tiles = width // tn
    weight = pl.BlockSpec((k, tn), lambda t, j: (t, col // tn + j))
    wide = lambda n: pl.BlockSpec((n, tn), lambda t, j: (0, t * tiles + j))
    return pl.pallas_call(
        functools.partial(mm_in_kernel, chunk_of(m), epilogue, start, finish, len(extra), len(deps)),
        grid=(2, tiles),
        out_shape=tuple(jax.ShapeDtypeStruct((n, 2 * width), dt) for n, dt in outs),
        in_specs=[pl.BlockSpec((m, 2 * k), lambda t, j: (0, 0)), weight, weight]
        + [wide(e.shape[0]) for e in extra]
        + [pl.BlockSpec(memory_space=pl.ANY)] * len(deps),
        out_specs=tuple(wide(n) for n, _ in outs),
        compiler_params=pltpu.CompilerParams(vmem_limit_bytes=56 * MIB),
        cost_estimate=pl.CostEstimate(
            flops=8 * m * k * width,
            bytes_accessed=4 * m * k + 8 * k * width + sum(2 * width * n * 2 for n, _ in outs),
            transcendentals=0,
        ),
    )(a, h, r, *extra, *deps)


def mm_out_kernel(chunk, half_tiles, n_extra, epilogue, a0_ref, a1_ref, h0_ref, h1_ref, r0_ref, r1_ref, *rest):
    extra, o_ref = rest[:n_extra], rest[-1]

    def run(w0_ref, w1_ref):
        def step(i, carry):
            rows = pl.ds(pl.multiple_of(i * chunk, 16), chunk)
            acc = nt(a0_ref[rows, :], w0_ref[...]) + nt(a1_ref[rows, :], w1_ref[...])
            more = [e[rows, :] if e.shape[0] > 8 else e[pl.ds(0, 1), :] for e in extra]
            o_ref[rows, :] = epilogue(acc, *more).astype(o_ref.dtype)
            return carry

        lax.fori_loop(0, a0_ref.shape[0] // chunk, step, 0)

    i = pl.program_id(0)

    @pl.when(i < half_tiles)
    def _():
        run(h0_ref, h1_ref)

    @pl.when(i >= half_tiles)
    def _():
        run(r0_ref, r1_ref)


def mm_out(a, m, h, r, col, width, td, epilogue, extra, dtype, deps=(), row=0):
    k = h.shape[0] // 2
    half = k // td
    at = col // width
    lhs = lambda t: pl.BlockSpec((m, width), lambda i: (0, t))
    if row:
        lhs = lambda t: pl.BlockSpec((pl.Element(m), pl.Element(width)), lambda i: (row, t * width))
    own = lambda t: pl.BlockSpec((td, width), lambda i: (t * half + jnp.minimum(i, half - 1), at))
    oth = lambda t: pl.BlockSpec((td, width), lambda i: (t * half + jnp.maximum(i - half, 0), at))
    wide = lambda n: pl.BlockSpec((min(n, m), td), lambda i: (0, i))
    return pl.pallas_call(
        functools.partial(mm_out_kernel, chunk_of(m), half, len(extra), epilogue),
        grid=(2 * half,),
        out_shape=jax.ShapeDtypeStruct((m, 2 * k), dtype),
        in_specs=[lhs(0), lhs(1), own(0), own(1), oth(0), oth(1)]
        + [wide(e.shape[0]) for e in extra]
        + [pl.BlockSpec(memory_space=pl.ANY)] * len(deps),
        out_specs=wide(m),
        compiler_params=pltpu.CompilerParams(vmem_limit_bytes=56 * MIB),
        cost_estimate=pl.CostEstimate(
            flops=8 * m * k * width,
            bytes_accessed=4 * m * width + 8 * k * width + 8 * m * k,
            transcendentals=0,
        ),
    )(a, a, h, h, r, r, *extra, *deps)


def put_plain(acc, rows, extra, outs, carry):
    outs[0][rows, :] = acc.astype(outs[0].dtype)
    return carry


def put_biased(acc, rows, extra, outs, carry):
    outs[0][rows, :] = (acc + extra[0][pl.ds(0, 1), :]).astype(outs[0].dtype)
    return carry


def put_scaled(acc, rows, extra, outs, carry):
    low = (acc + extra[0][pl.ds(0, 1), :]).astype(BF).astype(F32)
    outs[0][rows, :] = (low * extra[0][pl.ds(1, 1), :]).astype(BF)
    return carry


def put_gelu(acc, rows, extra, outs, carry):
    inner = acc + extra[0][pl.ds(0, 1), :]
    out, slope = gelu_parts(inner)
    outs[0][rows, :] = out.astype(BF)
    outs[1][rows, :] = slope.astype(BF)
    return carry


def put_sloped(acc, rows, extra, outs, carry):
    grad = acc * extra[0][rows, :].astype(F32)
    outs[0][rows, :] = grad.astype(BF)
    return carry + jnp.sum(grad, axis=0, keepdims=True)


def row_of_zeros(tn):
    return jnp.zeros((1, tn), F32)


def put_sum(carry, outs):
    outs[1][...] = jnp.broadcast_to(carry, outs[1].shape)


def eight(*rows):
    return jnp.concatenate([jnp.stack(rows), jnp.zeros((8 - len(rows), rows[0].shape[0]), F32)])


def gelu_parts(v):
    size = jnp.abs(v)
    t = 1.0 / ((0.3275911 * math.sqrt(0.5)) * size + 1.0)
    bell = jnp.exp(-0.5 * (v * v))
    poly = (0.5 * 1.061405429) * t - 0.5 * 1.453152027
    poly = (poly * t + 0.5 * 1.421413741) * t - 0.5 * 0.284496736
    poly = (poly * t + 0.5 * 0.254829592) * t
    low = bell * (poly - size * (1.0 / math.sqrt(2.0 * math.pi)))
    return jnp.maximum(v, 0.0) - size * (poly * bell), jnp.where(v < 0.0, low, 1.0 - low)


def norm_parts(v):
    centered = v - jnp.mean(v, axis=-1, keepdims=True)
    rstd = lax.rsqrt(jnp.mean(centered * centered, axis=-1, keepdims=True) + LN_EPS)
    return centered * rstd, rstd


def norm_back(c, vhat, rstd, gain):
    gc = c * gain
    back = (
        gc
        - jnp.mean(gc, axis=-1, keepdims=True)
        - vhat * jnp.mean(gc * vhat, axis=-1, keepdims=True)
    ) * rstd
    return back, jnp.sum(c * vhat, axis=0), jnp.sum(c, axis=0)


def make(n_pb, n_pa, n_ta):
    cores = 2
    n_x = n_pb // cores
    blocks = n_pb * n_pa

    def px(v, k):
        return lax.ppermute(v, "pb", [(i, i ^ (cores * k)) for i in range(n_pb)])

    def pc(v):
        return lax.ppermute(v, "pb", [(i, i ^ 1) for i in range(n_pb)])

    def pz(v, k):
        return lax.ppermute(v, "pa", [(i, i ^ k) for i in range(n_pa)])

    def py(v):
        return lax.ppermute(v, "ta", [(i, i ^ 1) for i in range(n_ta)])

    x_bits = n_x.bit_length() - 1
    z_bits = n_pa.bit_length() - 1

    def after(v, *deps):
        return tie(v, *deps) if deps else v

    every = slice(None)

    def z_go(have, bit):
        return pz(have, 1 << bit)

    def z_end(have, other, deps=()):
        n, w, cols = have.shape
        (out,) = assemble(
            (have, other), ((n, 2, w, cols),), ((0, (), 0, (every, 0)), (1, (), 0, (every, 1))), deps
        )
        return out.reshape(2 * n, w, cols)

    def z_last(have, other, deps=()):
        n, w, cols = have.shape
        h = n // 2
        near, far = assemble(
            (have, other), ((h, 2, w, cols), (h, 2, w, cols)),
            tuple(
                (source, (pl.ds(s * h, h),), s, (every, source)) for s in range(2) for source in range(2)
            ),
            deps,
        )
        return near.reshape(n, w, cols), far.reshape(n, w, cols)

    def z_rest(have, other):
        have = z_end(have, other)
        for bit in reversed(range(1, z_bits - 1)):
            have = z_end(have, z_go(have, bit))
        return have, z_go(have, 0)

    def gather_z(shard):
        have = shard[None]
        for bit in reversed(range(z_bits)):
            have = z_end(have, z_go(have, bit))
        return have.reshape(-1, have.shape[-1])

    def joined(parts, deps=()):
        (out,) = assemble(
            tuple(parts), ((len(parts),) + parts[0].shape,),
            tuple((i, (), 0, (i,)) for i in range(len(parts))), deps,
        )
        return out

    def spread_x(a):
        have, arrays = [(0, None)], [a]
        for bit in range(x_bits):
            whole = arrays[0] if bit == 0 else joined([arrays[i] if p is None else arrays[i][p] for i, p in have])
            arrays.append(px(whole, 1 << bit))
            last = len(arrays) - 1
            have = have + ([(last, None)] if bit == 0 else [(last, p) for p in range(len(have))])
        return [arrays[i] if p is None else arrays[i][p] for i, p in have]

    def xy_go(near, far):
        return spread_x(near), [far, py(far)]

    def xy_one(going, deps=()):
        near_xs, far_ts = going
        return joined(near_xs, deps), joined(far_ts, deps)

    def xy_two_go(near_x, far_t):
        return near_x, py(near_x), spread_x(far_t)

    def xy_two(going, deps=()):
        near_x, near_oth, far_x = going
        _, h, w, cols = near_x.shape
        copies = []
        for x in range(n_x):
            for t in range(n_ta):
                copies.append((t, (x,), 0, (t, x, 0)))
                copies.append((n_ta + x, (t,), 0, (t, x, 1)))
        (out,) = assemble(
            (near_x, near_oth, *far_x), ((n_ta, n_x, 2, h, w, cols),), tuple(copies), deps
        )
        return out.reshape(-1, cols)

    def add(a, b):
        return (a.astype(F32) + b.astype(F32)).astype(a.dtype)

    def away_part(lhs, rhs):
        return pc(tn(lhs[:, lhs.shape[1] // 2 :], rhs).astype(BF))

    def core_part(lhs, rhs, away):
        return (tn(lhs[:, : lhs.shape[1] // 2], rhs) + away.astype(F32)).astype(BF)

    def p1_send(parts, deps=()):
        rows = parts[0].shape[0]
        size = rows // n_x
        half = size // 2
        widths = [r.shape[1] // n_ta for r in parts]
        cols = sum(widths)
        copies = []
        for i, n in enumerate(widths):
            at = sum(widths[:i])
            for t in range(n_ta):
                for x in range(n_x):
                    copies.append((
                        i, (pl.ds(x * size, half), pl.ds(t * n, n)), x, (every, pl.ds(t * cols + at, n)),
                    ))
                    copies.append((
                        i, (pl.ds(x * size + half, half), pl.ds(t * n, n)),
                        n_x + t, (pl.ds(x * half, half), pl.ds(at, n)),
                    ))
        shapes = ((half, n_ta * cols),) * n_x + ((n_x * half, cols),) * n_ta
        out = assemble(tuple(parts), shapes, tuple(copies), deps)
        return out[:n_x], out[n_x], out[n_x + 1]

    def p1_go(sent):
        near, far_own, far_oth = sent
        return [px(near[k], k) for k in range(1, n_x)], py(far_oth)

    def p1_end(sent, got, deps=()):
        near, far_own, _ = sent
        half, cols = near[0].shape[0], far_own.shape[1]
        n = len(got[0])
        pieces = []
        for t in range(n_ta):
            at = (every, pl.ds(t * cols, cols))
            pieces.append((t, (), [(i, at) for i in range(n + 1)]))
        for x in range(n_x):
            at = (pl.ds(x * half, half), every)
            pieces.append((n_ta + x, (), [(n + 1, at), (n + 2, at)]))
        pieces = [(o, to or (every, every), terms) for o, to, terms in pieces]
        out = sums(
            (near[0], *got[0], far_own, got[1]), (((half, cols), BF),) * (n_ta + n_x), pieces, deps
        )
        return out[0], out[1], out[2:]

    def p2_go(state):
        near_own, near_oth, far = state
        return py(near_oth), [px(far[k], k) for k in range(1, n_x)]

    def p2_end(state, got, w, deps=()):
        half, cols = state[0].shape
        h = half // w
        pieces = []
        for b in range(2 * h):
            at = (pl.ds((b % h) * w, w), every)
            terms = [(0, at), (1, at)] if b < h else [(i, at) for i in range(2, 3 + len(got[1]))]
            pieces.append((b % 2, (b // 2,), terms))
        return sums(
            (state[0], got[0], state[2][0], *got[1]), (((h, w, cols), BF),) * 2, pieces, deps
        )

    def z_next(keep, got, deps=()):
        n, w, cols = keep.shape
        pieces = [(b % 2, (b // 2,), [(0, (b,)), (1, (b,))]) for b in range(n)]
        return sums((keep, got), (((n // 2, w, cols), BF),) * 2, pieces, deps)

    def z_done(keep, got, deps=()):
        _, w, cols = keep.shape
        (out,) = sums((keep, got), (((1, w, cols), F32),), [(0, (0,), [(0, (0,)), (1, (0,))])], deps)
        return out[0]

    def z_split(cur):
        cur = cur.reshape((cur.shape[0] // 2, 2) + cur.shape[1:])
        return cur[:, 0], cur[:, 1]

    def reduce_z(cur):
        for bit in range(z_bits):
            keep, give = z_split(cur)
            got = pz(give, 1 << bit)
            cur = keep.astype(F32) + got.astype(F32) if bit == z_bits - 1 else add(keep, got)
        return cur[0]

    def reduce_z_from(keep, give, first):
        for bit in range(first, z_bits - 1):
            keep, give = z_next(keep, pz(give, 1 << bit))
        return z_done(keep, pz(give, 1 << (z_bits - 1)))

    def on_device(
        rows_in, w_qkv, b_qv, w_out, b_out, ln1_gain, ln1_bias, w_in, b_in, w_fin, b_fin,
        ln2_gain, ln2_bias, w_head, b_head, lengths, query_len, score_grad,
    ):
        t0 = lax.axis_index("ta")
        z0 = lax.axis_index("pa")
        p0 = lax.axis_index("pb")
        x0, c0 = p0 // cores, p0 % cores
        first_t = t0 == 0
        all_rows, width = rows_in.shape
        half_rows = all_rows // n_ta
        n_q, n_p = query_len.shape[1], lengths.shape[1]
        q_here = n_q // n_ta
        slots = q_here * QLEN
        toks = half_rows - slots
        block = width // blocks
        heads_half = w_qkv.shape[2]
        scale = 1.0 / math.sqrt(HDIM)

        per_tile = LANES // block
        z_tiles = n_pa // per_tile
        low_bits = per_tile.bit_length() - 1
        forward, backward = [], []
        for c in range(cores):
            for x in range(n_x):
                for z in range(z_tiles):
                    forward.append((((x ^ x0) * cores) + (c ^ c0)) * z_tiles + (z ^ (z0 // per_tile)))
        for x in range(n_x):
            for c in range(cores):
                for z in range(z_tiles):
                    backward.append((((c ^ c0) * n_x) + (x ^ x0)) * z_tiles + (z ^ (z0 // per_tile)))
        low = z0 % per_tile
        as_info = lambda v: jnp.stack([jnp.asarray(a, jnp.int32) for a in v])
        row_info = as_info(forward + [low, t0 * half_rows, (1 - t0) * half_rows + slots])
        vec_info = as_info(forward + [low, 0])
        back_info = as_info(backward + [low, 0])

        rows = permute(rows_in, row_info, (half_rows, toks), block, low_bits)
        vecs = jnp.stack(
            [b_out, ln1_gain, ln1_bias, b_fin, ln2_gain, ln2_bias, b_out, b_out]
        )
        vecs = permute(vecs, vec_info, (8,), block, low_bits)
        b_out_r, g1, be1, b_fin_r, g2, be2 = (vecs[i] for i in range(6))
        pairs = heads_half // LANES
        all_pairs = n_ta * pairs
        ff_half = w_in.shape[1]
        head_half = width // n_ta
        qkv_half = 3 * heads_half
        swapped = lambda v: jnp.concatenate([v[..., v.shape[-1] // 2 :], v[..., : v.shape[-1] // 2]], axis=-1)
        in_order = lambda v: jnp.where(first_t, v, swapped(v))

        row_id = jnp.arange(half_rows + toks, dtype=jnp.int32)
        is_slot = row_id < slots
        token = jnp.where(
            row_id < half_rows, t0 * toks + row_id - slots, (1 - t0) * toks + row_id - half_rows
        )
        ends = jnp.cumsum(lengths[0])
        pid = jnp.sum((token[:, None] >= ends[None, :]).astype(jnp.int32), axis=1)
        q_lens = lax.dynamic_index_in_dim(query_len, z0, 0, keepdims=False)
        q_lens = lax.dynamic_slice_in_dim(q_lens, t0 * q_here, q_here, 0)
        limit = jnp.sum(
            jnp.where(
                (row_id // QLEN)[:, None] == jnp.arange(q_here, dtype=jnp.int32)[None, :],
                q_lens[None, :], 0,
            ),
            axis=1,
        )
        dead = is_slot & (row_id % QLEN >= limit)
        seg = jnp.where(is_slot, n_p + row_id // QLEN, pid)
        lane_c = jnp.arange(LANES, dtype=jnp.int32)[None, :] % HDIM
        same = seg[:, None] == lane_c
        aug_k = jnp.where(
            lane_c < 6, same & ~dead[:, None], jnp.where(lane_c == 6, dead[:, None], (lane_c >= 7) & (lane_c < 10))
        )
        aug_k = aug_k.astype(BF)
        aug_q = jnp.where((lane_c < 7) & ~same[:half_rows], BIG, 0.0).astype(BF)

        packed = lambda v: v.reshape(v.shape[0], 3, pairs, LANES).transpose(0, 2, 1, 3)
        shard_q = packed(w_qkv.transpose(1, 0, 2).reshape(block, qkv_half)).reshape(block, -1)
        shard_m = jnp.concatenate([w_in, w_out.T], axis=1)
        head_mine = lax.dynamic_slice_in_dim(w_head, t0 * head_half, head_half, 1)
        shard_e = jnp.concatenate([w_fin.T, head_mine], axis=1)

        q_all = [shard_q] + [pz(shard_q, k) for k in range(1, n_pa)]
        near_q, far_q = joined(q_all[: n_pa // 2]), joined(q_all[n_pa // 2 :])
        m_0 = tie(shard_m[None], near_q)
        m_1 = z_go(m_0, z_bits - 1)
        near_q, far_q = xy_one(xy_go(near_q, far_q), (rows, aug_q, aug_k))
        h_q = xy_two(xy_two_go(near_q, far_q), (m_1,))
        r_q = pc(h_q)
        m_2, m_3 = z_rest(m_0, m_1)
        bias_of = lambda b: packed(jnp.concatenate([b[0], jnp.zeros_like(b[0]), b[1]])[None]).reshape(-1)
        qkv_bias = jnp.concatenate([bias_of(b_qv), bias_of(py(b_qv))])
        b_in_r = jnp.concatenate([b_in, py(b_in)])

        col_scale = jnp.tile(jnp.repeat(jnp.array([scale, 1.0, 1.0], F32), LANES), all_pairs)
        (qkv,) = mm_in(
            rows, h_q, r_q, 0, qkv_half, qkv_half // 2, put_scaled, (eight(qkv_bias, col_scale),),
            ((half_rows + toks, BF),), deps=(m_2,),
        )
        near_m, far_m = z_last(m_2, m_3, (qkv,))
        e_0 = tie(shard_e[None], near_m)
        e_1 = z_go(e_0, z_bits - 1)
        n_call = all_pairs // 4
        part = lambda i, kept, deps: attend(
            qkv, half_rows, aug_q, aug_k, slots, toks, i * n_call, n_call, kept, deps
        )
        going = xy_go(near_m, far_m)
        kept = part(0, (), (near_m, e_0))
        near_m, far_m = xy_one(going, (kept[0],))
        going = xy_two_go(near_m, far_m)
        e_2 = z_end(e_0, e_1, (kept[0],))
        for bit in reversed(range(1, z_bits - 1)):
            e_2 = z_end(e_2, z_go(e_2, bit))
        e_3 = z_go(e_2, 0)
        kept = part(1, kept, (near_m, far_m, e_2))
        kept = part(2, kept, ())
        near_e, far_e = z_last(e_2, e_3, (kept[0],))
        going_e = xy_go(near_e, far_e)
        kept = part(3, kept, (near_e,))
        h_m = xy_two(going, (kept[0],))
        r_m = pc(h_m)
        near_e, far_e = xy_one(going_e, (h_m,))
        ctx, logs = kept
        h_one = mm_out(
            ctx, half_rows, h_m, r_m, ff_half, heads_half, heads_half // 2,
            lambda acc, res, b: acc + res.astype(F32) + b, (rows, eight(b_out_r)), F32,
            (near_e, far_e),
        )
        v1, r1 = norm_parts(h_one)
        normed = v1 * g1 + be1
        normed_low = normed.astype(BF)
        active, slope = mm_in(
            normed_low, h_m, r_m, 0, ff_half, ff_half // 4, put_gelu, (eight(b_in_r),),
            ((half_rows, BF), (half_rows, BF)),
        )
        h_e = xy_two(xy_two_go(near_e, far_e), (active,))
        r_e = pc(h_e)
        h_two = mm_out(
            active, half_rows, h_e, r_e, 0, ff_half, heads_half // 2,
            lambda acc, res, b: acc + res + b, (normed, eight(b_fin_r)), F32,
        )
        v2, r2 = norm_parts(h_two)
        output_low = (v2 * g2 + be2).astype(BF)
        (raw,) = mm_in(
            output_low, h_e, r_e, ff_half, head_half, head_half, put_biased,
            (eight(in_order(b_head)),), ((half_rows, F32),),
        )
        inv = lax.rsqrt(jnp.sum(raw * raw, axis=-1, keepdims=True) + UNIT_EPS)
        unit = raw * inv
        unit_low = unit.astype(BF)

        passages = unit_low[slots:]
        own = unit_low[:slots]
        others = joined([pz(own, k)[None] for k in range(1, n_pa)]).reshape(-1, width)
        asked = jnp.concatenate([own, others, swapped(py(own)), swapped(py(others))], axis=0)
        n_asked = asked.shape[0]
        z_rel = jnp.arange(n_pa, dtype=jnp.int32) ^ z0
        swap_t = lambda a: jnp.where(first_t, a, a[::-1])
        lens = swap_t(
            jnp.take(query_len, z_rel, axis=0).reshape(n_pa, n_ta, q_here).transpose(1, 0, 2)
        )
        valid = (
            jnp.arange(QLEN, dtype=jnp.int32)[None, None, None, :] < lens[..., None]
        ).astype(F32)
        up = swap_t(
            jnp.take(score_grad[0], z_rel, axis=0).reshape(n_pa, n_ta, q_here, n_p).transpose(1, 0, 2, 3)
        )
        token_grad = (up[:, :, :, None, :] * valid[..., None]).reshape(n_asked, n_p)
        member = (
            pid[slots:half_rows, None] == jnp.arange(n_p, dtype=jnp.int32)[None, :]
        ).astype(F32)
        powers = jnp.exp(nt(asked, passages) * (1.0 / SHARP))
        sums = jnp.dot(powers, member, precision=lax.Precision.HIGHEST)
        theirs = py(sums.reshape(n_ta, n_asked // n_ta, n_p)[::-1])
        sums = sums + theirs.reshape(n_asked, n_p)
        soft = (SHARP * jnp.log(sums)).reshape(n_ta, n_pa, q_here, QLEN, n_p)
        scores = jnp.sum(soft[0] * valid[0][..., None], axis=2)
        scores = jnp.take(scores, z_rel, axis=0)[None]
        coef = token_grad / sums
        coef_j = sum(coef[:, i : i + 1] * member[:, i][None, :] for i in range(n_p))
        sim_grad = (powers * coef_j).astype(BF)
        ask_grad = nn(sim_grad, passages).astype(BF).reshape(n_ta, n_pa * slots, width)
        ask_sum = add(ask_grad[0], py(swapped(ask_grad[1])))
        passage_grad = tn(sim_grad, asked)
        own_grad = ask_sum[:slots].astype(F32)
        for k in range(1, n_pa):
            own_grad = own_grad + pz(ask_sum[k * slots : (k + 1) * slots], k).astype(F32)
        unit_grad = jnp.concatenate([own_grad, passage_grad], axis=0)

        raw_grad = inv * (unit_grad - unit * jnp.sum(unit * unit_grad, axis=-1, keepdims=True))
        g_b_head = in_order(jnp.sum(raw_grad, axis=0))
        raw_low = raw_grad.astype(BF)
        output_grad = mm_out(
            raw_low, half_rows, h_e, r_e, ff_half, head_half, heads_half // 2, lambda acc: acc, (), F32
        )
        h_two_grad, g_g2, g_be2 = norm_back(output_grad, v2, r2, g2)
        g_b_fin = jnp.sum(h_two_grad, axis=0)
        branch_low = h_two_grad.astype(BF)
        away_fin = away_part(branch_low, active)
        away_head = away_part(output_low, raw_low)
        inner_low, sums_in = mm_in(
            branch_low, h_e, r_e, 0, ff_half, ff_half // 2, put_sloped, (slope,),
            ((half_rows, BF), (8, F32)), row_of_zeros, put_sum,
        )
        *near, far_own, far_oth = own_parts(
            n_x, branch_low, active, away_fin, output_low, raw_low, away_head, (inner_low,)
        )
        sent_f = (near, far_own, far_oth)
        got_f = p1_go(sent_f)
        away_in = away_part(normed_low, inner_low)
        normed_grad = mm_out(
            inner_low, half_rows, h_m, r_m, 0, ff_half, heads_half // 2,
            lambda acc, res: acc + res, (h_two_grad,), F32, (sent_f[0][-1], sent_f[2]),
        )
        state_f = p1_end(sent_f, got_f, (normed_grad,))
        got_f = p2_go(state_f)
        h_one_grad, g_g1, g_be1 = norm_back(normed_grad, v1, r1, g1)
        g_b_out = jnp.sum(h_one_grad, axis=0)
        attended_low = h_one_grad.astype(BF)
        away_out = away_part(attended_low, ctx)
        (d_ctx,) = mm_in(
            attended_low, h_m, r_m, ff_half, heads_half, heads_half, put_plain, (), ((half_rows, BF),),
            deps=(state_f[1], state_f[2][-1]),
        )
        *near, far_own, far_oth = own_parts(
            n_x, normed_low, inner_low, away_in, attended_low, ctx, away_out, (d_ctx,)
        )
        sent_m = (near, far_own, far_oth)
        got_m = p1_go(sent_m)

        back = lambda i, kept, deps: attend_back(
            qkv, ctx, d_ctx, logs, aug_k, slots, 2 * toks // 5, scale,
            ((i + 2) % 4) * n_call, n_call, kept, deps,
        )
        quarter = qkv_half // 2
        columns = lambda a, i: a[:, i * quarter : (i + 1) * quarter]
        rows_x = width // (cores * n_x)
        x_blocks = lambda part: [part[k * rows_x : (k + 1) * rows_x] for k in range(n_x)]
        x_go = lambda blocks_of: [px(blocks_of[k], k) for k in range(1, n_x)]

        def x_end(blocks_of, got):
            total = blocks_of[0]
            for g in got:
                total = add(total, g)
            return total

        keep_f, give_f = p2_end(state_f, got_f, block, (sent_m[2],))
        z_f = pz(give_f, 1)
        kept = back(0, (), (sent_m[0][-1], sent_m[2], give_f))
        keep_f, give_f = z_next(keep_f, z_f, (kept[1],))
        z_f = pz(give_f, 2)
        state_m = p1_end(sent_m, got_m, (kept[1],))
        got_m = p2_go(state_m)
        kept = back(1, kept, (give_f, state_m[1], state_m[2][-1]))
        if z_bits == 2:
            out_f = z_done(keep_f, z_f, (kept[1],))
        else:
            out_f = reduce_z_from(*z_next(keep_f, z_f), 2)
        keep_m, give_m = p2_end(state_m, got_m, block, (kept[1],))
        z_m = pz(give_m, 1)
        rows = tie(rows, give_m, out_f)
        away_1 = away_part(rows, kept[0][:, qkv_half:])
        part_1 = core_part(rows, kept[0][:, qkv_half:], away_1)
        sent_1 = x_blocks(part_1)
        got_1 = x_go(sent_1)
        kept = back(2, kept, (sent_1[1], give_m))
        keep_m, give_m = z_next(keep_m, z_m, (kept[1],))
        z_m = pz(give_m, 2)
        rows = tie(rows, give_m)
        away_2 = away_part(rows, columns(kept[0], 0))
        y_1 = x_end(sent_1, [tie(g, kept[1]) for g in got_1])
        part_2 = core_part(rows, columns(kept[0], 0), tie(away_2, y_1))
        sent_2 = x_blocks(part_2)
        got_2 = x_go(sent_2)
        g_w_fin, g_head = out_f[:, :ff_half], out_f[:, ff_half:]
        n_h = block // n_ta
        head_keep = jnp.where(first_t, g_head[:n_h], g_head[n_h:])
        head_got = py(jnp.where(first_t, g_head[n_h:], g_head[:n_h]))
        kept = back(3, kept, (y_1, sent_2[1], give_m))
        head_got = tie(head_got, kept[1])
        d_qkv, sums_qv = kept
        y_1 = py(y_1)
        if z_bits == 2:
            out_m = z_done(keep_m, z_m, (sums_qv,))
        else:
            out_m = reduce_z_from(*z_next(keep_m, z_m), 2)
        y_1 = tie(y_1, sums_qv)
        rows = tie(rows, y_1, out_m, head_got)
        away_3 = away_part(rows, columns(d_qkv, 1))
        to_other = mm_out(
            d_qkv, toks, h_q, r_q, 0, qkv_half, heads_half // 2, lambda acc: acc, (), BF,
            (away_3,), row=half_rows,
        )
        to_other_part = to_other
        d_qkv = tie(d_qkv, to_other)
        part_3 = core_part(rows, columns(d_qkv, 1), away_3)
        sent_3 = x_blocks(part_3)
        got_3 = x_go(sent_3)
        to_other = py(to_other)
        q_2 = add(x_end(sent_2, [tie(g, to_other_part) for g in got_2]), y_1[:, :quarter]).reshape(n_pa, block, -1)
        grad_rows = mm_out(
            d_qkv, half_rows, h_q, r_q, 0, qkv_half, heads_half // 2,
            lambda acc, res: acc + res, (h_one_grad,), F32, (sent_3[1], q_2),
        )
        to_other = tie(to_other, grad_rows)
        got_3 = [tie(g, grad_rows) for g in got_3]
        q_3 = add(x_end(sent_3, got_3), y_1[:, quarter:]).reshape(n_pa, block, -1)
        keep_q, give_q = z_split(jnp.concatenate([q_2, q_3], axis=2))
        keep_q, give_q = z_split(add(keep_q, pz(give_q, 1)))
        to_other, keep_q = tie(to_other, give_q), tie(keep_q, to_other)
        sums_qv = tie(sums_qv, part_3)
        if z_bits == 2:
            out_q = (keep_q.astype(F32) + pz(give_q, 2).astype(F32))[0]
        else:
            out_q = reduce_z_from(*z_next(keep_q, pz(give_q, 2)), 2)
        g_w_qkv = out_q.reshape(block, pairs, 3, LANES).transpose(2, 0, 1, 3).reshape(3, block, heads_half)
        g_w_in, g_w_out = out_m[:, :ff_half], out_m[:, ff_half:]
        g_w_head = in_order(jnp.concatenate([head_keep, head_got], axis=1))
        grad_rows = permute(
            grad_rows, back_info, (half_rows,), block, low_bits, slots, (to_other,)
        )

        d_vecs = permute(
            eight(g_b_out, g_g1, g_be1, g_b_fin, g_g2, g_be2), back_info, (8,), block, low_bits
        )
        vec = jnp.concatenate(
            [d_vecs, in_order(sums_in[0]).reshape(-1, width), g_b_head[None], in_order(sums_qv[:2])]
        )
        vec = vec + pc(vec)
        for bit in range(x_bits):
            vec = vec + px(vec, 1 << bit)
        vec = tie(vec, to_other)
        vec = vec + py(vec)
        for bit in range(z_bits):
            vec = vec + pz(vec, 1 << bit)
        place = (p0 * n_pa + z0) * n_ta + t0
        w32 = width // (blocks * n_ta)
        ff_rows = n_ta * ff_half // width
        mine = lax.dynamic_slice_in_dim(vec, place * w32, w32, 1)
        o_b_out, o_g1, o_be1, o_b_fin, o_g2, o_be2 = (mine[i] for i in range(6))
        o_b_head, o_bqv = mine[8 + ff_rows], mine[9 + ff_rows : 11 + ff_rows]
        o_b_in = lax.dynamic_slice_in_dim(
            vec[8 : 8 + ff_rows].reshape(-1), place * (ff_rows * w32), ff_rows * w32, 0
        )
        return (
            scores, grad_rows, g_w_qkv, o_bqv, g_w_out.T, o_b_out, o_g1, o_be1,
            g_w_in, o_b_in, g_w_fin.T, o_b_fin, o_g2, o_be2, g_w_head, o_b_head,
        )

    return on_device


def solution(mesh):
    both = ("pb", "pa")
    every = ("pb", "pa", "ta")
    in_specs = (
        P(both, None), P(None, both, "ta"), P(None, "ta"), P("ta", both), P(), P(), P(),
        P(both, "ta"), P("ta"), P("ta", both), P(), P(), P(), P(both, None), P(),
        P(both, None), P("pb", None), P("pb", None, None, "pa"),
    )
    out_specs = (
        P("pb", None, "ta", "pa"), P(every, None), P(None, both, "ta"), P(None, every),
        P("ta", both), P(every), P(every), P(every), P(both, "ta"), P(every), P("ta", both),
        P(every), P(every), P(every), P(every, None), P(every),
    )
    step = make(mesh.shape["pb"], mesh.shape["pa"], mesh.shape["ta"])
    return jax.shard_map(step, mesh=mesh, in_specs=in_specs, out_specs=out_specs, check_vma=False)
```

```python
import functools
import math

import jax
import jax.numpy as jnp
from jax import lax
from jax.experimental import pallas as pl
from jax.experimental.pallas import tpu as pltpu
from jax.sharding import PartitionSpec as P

HDIM = 64
QLEN = 32
LANES = 128
SHARP = 0.02
LN_EPS = 1e-05
UNIT_EPS = 1e-06
BIG = -1e30
BF = jnp.bfloat16
F32 = jnp.float32
MIB = 1024 * 1024


def nn(a, b):
    return lax.dot_general(a, b, (((1,), (0,)), ((), ())), preferred_element_type=F32)


def nt(a, b):
    return lax.dot_general(a, b, (((1,), (1,)), ((), ())), preferred_element_type=F32)


def tn(a, b):
    return lax.dot_general(a, b, (((0,), (0,)), ((), ())), preferred_element_type=F32)


def permute_kernel(segments, block, low_bits, skip, info, x_ref, *rest):
    o_ref = rest[-1]
    tiles = x_ref.shape[1] // LANES
    lane = lax.broadcasted_iota(jnp.int32, (1, LANES), 1)
    low = info[tiles]
    for j in range(tiles):
        source = pl.multiple_of(info[j] * LANES, LANES)
        row = 0
        for i, length in enumerate(segments):
            start = pl.multiple_of(info[tiles + 1 + i], 16)
            part = x_ref[pl.ds(start, length), pl.ds(source, LANES)]
            if skip is not None:
                more = rest[0][:, pl.ds(source, LANES)].astype(F32)
                part = jnp.concatenate([part[:skip], part[skip:] + more], axis=0)
            if low_bits:
                part = part.astype(F32)
                for bit in range(low_bits):
                    step = block << bit
                    up = pltpu.roll(part, step, 1)
                    down = pltpu.roll(part, LANES - step, 1)
                    swapped = jnp.where((lane & step) != 0, up, down)
                    part = jnp.where((low & (1 << bit)) != 0, swapped, part)
                part = part.astype(o_ref.dtype)
            o_ref[pl.ds(row, length), pl.ds(j * LANES, LANES)] = part
            row += length


def permute(x, info, segments, block, low_bits, skip=None, more=()):
    rows = sum(segments)
    return pl.pallas_call(
        functools.partial(permute_kernel, segments, block, low_bits, skip),
        out_shape=jax.ShapeDtypeStruct((rows, x.shape[1]), x.dtype),
        in_specs=[
            pl.BlockSpec(memory_space=pltpu.SMEM),
            pl.BlockSpec(memory_space=pltpu.VMEM),
        ]
        + [pl.BlockSpec(memory_space=pltpu.VMEM)] * len(more),
        out_specs=pl.BlockSpec(memory_space=pltpu.VMEM),
        compiler_params=pltpu.CompilerParams(vmem_limit_bytes=56 * MIB),
        cost_estimate=pl.CostEstimate(
            flops=rows * x.shape[1], bytes_accessed=4 * rows * x.shape[1], transcendentals=0
        ),
    )(info, x, *more)


def pick(sel, a, b):
    return jnp.where(sel, a.astype(F32), b.astype(F32)).astype(BF)


def split3(v):
    hi = v.astype(BF).astype(F32)
    mid = (v - hi).astype(BF).astype(F32)
    return hi, mid, v - hi - mid


def in_columns(col, v, base):
    hi, mid, lo = split3(v)
    return jnp.where(col == 7, hi, jnp.where(col == 8, mid, jnp.where(col == 9, lo, base)))


def attend_kernel(slots, tile_q, n_deps, q_ref, k_ref, v_ref, aq_ref, ak_ref, *rest):
    o_ref, l_ref, kx_ref, vx_ref = rest[n_deps:]
    lane = lax.broadcasted_iota(jnp.int32, (1, LANES), 1)
    col = lane % HDIM
    sides = (lane < HDIM, lane >= HDIM)
    for h, sel in enumerate(sides):
        kx_ref[h] = pick(sel, k_ref[...], ak_ref[...])
        vx_ref[h] = pick(sel, v_ref[...], jnp.ones_like(v_ref[...]))
    keys = k_ref.shape[0]

    def work(q_at, q_n, k_at, k_n):
        rows = pl.ds(q_at, q_n)
        q, aug = q_ref[rows, :], aq_ref[rows, :]
        outs, logs = [], []
        for h, sel in enumerate(sides):
            s = nt(pick(sel, q, aug), kx_ref[h, pl.ds(k_at, k_n), :])
            top = jnp.max(s, axis=1, keepdims=True)
            p = jnp.exp(s - top).astype(BF)
            o = nn(p, vx_ref[h, pl.ds(k_at, k_n), :])
            outs.append(o / pltpu.roll(o, HDIM, 1))
            logs.append(in_columns(col, -(top + jnp.log(o)), aug.astype(F32)))
        o_ref[rows, :] = jnp.where(sides[0], outs[0], outs[1]).astype(BF)
        l_ref[rows, :] = jnp.where(sides[0], logs[1], logs[0]).astype(BF)

    work(0, slots, 0, slots)
    tokens = q_ref.shape[0] - slots

    def step(i, carry):
        work(pl.multiple_of(slots + i * tile_q, 16), tile_q, slots, keys - slots)
        return carry

    lax.fori_loop(0, tokens // tile_q, step, 0)


def attend(qkv, rows, aug_q, aug_k, slots, tile_q, first, count, kept, deps=()):
    keys, width = qkv.shape[0], qkv.shape[1] // 3
    of = lambda n, m: pl.BlockSpec((n, LANES), lambda j: (0, 3 * (first + j) + m))
    out = pl.BlockSpec((rows, LANES), lambda j: (0, first + j))
    fixed = lambda n: pl.BlockSpec((n, LANES), lambda j: (0, 0))
    deps = tuple(kept) + tuple(deps)
    return pl.pallas_call(
        functools.partial(attend_kernel, slots, tile_q, len(deps)),
        grid=(count,),
        out_shape=(jax.ShapeDtypeStruct((rows, width), BF), jax.ShapeDtypeStruct((rows, width), BF)),
        in_specs=[of(rows, 0), of(keys, 1), of(keys, 2), fixed(rows), fixed(keys)]
        + [pl.BlockSpec(memory_space=pl.ANY)] * len(deps),
        out_specs=(out, out),
        input_output_aliases={5 + i: i for i in range(len(kept))},
        scratch_shapes=[pltpu.VMEM((2, keys, LANES), BF), pltpu.VMEM((2, keys, LANES), BF)],
        compiler_params=pltpu.CompilerParams(vmem_limit_bytes=56 * MIB),
        cost_estimate=pl.CostEstimate(
            flops=16 * rows * keys * count * LANES,
            bytes_accessed=2 * (3 * rows + 2 * keys) * count * LANES,
            transcendentals=2 * rows * keys * count,
        ),
    )(qkv, qkv, qkv, aug_q, aug_k, *deps)


def attend_back_kernel(
    slots, tile_k, scale, n_deps,
    q_ref, k_ref, v_ref, o_ref, do_ref, l_ref, ak_ref, *rest,
):
    (
        dqkv_ref, sum_ref,
        qx_ref, qz_ref, dx_ref, dz_ref, kx_ref, vx_ref, kt_ref, acc_ref,
    ) = rest[n_deps:]
    lane = lax.broadcasted_iota(jnp.int32, (1, LANES), 1)
    col = lane % HDIM
    sides = (lane < HDIM, lane >= HDIM)
    rows, keys = q_ref.shape[0], k_ref.shape[0]
    tokens = rows - slots
    grad = do_ref[...].astype(F32)
    prod = grad * o_ref[...].astype(F32)
    zero = jnp.zeros_like(grad)
    for h, sel in enumerate(sides):
        delta = jnp.sum(jnp.where(sel, prod, 0.0), axis=1, keepdims=True)
        qx_ref[h] = pick(sel, q_ref[...], l_ref[...])
        qz_ref[h] = pick(sel, q_ref[...], zero)
        dx_ref[h] = jnp.where(sel, grad, in_columns(col, -delta, zero)).astype(BF)
        dz_ref[h] = jnp.where(sel, grad, 0.0).astype(BF)
        kx_ref[h] = pick(sel, k_ref[...], ak_ref[...])
        vx_ref[h] = pick(sel, v_ref[...], ak_ref[...])
        kt_ref[h] = jnp.where(sel, k_ref[...].astype(F32), 0.0).T.astype(BF)

    def work(q_at, q_n, k_at, k_n, kt_at):
        dq = None
        dk = jnp.zeros((k_n, LANES), F32)
        dv = jnp.zeros((k_n, LANES), F32)
        for h in range(2):
            at, of = pl.ds(k_at, k_n), pl.ds(q_at, q_n)
            p = jnp.exp(nt(kx_ref[h, at, :], qx_ref[h, of, :]))
            dp = nt(vx_ref[h, at, :], dx_ref[h, of, :])
            ds = (p * dp).astype(BF)
            dv += nn(p.astype(BF), dz_ref[h, of, :])
            dk += nn(ds, qz_ref[h, of, :])
            part = nn(kt_ref[h, :, pl.ds(kt_at, k_n)], ds)
            dq = part if dq is None else dq + part
        return dq, dk, dv

    def keep(at, n, dk, dv):
        dqkv_ref[pl.ds(at, n), pl.ds(LANES, LANES)] = dk.astype(BF)
        dqkv_ref[pl.ds(at, n), pl.ds(2 * LANES, LANES)] = dv.astype(BF)

    dq, dk, dv = work(0, slots, 0, slots, 0)
    dq = dq.T * scale
    dqkv_ref[pl.ds(0, slots), pl.ds(0, LANES)] = dq.astype(BF)
    keep(0, slots, dk, dv)
    acc_ref[...] = jnp.zeros_like(acc_ref)
    sum_v = jnp.sum(dv, axis=0, keepdims=True)
    sum_q = jnp.sum(dq, axis=0, keepdims=True)
    for i in range((keys - slots) // tile_k):
        at = slots + i * tile_k
        dq, dk, dv = work(slots, tokens, at, tile_k, at)
        acc_ref[...] += dq
        keep(at, tile_k, dk, dv)
        sum_v += jnp.sum(dv, axis=0, keepdims=True)
    dq = acc_ref[...].T * scale
    dqkv_ref[pl.ds(slots, tokens), pl.ds(0, LANES)] = dq.astype(BF)
    dqkv_ref[pl.ds(rows, keys - rows), pl.ds(0, LANES)] = jnp.zeros((keys - rows, LANES), BF)
    sum_q += jnp.sum(dq, axis=0, keepdims=True)
    sum_ref[pl.ds(0, 1), :] = sum_q
    sum_ref[pl.ds(1, 1), :] = sum_v
    sum_ref[pl.ds(2, 6), :] = jnp.zeros((6, LANES), F32)


def attend_back(qkv, o, do, logs, aug_k, slots, tile_k, scale, first, count, kept, deps=()):
    rows, width = o.shape
    keys = qkv.shape[0]
    of = lambda n, m: pl.BlockSpec((n, LANES), lambda j: (0, 3 * (first + j) + m))
    col = lambda n: pl.BlockSpec((n, LANES), lambda j: (0, first + j))
    fixed = lambda n: pl.BlockSpec((n, LANES), lambda j: (0, 0))
    wide = lambda n: pltpu.VMEM((2, n, LANES), BF)
    deps = tuple(kept) + tuple(deps)
    return pl.pallas_call(
        functools.partial(attend_back_kernel, slots, tile_k, scale, len(deps)),
        grid=(count,),
        out_shape=(
            jax.ShapeDtypeStruct((keys, 3 * width), BF),
            jax.ShapeDtypeStruct((8, width), F32),
        ),
        in_specs=[of(rows, 0), of(keys, 1), of(keys, 2), col(rows), col(rows), col(rows), fixed(keys)]
        + [pl.BlockSpec(memory_space=pl.ANY)] * len(deps),
        out_specs=(pl.BlockSpec((keys, 3 * LANES), lambda j: (0, first + j)), col(8)),
        input_output_aliases={7 + i: i for i in range(len(kept))},
        scratch_shapes=[
            wide(rows), wide(rows), wide(rows), wide(rows), wide(keys), wide(keys),
            pltpu.VMEM((2, LANES, keys), BF),
            pltpu.VMEM((LANES, rows - slots), F32),
        ],
        compiler_params=pltpu.CompilerParams(vmem_limit_bytes=56 * MIB),
        cost_estimate=pl.CostEstimate(
            flops=40 * rows * keys * count * LANES,
            bytes_accessed=2 * (6 * rows + 4 * keys) * count * LANES,
            transcendentals=2 * rows * keys * count,
        ),
    )(qkv, qkv, qkv, o, do, logs, aug_k, *deps)


def nothing(*refs):
    return None


def tie(x, *deps):
    anywhere = pl.BlockSpec(memory_space=pl.ANY)
    return pl.pallas_call(
        nothing,
        out_shape=jax.ShapeDtypeStruct(x.shape, x.dtype),
        in_specs=[anywhere] * (1 + len(deps)),
        out_specs=anywhere,
        input_output_aliases={0: 0},
        cost_estimate=pl.CostEstimate(flops=0, bytes_accessed=0, transcendentals=0),
    )(x, *deps)


def assemble_kernel(n_in, n_deps, n_out, copies, *refs):
    ins, outs, sem = refs[:n_in], refs[n_in + n_deps : n_in + n_deps + n_out], refs[-1]
    started = []
    for i, (source, at, target, to) in enumerate(copies):
        src = ins[source].at[at] if at else ins[source]
        dst = outs[target].at[to] if to else outs[target]
        started.append(pltpu.make_async_copy(src, dst, sem.at[i]))
    for c in started:
        c.start()
    for c in started:
        c.wait()


def assemble(arrays, shapes, copies, deps=()):
    anywhere = pl.BlockSpec(memory_space=pl.ANY)
    vmem = pl.BlockSpec(memory_space=pltpu.VMEM)
    size = sum(math.prod(s) for s in shapes)
    return pl.pallas_call(
        functools.partial(assemble_kernel, len(arrays), len(deps), len(shapes), copies),
        out_shape=tuple(jax.ShapeDtypeStruct(s, arrays[0].dtype) for s in shapes),
        in_specs=[anywhere] * (len(arrays) + len(deps)),
        out_specs=tuple(vmem for _ in shapes),
        scratch_shapes=[pltpu.SemaphoreType.DMA((len(copies),))],
        compiler_params=pltpu.CompilerParams(vmem_limit_bytes=56 * MIB),
        cost_estimate=pl.CostEstimate(flops=0, bytes_accessed=4 * size, transcendentals=0),
    )(*arrays, *deps)


def sums_kernel(n_in, n_deps, n_out, pieces, *refs):
    ins, outs = refs[:n_in], refs[n_in + n_deps : n_in + n_deps + n_out]
    for target, to, terms in pieces:
        total = ins[terms[0][0]][terms[0][1]].astype(F32)
        for source, at in terms[1:]:
            total = total + ins[source][at].astype(F32)
        outs[target][to] = total.astype(outs[target].dtype)


def sums(arrays, outs, pieces, deps=()):
    anywhere = pl.BlockSpec(memory_space=pl.ANY)
    vmem = pl.BlockSpec(memory_space=pltpu.VMEM)
    size = sum(a.size for a in arrays)
    return pl.pallas_call(
        functools.partial(sums_kernel, len(arrays), len(deps), len(outs), pieces),
        out_shape=tuple(jax.ShapeDtypeStruct(s, dt) for s, dt in outs),
        in_specs=[vmem] * len(arrays) + [anywhere] * len(deps),
        out_specs=tuple(vmem for _ in outs),
        compiler_params=pltpu.CompilerParams(vmem_limit_bytes=56 * MIB),
        cost_estimate=pl.CostEstimate(flops=size, bytes_accessed=4 * size, transcendentals=0),
    )(*arrays, *deps)


def own_kernel(n_x, tiles, n_deps, la_ref, lb_ref, ra_ref, rb_ref, ga_ref, gb_ref, *rest):
    rest, (ta_ref, tb_ref) = rest[n_deps:-2], rest[-2:]
    nears, far_own, far_oth = rest[:n_x], rest[n_x], rest[n_x + 1]
    t, j = pl.program_id(0), pl.program_id(1)
    size = ga_ref.shape[0] // n_x
    half = size // 2

    @pl.when((t == 0) & (j == 0))
    def _():
        ta_ref[...] = la_ref[...].astype(F32).T.astype(BF)
        tb_ref[...] = lb_ref[...].astype(F32).T.astype(BF)

    def run(l_ref, r_ref, g_ref):
        part = (nn(l_ref[...], r_ref[...]) + g_ref[...].astype(F32)).astype(BF)
        for x in range(n_x):
            nears[x][...] = part[x * size : x * size + half]

        @pl.when(t == 0)
        def _():
            for x in range(n_x):
                far_own[pl.ds(x * half, half), :] = part[x * size + half : (x + 1) * size]

        @pl.when(t > 0)
        def _():
            for x in range(n_x):
                far_oth[pl.ds(x * half, half), :] = part[x * size + half : (x + 1) * size]

    @pl.when(j < tiles)
    def _():
        run(ta_ref, ra_ref, ga_ref)

    @pl.when(j == tiles)
    def _():
        run(tb_ref, rb_ref, gb_ref)


def own_parts(n_x, lhs_a, rhs_a, away_a, lhs_b, rhs_b, away_b, deps=()):
    m = lhs_a.shape[0]
    k = away_a.shape[0]
    tile = rhs_b.shape[1] // 2
    tiles = rhs_a.shape[1] // (2 * tile)
    cols = (tiles + 1) * tile
    half = k // (2 * n_x)
    left = pl.BlockSpec((m, k), lambda t, j: (0, 0))
    first = lambda n: pl.BlockSpec((n, tile), lambda t, j: (0, t * tiles + jnp.minimum(j, tiles - 1)))
    second = lambda n: pl.BlockSpec((n, tile), lambda t, j: (0, t))
    return pl.pallas_call(
        functools.partial(own_kernel, n_x, tiles, len(deps)),
        grid=(2, tiles + 1),
        out_shape=(jax.ShapeDtypeStruct((half, 2 * cols), BF),) * n_x
        + (jax.ShapeDtypeStruct((n_x * half, cols), BF),) * 2,
        in_specs=[left, left, first(m), second(m), first(k), second(k)]
        + [pl.BlockSpec(memory_space=pl.ANY)] * len(deps),
        out_specs=(pl.BlockSpec((half, tile), lambda t, j: (0, t * (tiles + 1) + j)),) * n_x
        + (
            pl.BlockSpec((n_x * half, tile), lambda t, j: (0, jnp.where(t == 0, j, tiles))),
            pl.BlockSpec((n_x * half, tile), lambda t, j: (0, jnp.where(t == 0, 0, j))),
        ),
        scratch_shapes=[pltpu.VMEM((k, m), BF), pltpu.VMEM((k, m), BF)],
        compiler_params=pltpu.CompilerParams(vmem_limit_bytes=56 * MIB),
        cost_estimate=pl.CostEstimate(
            flops=4 * m * k * cols, bytes_accessed=4 * (m + 2 * k) * cols, transcendentals=0
        ),
    )(lhs_a, lhs_b, rhs_a, rhs_b, away_a, away_b, *deps)


def chunk_of(m):
    return m if m <= 704 else m // 2


def mm_in_kernel(chunk, epilogue, start, finish, n_extra, n_deps, a_ref, h_ref, r_ref, *rest):
    extra, outs = rest[:n_extra], rest[n_extra + n_deps :]
    k = h_ref.shape[0]

    def step(i, carry):
        rows = pl.ds(pl.multiple_of(i * chunk, 16), chunk)
        acc = nn(a_ref[rows, pl.ds(0, k)], h_ref[...]) + nn(a_ref[rows, pl.ds(k, k)], r_ref[...])
        return epilogue(acc, rows, extra, outs, carry)

    last = lax.fori_loop(0, a_ref.shape[0] // chunk, step, start(h_ref.shape[1]))
    finish(last, outs)


def nought(tn):
    return 0


def leave(carry, outs):
    return None


def mm_in(a, h, r, col, width, tn, epilogue, extra, outs, start=nought, finish=leave, deps=()):
    m, k = a.shape[0], h.shape[0] // 2
    tiles = width // tn
    weight = pl.BlockSpec((k, tn), lambda t, j: (t, col // tn + j))
    wide = lambda n: pl.BlockSpec((n, tn), lambda t, j: (0, t * tiles + j))
    return pl.pallas_call(
        functools.partial(mm_in_kernel, chunk_of(m), epilogue, start, finish, len(extra), len(deps)),
        grid=(2, tiles),
        out_shape=tuple(jax.ShapeDtypeStruct((n, 2 * width), dt) for n, dt in outs),
        in_specs=[pl.BlockSpec((m, 2 * k), lambda t, j: (0, 0)), weight, weight]
        + [wide(e.shape[0]) for e in extra]
        + [pl.BlockSpec(memory_space=pl.ANY)] * len(deps),
        out_specs=tuple(wide(n) for n, _ in outs),
        compiler_params=pltpu.CompilerParams(vmem_limit_bytes=56 * MIB),
        cost_estimate=pl.CostEstimate(
            flops=8 * m * k * width,
            bytes_accessed=4 * m * k + 8 * k * width + sum(2 * width * n * 2 for n, _ in outs),
            transcendentals=0,
        ),
    )(a, h, r, *extra, *deps)


def mm_out_kernel(chunk, half_tiles, n_extra, epilogue, a0_ref, a1_ref, h0_ref, h1_ref, r0_ref, r1_ref, *rest):
    extra, o_ref = rest[:n_extra], rest[-1]

    def run(w0_ref, w1_ref):
        def step(i, carry):
            rows = pl.ds(pl.multiple_of(i * chunk, 16), chunk)
            acc = nt(a0_ref[rows, :], w0_ref[...]) + nt(a1_ref[rows, :], w1_ref[...])
            more = [e[rows, :] if e.shape[0] > 8 else e[pl.ds(0, 1), :] for e in extra]
            o_ref[rows, :] = epilogue(acc, *more).astype(o_ref.dtype)
            return carry

        lax.fori_loop(0, a0_ref.shape[0] // chunk, step, 0)

    i = pl.program_id(0)

    @pl.when(i < half_tiles)
    def _():
        run(h0_ref, h1_ref)

    @pl.when(i >= half_tiles)
    def _():
        run(r0_ref, r1_ref)


def mm_out(a, m, h, r, col, width, td, epilogue, extra, dtype, deps=(), row=0):
    k = h.shape[0] // 2
    half = k // td
    at = col // width
    lhs = lambda t: pl.BlockSpec((m, width), lambda i: (0, t))
    if row:
        lhs = lambda t: pl.BlockSpec((pl.Element(m), pl.Element(width)), lambda i: (row, t * width))
    own = lambda t: pl.BlockSpec((td, width), lambda i: (t * half + jnp.minimum(i, half - 1), at))
    oth = lambda t: pl.BlockSpec((td, width), lambda i: (t * half + jnp.maximum(i - half, 0), at))
    wide = lambda n: pl.BlockSpec((min(n, m), td), lambda i: (0, i))
    return pl.pallas_call(
        functools.partial(mm_out_kernel, chunk_of(m), half, len(extra), epilogue),
        grid=(2 * half,),
        out_shape=jax.ShapeDtypeStruct((m, 2 * k), dtype),
        in_specs=[lhs(0), lhs(1), own(0), own(1), oth(0), oth(1)]
        + [wide(e.shape[0]) for e in extra]
        + [pl.BlockSpec(memory_space=pl.ANY)] * len(deps),
        out_specs=wide(m),
        compiler_params=pltpu.CompilerParams(vmem_limit_bytes=56 * MIB),
        cost_estimate=pl.CostEstimate(
            flops=8 * m * k * width,
            bytes_accessed=4 * m * width + 8 * k * width + 8 * m * k,
            transcendentals=0,
        ),
    )(a, a, h, h, r, r, *extra, *deps)


def put_plain(acc, rows, extra, outs, carry):
    outs[0][rows, :] = acc.astype(outs[0].dtype)
    return carry


def put_biased(acc, rows, extra, outs, carry):
    outs[0][rows, :] = (acc + extra[0][pl.ds(0, 1), :]).astype(outs[0].dtype)
    return carry


def put_scaled(acc, rows, extra, outs, carry):
    low = (acc + extra[0][pl.ds(0, 1), :]).astype(BF).astype(F32)
    outs[0][rows, :] = (low * extra[0][pl.ds(1, 1), :]).astype(BF)
    return carry


def put_gelu(acc, rows, extra, outs, carry):
    inner = acc + extra[0][pl.ds(0, 1), :]
    out, slope = gelu_parts(inner)
    outs[0][rows, :] = out.astype(BF)
    outs[1][rows, :] = slope.astype(BF)
    return carry


def put_sloped(acc, rows, extra, outs, carry):
    grad = acc * extra[0][rows, :].astype(F32)
    outs[0][rows, :] = grad.astype(BF)
    return carry + jnp.sum(grad, axis=0, keepdims=True)


def row_of_zeros(tn):
    return jnp.zeros((1, tn), F32)


def put_sum(carry, outs):
    outs[1][...] = jnp.broadcast_to(carry, outs[1].shape)


def eight(*rows):
    return jnp.concatenate([jnp.stack(rows), jnp.zeros((8 - len(rows), rows[0].shape[0]), F32)])


def gelu_parts(v):
    size = jnp.abs(v)
    t = 1.0 / ((0.3275911 * math.sqrt(0.5)) * size + 1.0)
    bell = jnp.exp(-0.5 * (v * v))
    poly = (0.5 * 1.061405429) * t - 0.5 * 1.453152027
    poly = (poly * t + 0.5 * 1.421413741) * t - 0.5 * 0.284496736
    poly = (poly * t + 0.5 * 0.254829592) * t
    low = bell * (poly - size * (1.0 / math.sqrt(2.0 * math.pi)))
    return jnp.maximum(v, 0.0) - size * (poly * bell), jnp.where(v < 0.0, low, 1.0 - low)


def norm_parts(v):
    centered = v - jnp.mean(v, axis=-1, keepdims=True)
    rstd = lax.rsqrt(jnp.mean(centered * centered, axis=-1, keepdims=True) + LN_EPS)
    return centered * rstd, rstd


def norm_back(c, vhat, rstd, gain):
    gc = c * gain
    back = (
        gc
        - jnp.mean(gc, axis=-1, keepdims=True)
        - vhat * jnp.mean(gc * vhat, axis=-1, keepdims=True)
    ) * rstd
    return back, jnp.sum(c * vhat, axis=0), jnp.sum(c, axis=0)


def make(n_pb, n_pa, n_ta):
    cores = 2
    n_x = n_pb // cores
    blocks = n_pb * n_pa

    def px(v, k):
        return lax.ppermute(v, "pb", [(i, i ^ (cores * k)) for i in range(n_pb)])

    def pc(v):
        return lax.ppermute(v, "pb", [(i, i ^ 1) for i in range(n_pb)])

    def pz(v, k):
        return lax.ppermute(v, "pa", [(i, i ^ k) for i in range(n_pa)])

    def py(v):
        return lax.ppermute(v, "ta", [(i, i ^ 1) for i in range(n_ta)])

    x_bits = n_x.bit_length() - 1
    z_bits = n_pa.bit_length() - 1

    def after(v, *deps):
        return tie(v, *deps) if deps else v

    every = slice(None)

    def z_go(have, bit):
        return pz(have, 1 << bit)

    def z_end(have, other, deps=()):
        n, w, cols = have.shape
        (out,) = assemble(
            (have, other), ((n, 2, w, cols),), ((0, (), 0, (every, 0)), (1, (), 0, (every, 1))), deps
        )
        return out.reshape(2 * n, w, cols)

    def z_last(have, other, deps=()):
        n, w, cols = have.shape
        h = n // 2
        near, far = assemble(
            (have, other), ((h, 2, w, cols), (h, 2, w, cols)),
            tuple(
                (source, (pl.ds(s * h, h),), s, (every, source)) for s in range(2) for source in range(2)
            ),
            deps,
        )
        return near.reshape(n, w, cols), far.reshape(n, w, cols)

    def z_rest(have, other):
        have = z_end(have, other)
        for bit in reversed(range(1, z_bits - 1)):
            have = z_end(have, z_go(have, bit))
        return have, z_go(have, 0)

    def gather_z(shard):
        have = shard[None]
        for bit in reversed(range(z_bits)):
            have = z_end(have, z_go(have, bit))
        return have.reshape(-1, have.shape[-1])

    def joined(parts, deps=()):
        (out,) = assemble(
            tuple(parts), ((len(parts),) + parts[0].shape,),
            tuple((i, (), 0, (i,)) for i in range(len(parts))), deps,
        )
        return out

    def spread_x(a):
        have, arrays = [(0, None)], [a]
        for bit in range(x_bits):
            whole = arrays[0] if bit == 0 else joined([arrays[i] if p is None else arrays[i][p] for i, p in have])
            arrays.append(px(whole, 1 << bit))
            last = len(arrays) - 1
            have = have + ([(last, None)] if bit == 0 else [(last, p) for p in range(len(have))])
        return [arrays[i] if p is None else arrays[i][p] for i, p in have]

    def xy_go(near, far):
        return spread_x(near), [far, py(far)]

    def xy_one(going, deps=()):
        near_xs, far_ts = going
        return joined(near_xs, deps), joined(far_ts, deps)

    def xy_two_go(near_x, far_t):
        return near_x, py(near_x), spread_x(far_t)

    def xy_two(going, deps=()):
        near_x, near_oth, far_x = going
        _, h, w, cols = near_x.shape
        copies = []
        for x in range(n_x):
            for t in range(n_ta):
                copies.append((t, (x,), 0, (t, x, 0)))
                copies.append((n_ta + x, (t,), 0, (t, x, 1)))
        (out,) = assemble(
            (near_x, near_oth, *far_x), ((n_ta, n_x, 2, h, w, cols),), tuple(copies), deps
        )
        return out.reshape(-1, cols)

    def add(a, b):
        return (a.astype(F32) + b.astype(F32)).astype(a.dtype)

    def away_part(lhs, rhs):
        return pc(tn(lhs[:, lhs.shape[1] // 2 :], rhs).astype(BF))

    def core_part(lhs, rhs, away):
        return (tn(lhs[:, : lhs.shape[1] // 2], rhs) + away.astype(F32)).astype(BF)

    def p1_send(parts, deps=()):
        rows = parts[0].shape[0]
        size = rows // n_x
        half = size // 2
        widths = [r.shape[1] // n_ta for r in parts]
        cols = sum(widths)
        copies = []
        for i, n in enumerate(widths):
            at = sum(widths[:i])
            for t in range(n_ta):
                for x in range(n_x):
                    copies.append((
                        i, (pl.ds(x * size, half), pl.ds(t * n, n)), x, (every, pl.ds(t * cols + at, n)),
                    ))
                    copies.append((
                        i, (pl.ds(x * size + half, half), pl.ds(t * n, n)),
                        n_x + t, (pl.ds(x * half, half), pl.ds(at, n)),
                    ))
        shapes = ((half, n_ta * cols),) * n_x + ((n_x * half, cols),) * n_ta
        out = assemble(tuple(parts), shapes, tuple(copies), deps)
        return out[:n_x], out[n_x], out[n_x + 1]

    def p1_go(sent):
        near, far_own, far_oth = sent
        return [px(near[k], k) for k in range(1, n_x)], py(far_oth)

    def p1_end(sent, got, deps=()):
        near, far_own, _ = sent
        half, cols = near[0].shape[0], far_own.shape[1]
        n = len(got[0])
        pieces = []
        for t in range(n_ta):
            at = (every, pl.ds(t * cols, cols))
            pieces.append((t, (), [(i, at) for i in range(n + 1)]))
        for x in range(n_x):
            at = (pl.ds(x * half, half), every)
            pieces.append((n_ta + x, (), [(n + 1, at), (n + 2, at)]))
        pieces = [(o, to or (every, every), terms) for o, to, terms in pieces]
        out = sums(
            (near[0], *got[0], far_own, got[1]), (((half, cols), BF),) * (n_ta + n_x), pieces, deps
        )
        return out[0], out[1], out[2:]

    def p2_go(state):
        near_own, near_oth, far = state
        return py(near_oth), [px(far[k], k) for k in range(1, n_x)]

    def p2_end(state, got, w, deps=()):
        half, cols = state[0].shape
        h = half // w
        pieces = []
        for b in range(2 * h):
            at = (pl.ds((b % h) * w, w), every)
            terms = [(0, at), (1, at)] if b < h else [(i, at) for i in range(2, 3 + len(got[1]))]
            pieces.append((b % 2, (b // 2,), terms))
        return sums(
            (state[0], got[0], state[2][0], *got[1]), (((h, w, cols), BF),) * 2, pieces, deps
        )

    def z_next(keep, got, deps=()):
        n, w, cols = keep.shape
        pieces = [(b % 2, (b // 2,), [(0, (b,)), (1, (b,))]) for b in range(n)]
        return sums((keep, got), (((n // 2, w, cols), BF),) * 2, pieces, deps)

    def z_done(keep, got, deps=()):
        _, w, cols = keep.shape
        (out,) = sums((keep, got), (((1, w, cols), F32),), [(0, (0,), [(0, (0,)), (1, (0,))])], deps)
        return out[0]

    def z_split(cur):
        cur = cur.reshape((cur.shape[0] // 2, 2) + cur.shape[1:])
        return cur[:, 0], cur[:, 1]

    def reduce_z(cur):
        for bit in range(z_bits):
            keep, give = z_split(cur)
            got = pz(give, 1 << bit)
            cur = keep.astype(F32) + got.astype(F32) if bit == z_bits - 1 else add(keep, got)
        return cur[0]

    def reduce_z_from(keep, give, first):
        for bit in range(first, z_bits - 1):
            keep, give = z_next(keep, pz(give, 1 << bit))
        return z_done(keep, pz(give, 1 << (z_bits - 1)))

    def on_device(
        rows_in, w_qkv, b_qv, w_out, b_out, ln1_gain, ln1_bias, w_in, b_in, w_fin, b_fin,
        ln2_gain, ln2_bias, w_head, b_head, lengths, query_len, score_grad,
    ):
        t0 = lax.axis_index("ta")
        z0 = lax.axis_index("pa")
        p0 = lax.axis_index("pb")
        x0, c0 = p0 // cores, p0 % cores
        first_t = t0 == 0
        all_rows, width = rows_in.shape
        half_rows = all_rows // n_ta
        n_q, n_p = query_len.shape[1], lengths.shape[1]
        q_here = n_q // n_ta
        slots = q_here * QLEN
        toks = half_rows - slots
        block = width // blocks
        heads_half = w_qkv.shape[2]
        scale = 1.0 / math.sqrt(HDIM)

        per_tile = LANES // block
        z_tiles = n_pa // per_tile
        low_bits = per_tile.bit_length() - 1
        forward, backward = [], []
        for c in range(cores):
            for x in range(n_x):
                for z in range(z_tiles):
                    forward.append((((x ^ x0) * cores) + (c ^ c0)) * z_tiles + (z ^ (z0 // per_tile)))
        for x in range(n_x):
            for c in range(cores):
                for z in range(z_tiles):
                    backward.append((((c ^ c0) * n_x) + (x ^ x0)) * z_tiles + (z ^ (z0 // per_tile)))
        low = z0 % per_tile
        as_info = lambda v: jnp.stack([jnp.asarray(a, jnp.int32) for a in v])
        row_info = as_info(forward + [low, t0 * half_rows, (1 - t0) * half_rows + slots])
        vec_info = as_info(forward + [low, 0])
        back_info = as_info(backward + [low, 0])

        rows = permute(rows_in, row_info, (half_rows, toks), block, low_bits)
        vecs = jnp.stack(
            [b_out, ln1_gain, ln1_bias, b_fin, ln2_gain, ln2_bias, b_out, b_out]
        )
        vecs = permute(vecs, vec_info, (8,), block, low_bits)
        b_out_r, g1, be1, b_fin_r, g2, be2 = (vecs[i] for i in range(6))
        pairs = heads_half // LANES
        all_pairs = n_ta * pairs
        ff_half = w_in.shape[1]
        head_half = width // n_ta
        qkv_half = 3 * heads_half
        swapped = lambda v: jnp.concatenate([v[..., v.shape[-1] // 2 :], v[..., : v.shape[-1] // 2]], axis=-1)
        in_order = lambda v: jnp.where(first_t, v, swapped(v))

        row_id = jnp.arange(half_rows + toks, dtype=jnp.int32)
        is_slot = row_id < slots
        token = jnp.where(
            row_id < half_rows, t0 * toks + row_id - slots, (1 - t0) * toks + row_id - half_rows
        )
        ends = jnp.cumsum(lengths[0])
        pid = jnp.sum((token[:, None] >= ends[None, :]).astype(jnp.int32), axis=1)
        q_lens = lax.dynamic_index_in_dim(query_len, z0, 0, keepdims=False)
        q_lens = lax.dynamic_slice_in_dim(q_lens, t0 * q_here, q_here, 0)
        limit = jnp.sum(
            jnp.where(
                (row_id // QLEN)[:, None] == jnp.arange(q_here, dtype=jnp.int32)[None, :],
                q_lens[None, :], 0,
            ),
            axis=1,
        )
        dead = is_slot & (row_id % QLEN >= limit)
        seg = jnp.where(is_slot, n_p + row_id // QLEN, pid)
        lane_c = jnp.arange(LANES, dtype=jnp.int32)[None, :] % HDIM
        same = seg[:, None] == lane_c
        aug_k = jnp.where(
            lane_c < 6, same & ~dead[:, None], jnp.where(lane_c == 6, dead[:, None], (lane_c >= 7) & (lane_c < 10))
        )
        aug_k = aug_k.astype(BF)
        aug_q = jnp.where((lane_c < 7) & ~same[:half_rows], BIG, 0.0).astype(BF)

        packed = lambda v: v.reshape(v.shape[0], 3, pairs, LANES).transpose(0, 2, 1, 3)
        shard_q = packed(w_qkv.transpose(1, 0, 2).reshape(block, qkv_half)).reshape(block, -1)
        shard_m = jnp.concatenate([w_in, w_out.T], axis=1)
        head_mine = lax.dynamic_slice_in_dim(w_head, t0 * head_half, head_half, 1)
        shard_e = jnp.concatenate([w_fin.T, head_mine], axis=1)

        q_all = [shard_q] + [pz(shard_q, k) for k in range(1, n_pa)]
        near_q, far_q = joined(q_all[: n_pa // 2]), joined(q_all[n_pa // 2 :])
        m_0 = tie(shard_m[None], near_q)
        m_1 = z_go(m_0, z_bits - 1)
        near_q, far_q = xy_one(xy_go(near_q, far_q), (rows, aug_q, aug_k))
        h_q = xy_two(xy_two_go(near_q, far_q), (m_1,))
        r_q = pc(h_q)
        m_2, m_3 = z_rest(m_0, m_1)
        bias_of = lambda b: packed(jnp.concatenate([b[0], jnp.zeros_like(b[0]), b[1]])[None]).reshape(-1)
        qkv_bias = jnp.concatenate([bias_of(b_qv), bias_of(py(b_qv))])
        b_in_r = jnp.concatenate([b_in, py(b_in)])

        col_scale = jnp.tile(jnp.repeat(jnp.array([scale, 1.0, 1.0], F32), LANES), all_pairs)
        (qkv,) = mm_in(
            rows, h_q, r_q, 0, qkv_half, qkv_half // 2, put_scaled, (eight(qkv_bias, col_scale),),
            ((half_rows + toks, BF),), deps=(m_2,),
        )
        near_m, far_m = z_last(m_2, m_3, (qkv,))
        e_0 = tie(shard_e[None], near_m)
        e_1 = z_go(e_0, z_bits - 1)
        n_call = all_pairs // 4
        part = lambda i, kept, deps: attend(
            qkv, half_rows, aug_q, aug_k, slots, toks, i * n_call, n_call, kept, deps
        )
        going = xy_go(near_m, far_m)
        kept = part(0, (), (near_m, e_0))
        near_m, far_m = xy_one(going, (kept[0],))
        going = xy_two_go(near_m, far_m)
        e_2 = z_end(e_0, e_1, (kept[0],))
        for bit in reversed(range(1, z_bits - 1)):
            e_2 = z_end(e_2, z_go(e_2, bit))
        e_3 = z_go(e_2, 0)
        kept = part(1, kept, (near_m, far_m, e_2))
        kept = part(2, kept, ())
        near_e, far_e = z_last(e_2, e_3, (kept[0],))
        going_e = xy_go(near_e, far_e)
        kept = part(3, kept, (near_e,))
        h_m = xy_two(going, (kept[0],))
        r_m = pc(h_m)
        near_e, far_e = xy_one(going_e, (h_m,))
        ctx, logs = kept
        h_one = mm_out(
            ctx, half_rows, h_m, r_m, ff_half, heads_half, heads_half // 2,
            lambda acc, res, b: acc + res.astype(F32) + b, (rows, eight(b_out_r)), F32,
            (near_e, far_e),
        )
        v1, r1 = norm_parts(h_one)
        normed = v1 * g1 + be1
        normed_low = normed.astype(BF)
        active, slope = mm_in(
            normed_low, h_m, r_m, 0, ff_half, ff_half // 4, put_gelu, (eight(b_in_r),),
            ((half_rows, BF), (half_rows, BF)),
        )
        h_e = xy_two(xy_two_go(near_e, far_e), (active,))
        r_e = pc(h_e)
        h_two = mm_out(
            active, half_rows, h_e, r_e, 0, ff_half, heads_half // 2,
            lambda acc, res, b: acc + res + b, (normed, eight(b_fin_r)), F32,
        )
        v2, r2 = norm_parts(h_two)
        output_low = (v2 * g2 + be2).astype(BF)
        (raw,) = mm_in(
            output_low, h_e, r_e, ff_half, head_half, head_half, put_biased,
            (eight(in_order(b_head)),), ((half_rows, F32),),
        )
        inv = lax.rsqrt(jnp.sum(raw * raw, axis=-1, keepdims=True) + UNIT_EPS)
        unit = raw * inv
        unit_low = unit.astype(BF)

        passages = unit_low[slots:]
        own = unit_low[:slots]
        others = joined([pz(own, k)[None] for k in range(1, n_pa)]).reshape(-1, width)
        asked = jnp.concatenate([own, others, swapped(py(own)), swapped(py(others))], axis=0)
        n_asked = asked.shape[0]
        z_rel = jnp.arange(n_pa, dtype=jnp.int32) ^ z0
        swap_t = lambda a: jnp.where(first_t, a, a[::-1])
        lens = swap_t(
            jnp.take(query_len, z_rel, axis=0).reshape(n_pa, n_ta, q_here).transpose(1, 0, 2)
        )
        valid = (
            jnp.arange(QLEN, dtype=jnp.int32)[None, None, None, :] < lens[..., None]
        ).astype(F32)
        up = swap_t(
            jnp.take(score_grad[0], z_rel, axis=0).reshape(n_pa, n_ta, q_here, n_p).transpose(1, 0, 2, 3)
        )
        token_grad = (up[:, :, :, None, :] * valid[..., None]).reshape(n_asked, n_p)
        member = (
            pid[slots:half_rows, None] == jnp.arange(n_p, dtype=jnp.int32)[None, :]
        ).astype(F32)
        powers = jnp.exp(nt(asked, passages) * (1.0 / SHARP))
        sums = jnp.dot(powers, member, precision=lax.Precision.HIGHEST)
        theirs = py(sums.reshape(n_ta, n_asked // n_ta, n_p)[::-1])
        sums = sums + theirs.reshape(n_asked, n_p)
        soft = (SHARP * jnp.log(sums)).reshape(n_ta, n_pa, q_here, QLEN, n_p)
        scores = jnp.sum(soft[0] * valid[0][..., None], axis=2)
        scores = jnp.take(scores, z_rel, axis=0)[None]
        coef = token_grad / sums
        coef_j = sum(coef[:, i : i + 1] * member[:, i][None, :] for i in range(n_p))
        sim_grad = (powers * coef_j).astype(BF)
        ask_grad = nn(sim_grad, passages).astype(BF).reshape(n_ta, n_pa * slots, width)
        ask_sum = add(ask_grad[0], py(swapped(ask_grad[1])))
        passage_grad = tn(sim_grad, asked)
        own_grad = ask_sum[:slots].astype(F32)
        for k in range(1, n_pa):
            own_grad = own_grad + pz(ask_sum[k * slots : (k + 1) * slots], k).astype(F32)
        unit_grad = jnp.concatenate([own_grad, passage_grad], axis=0)

        raw_grad = inv * (unit_grad - unit * jnp.sum(unit * unit_grad, axis=-1, keepdims=True))
        g_b_head = in_order(jnp.sum(raw_grad, axis=0))
        raw_low = raw_grad.astype(BF)
        output_grad = mm_out(
            raw_low, half_rows, h_e, r_e, ff_half, head_half, heads_half // 2, lambda acc: acc, (), F32
        )
        h_two_grad, g_g2, g_be2 = norm_back(output_grad, v2, r2, g2)
        g_b_fin = jnp.sum(h_two_grad, axis=0)
        branch_low = h_two_grad.astype(BF)
        away_fin = away_part(branch_low, active)
        away_head = away_part(output_low, raw_low)
        inner_low, sums_in = mm_in(
            branch_low, h_e, r_e, 0, ff_half, ff_half // 2, put_sloped, (slope,),
            ((half_rows, BF), (8, F32)), row_of_zeros, put_sum,
        )
        *near, far_own, far_oth = own_parts(
            n_x, branch_low, active, away_fin, output_low, raw_low, away_head, (inner_low,)
        )
        sent_f = (near, far_own, far_oth)
        got_f = p1_go(sent_f)
        away_in = away_part(normed_low, inner_low)
        normed_grad = mm_out(
            inner_low, half_rows, h_m, r_m, 0, ff_half, heads_half // 2,
            lambda acc, res: acc + res, (h_two_grad,), F32, (sent_f[0][-1], sent_f[2]),
        )
        state_f = p1_end(sent_f, got_f, (normed_grad,))
        got_f = p2_go(state_f)
        h_one_grad, g_g1, g_be1 = norm_back(normed_grad, v1, r1, g1)
        g_b_out = jnp.sum(h_one_grad, axis=0)
        attended_low = h_one_grad.astype(BF)
        away_out = away_part(attended_low, ctx)
        (d_ctx,) = mm_in(
            attended_low, h_m, r_m, ff_half, heads_half, heads_half, put_plain, (), ((half_rows, BF),),
            deps=(state_f[1], state_f[2][-1]),
        )
        *near, far_own, far_oth = own_parts(
            n_x, normed_low, inner_low, away_in, attended_low, ctx, away_out, (d_ctx,)
        )
        sent_m = (near, far_own, far_oth)
        got_m = p1_go(sent_m)

        back = lambda i, kept, deps: attend_back(
            qkv, ctx, d_ctx, logs, aug_k, slots, 2 * toks // 5, scale,
            ((i + 2) % 4) * n_call, n_call, kept, deps,
        )
        quarter = qkv_half // 2
        columns = lambda a, i: a[:, i * quarter : (i + 1) * quarter]
        rows_x = width // (cores * n_x)
        x_blocks = lambda part: [part[k * rows_x : (k + 1) * rows_x] for k in range(n_x)]
        x_go = lambda blocks_of: [px(blocks_of[k], k) for k in range(1, n_x)]

        def x_end(blocks_of, got):
            total = blocks_of[0]
            for g in got:
                total = add(total, g)
            return total

        keep_f, give_f = p2_end(state_f, got_f, block, (sent_m[2],))
        z_f = pz(give_f, 1)
        kept = back(0, (), (sent_m[0][-1], sent_m[2], give_f))
        keep_f, give_f = z_next(keep_f, z_f, (kept[1],))
        z_f = pz(give_f, 2)
        state_m = p1_end(sent_m, got_m, (kept[1],))
        got_m = p2_go(state_m)
        kept = back(1, kept, (give_f, state_m[1], state_m[2][-1]))
        if z_bits == 2:
            out_f = z_done(keep_f, z_f, (kept[1],))
        else:
            out_f = reduce_z_from(*z_next(keep_f, z_f), 2)
        keep_m, give_m = p2_end(state_m, got_m, block, (kept[1],))
        z_m = pz(give_m, 1)
        rows = tie(rows, give_m, out_f)
        away_1 = away_part(rows, kept[0][:, qkv_half:])
        part_1 = core_part(rows, kept[0][:, qkv_half:], away_1)
        sent_1 = x_blocks(part_1)
        got_1 = x_go(sent_1)
        kept = back(2, kept, (sent_1[1], give_m))
        keep_m, give_m = z_next(keep_m, z_m, (kept[1],))
        z_m = pz(give_m, 2)
        rows = tie(rows, give_m)
        away_2 = away_part(rows, columns(kept[0], 0))
        y_1 = x_end(sent_1, [tie(g, kept[1]) for g in got_1])
        part_2 = core_part(rows, columns(kept[0], 0), tie(away_2, y_1))
        sent_2 = x_blocks(part_2)
        got_2 = x_go(sent_2)
        g_w_fin, g_head = out_f[:, :ff_half], out_f[:, ff_half:]
        n_h = block // n_ta
        head_keep = jnp.where(first_t, g_head[:n_h], g_head[n_h:])
        head_got = py(jnp.where(first_t, g_head[n_h:], g_head[:n_h]))
        kept = back(3, kept, (y_1, sent_2[1], give_m))
        head_got = tie(head_got, kept[1])
        d_qkv, sums_qv = kept
        y_1 = py(y_1)
        if z_bits == 2:
            out_m = z_done(keep_m, z_m, (sums_qv,))
        else:
            out_m = reduce_z_from(*z_next(keep_m, z_m), 2)
        y_1 = tie(y_1, sums_qv)
        rows = tie(rows, y_1, out_m, head_got)
        away_3 = away_part(rows, columns(d_qkv, 1))
        to_other = mm_out(
            d_qkv, toks, h_q, r_q, 0, qkv_half, heads_half // 2, lambda acc: acc, (), BF,
            (away_3,), row=half_rows,
        )
        to_other_part = to_other
        d_qkv = tie(d_qkv, to_other)
        part_3 = core_part(rows, columns(d_qkv, 1), away_3)
        sent_3 = x_blocks(part_3)
        got_3 = x_go(sent_3)
        to_other = py(to_other)
        q_2 = add(x_end(sent_2, [tie(g, to_other_part) for g in got_2]), y_1[:, :quarter]).reshape(n_pa, block, -1)
        grad_rows = mm_out(
            d_qkv, half_rows, h_q, r_q, 0, qkv_half, heads_half // 2,
            lambda acc, res: acc + res, (h_one_grad,), F32, (sent_3[1], q_2),
        )
        to_other = tie(to_other, grad_rows)
        got_3 = [tie(g, grad_rows) for g in got_3]
        q_3 = add(x_end(sent_3, got_3), y_1[:, quarter:]).reshape(n_pa, block, -1)
        keep_q, give_q = z_split(jnp.concatenate([q_2, q_3], axis=2))
        keep_q, give_q = z_split(add(keep_q, pz(give_q, 1)))
        to_other, keep_q = tie(to_other, give_q), tie(keep_q, to_other)
        sums_qv = tie(sums_qv, part_3)
        if z_bits == 2:
            out_q = (keep_q.astype(F32) + pz(give_q, 2).astype(F32))[0]
        else:
            out_q = reduce_z_from(*z_next(keep_q, pz(give_q, 2)), 2)
        g_w_qkv = out_q.reshape(block, pairs, 3, LANES).transpose(2, 0, 1, 3).reshape(3, block, heads_half)
        g_w_in, g_w_out = out_m[:, :ff_half], out_m[:, ff_half:]
        g_w_head = in_order(jnp.concatenate([head_keep, head_got], axis=1))
        grad_rows = permute(
            grad_rows, back_info, (half_rows,), block, low_bits, slots, (to_other,)
        )

        d_vecs = permute(
            eight(g_b_out, g_g1, g_be1, g_b_fin, g_g2, g_be2), back_info, (8,), block, low_bits
        )
        vec = jnp.concatenate(
            [d_vecs, in_order(sums_in[0]).reshape(-1, width), g_b_head[None], in_order(sums_qv[:2])]
        )
        vec = vec + pc(vec)
        for bit in range(x_bits):
            vec = vec + px(vec, 1 << bit)
        vec = tie(vec, to_other)
        vec = vec + py(vec)
        vec = vec + sum(pz(vec, k) for k in range(1, n_pa))
        place = (p0 * n_pa + z0) * n_ta + t0
        w32 = width // (blocks * n_ta)
        ff_rows = n_ta * ff_half // width
        mine = lax.dynamic_slice_in_dim(vec, place * w32, w32, 1)
        o_b_out, o_g1, o_be1, o_b_fin, o_g2, o_be2 = (mine[i] for i in range(6))
        o_b_head, o_bqv = mine[8 + ff_rows], mine[9 + ff_rows : 11 + ff_rows]
        o_b_in = lax.dynamic_slice_in_dim(
            vec[8 : 8 + ff_rows].reshape(-1), place * (ff_rows * w32), ff_rows * w32, 0
        )
        return (
            scores, grad_rows, g_w_qkv, o_bqv, g_w_out.T, o_b_out, o_g1, o_be1,
            g_w_in, o_b_in, g_w_fin.T, o_b_fin, o_g2, o_be2, g_w_head, o_b_head,
        )

    return on_device


def solution(mesh):
    both = ("pb", "pa")
    every = ("pb", "pa", "ta")
    in_specs = (
        P(both, None), P(None, both, "ta"), P(None, "ta"), P("ta", both), P(), P(), P(),
        P(both, "ta"), P("ta"), P("ta", both), P(), P(), P(), P(both, None), P(),
        P(both, None), P("pb", None), P("pb", None, None, "pa"),
    )
    out_specs = (
        P("pb", None, "ta", "pa"), P(every, None), P(None, both, "ta"), P(None, every),
        P("ta", both), P(every), P(every), P(every), P(both, "ta"), P(every), P("ta", both),
        P(every), P(every), P(every), P(every, None), P(every),
    )
    step = make(mesh.shape["pb"], mesh.shape["pa"], mesh.shape["ta"])
    return jax.shard_map(step, mesh=mesh, in_specs=in_specs, out_specs=out_specs, check_vma=False)
```
